32 devices in a mesh: dp: 4 (over z), shard: 8 (over y, x, core).
Axes of the slice: x: 2, y: 2, z: 4, core: 2. Of those that a mesh axis runs over, the one named last changes fastest.
Arguments:
- conditions: bfloat16 [32, 3, 512, 512], P(('dp', 'shard')), may hold values from -6 to 6
- clean_latents: float32 [32, 4, 4096], P(('dp', 'shard')), may hold values from -6 to 6
- noise_field: float32 [32, 4, 4096], P(('dp', 'shard')), may hold values from -6 to 6
- timesteps: int32 [32], P(('dp', 'shard')), may hold values from 0 to 999
- text_states: bfloat16 [32, 77, 768], P(('dp', 'shard')), may hold values from -6 to 6
- text_lengths: int32 [32], P(('dp', 'shard')), may hold values from 5 to 77
- item_valid: int32 [32], P(('dp', 'shard')), may hold values 0 or 1
- unet_conv: bfloat16 [36, 320], replicated, may hold values from -1 to 1
- res_conv: bfloat16 [2, 2880, 320], replicated, may hold values from -0.109375 to 0.109375
- time_mlp: bfloat16 [320, 1280], replicated, may hold values from -0.3125 to 0.3125
- time_proj: bfloat16 [1280, 320], replicated, may hold values from -0.3125 to 0.3125
- query_proj: bfloat16 [320, 320], replicated, may hold values from -0.3125 to 0.3125
- keyvalue_proj: bfloat16 [768, 640], replicated, may hold values from -0.21875 to 0.21875
- output_proj: bfloat16 [320, 320], replicated, may hold values from -1.25 to 1.25
- geglu_in: bfloat16 [320, 2560], replicated, may hold values from -0.3125 to 0.3125
- geglu_out: bfloat16 [1280, 320], replicated, may hold values from -0.3125 to 0.3125
- velocity_proj: bfloat16 [320, 4], replicated, may hold values from -0.3125 to 0.3125
- adapter_in: float32 [1728, 320], P('shard'), may hold values from -0.15625 to 0.15625
- adapter_conv: float32 [2880, 320], P('shard'), may hold values from -0.109375 to 0.109375
- adapter_out: float32 [320, 320], P('shard'), may hold values from -0.3125 to 0.3125
- adapter_bias: float32 [960], P('shard'), may hold values from -0.25 to 0.25
- first_in: float32 [1728, 320], P('shard'), may hold values from -4.7683716e-06 to 4.7683716e-06
- first_conv: float32 [2880, 320], P('shard'), may hold values from -4.7683716e-06 to 4.7683716e-06
- first_out: float32 [320, 320], P('shard'), may hold values from -4.7683716e-06 to 4.7683716e-06
- first_bias: float32 [960], P('shard'), may hold values from -1.5258789e-05 to 1.5258789e-05
- second_in: float32 [1728, 320], P('shard'), may hold values from 6.337457e-14 to 2.5349829e-13
- second_conv: float32 [2880, 320], P('shard'), may hold values from 6.337457e-14 to 2.5349829e-13
- second_out: float32 [320, 320], P('shard'), may hold values from 6.337457e-14 to 2.5349829e-13
- second_bias: float32 [960], P('shard'), may hold values from 5.703711e-13 to 2.2814845e-12
Outputs:
- loss_sum: float32 [], replicated
- item_count: float32 [], replicated
- grad_norm: float32 [], replicated
- new_first_in: float32 [1728, 320], P('shard')
- new_first_conv: float32 [2880, 320], P('shard')
- new_first_out: float32 [320, 320], P('shard')
- new_first_bias: float32 [960], P('shard')
- new_second_in: float32 [1728, 320], P('shard')
- new_second_conv: float32 [2880, 320], P('shard')
- new_second_out: float32 [320, 320], P('shard')
- new_second_bias: float32 [960], P('shard')
- new_adapter_in: float32 [1728, 320], P('shard')
- new_adapter_conv: float32 [2880, 320], P('shard')
- new_adapter_out: float32 [320, 320], P('shard')
- new_adapter_bias: float32 [960], P('shard')
The draws below stay inside these ranges and needn't reach their ends.
All inputs are finite; a program needn't handle non-finite values. No bound on the sum of `item_valid` on one device may be relied on, other than what follows from the above.
Results may differ from the reference program's by a relative error of at most 0.02.
Values may be sent and summed in bfloat16 or wider, within the bound.
No kernel may reach another device: no remote copies, remote signals or barrier semaphores. Data moves between devices by JAX's collectives and lax.ppermute only.
A program may use at most 320 MiB of HBM per device.

```python
import math
import jax
import jax.numpy as jnp
from jax import lax

WIDTH = 320
HEADS = 8
HEAD_D = 40
CLIP_D = 768
GROUPS = 32
FF_D = 1280
TIME_D = 1280
UNSHUF = 192
TEXT = 77
LATENT = 4
STEP = 10
IMG = 512
PIXELS = 4096
ITEMS = 32


def touch_ends(entries, rng, least, high):
    dims = entries.shape
    spot = [jax.random.randint(jax.random.fold_in(rng, axis), (), 0, dims[axis]) for axis in range(len(dims))]
    entries = entries.at[tuple(spot)].set(least)
    longest = dims.index(max(dims))
    spot[longest] = (spot[longest] + 1) % dims[longest]
    return entries.at[tuple(spot)].set(high)


def block_levels(rng, extent, split, least, high):
    factor_of, own = 1.0, jax.random.fold_in(rng, 6)
    for axis_at, parts in split:
        heights = jnp.exp(jax.random.uniform(jax.random.fold_in(own, axis_at), (parts,), jnp.float32, least / len(split), high / len(split)))
        factor_of = factor_of * jnp.repeat(heights, extent[axis_at] // parts).reshape([-1 if axis == axis_at else 1 for axis in range(len(extent))])
    return factor_of


def bell_draw(key, dims, deviation, most, split=(), held_as=jnp.bfloat16):
    array = deviation * jax.random.normal(key, dims, jnp.float32)
    if split:
        array = array * block_levels(key, dims, split, -0.22, 0.18)
    return jnp.clip(array, -most, most).astype(held_as)


def setup_inputs(seed: int = 0) -> dict:
    splits = jax.random.split(jax.random.key(seed), 30)
    conditions = bell_draw(splits[0], (ITEMS, 3, IMG, IMG), 1.0, 6.0, ((0, 32),))
    clean_latents = bell_draw(splits[1], (ITEMS, LATENT, PIXELS), 1.0, 6.0, ((0, 32),), jnp.float32)
    noise_field = bell_draw(splits[2], (ITEMS, LATENT, PIXELS), 1.0, 6.0, ((0, 32),), jnp.float32)
    timesteps = touch_ends(jax.random.randint(splits[3], (ITEMS,), 0, 1000), jax.random.fold_in(splits[3], 1), 0, 999).astype(jnp.int32)
    text_states = bell_draw(splits[4], (ITEMS, TEXT, CLIP_D), 1.0, 6.0, ((0, 32),))
    text_lengths = touch_ends(jax.random.randint(splits[5], (ITEMS,), 5, TEXT + 1), jax.random.fold_in(splits[5], 1), 5, TEXT).astype(jnp.int32)
    item_valid = touch_ends((jax.random.randint(splits[6], (ITEMS,), 0, 4) < 3).astype(jnp.int32), jax.random.fold_in(splits[6], 1), 0, 1)
    unet_conv = bell_draw(splits[7], (9 * LATENT, WIDTH), (9 * LATENT) ** -0.5, 1.0)
    res_conv = bell_draw(splits[8], (2, 9 * WIDTH, WIDTH), (9 * WIDTH) ** -0.5, 0.109375)
    time_mlp = bell_draw(splits[9], (WIDTH, TIME_D), WIDTH ** -0.5, 0.3125)
    time_proj = bell_draw(splits[10], (TIME_D, WIDTH), (TIME_D // 4) ** -0.5, 0.3125)
    query_proj = bell_draw(splits[11], (WIDTH, WIDTH), WIDTH ** -0.5, 0.3125)
    keyvalue_proj = bell_draw(splits[12], (CLIP_D, 2 * WIDTH), CLIP_D ** -0.5, 0.21875)
    output_proj = bell_draw(splits[13], (WIDTH, WIDTH), (WIDTH // 16) ** -0.5, 1.25)
    geglu_in = bell_draw(splits[14], (WIDTH, 2 * FF_D), WIDTH ** -0.5, 0.3125)
    geglu_out = bell_draw(splits[15], (FF_D, WIDTH), WIDTH ** -0.5, 0.3125)
    velocity_proj = bell_draw(splits[16], (WIDTH, LATENT), WIDTH ** -0.5, 0.3125)
    adapter_in = bell_draw(splits[17], (9 * UNSHUF, WIDTH), (9 * UNSHUF) ** -0.5, 0.15625, ((0, 8),), jnp.float32)
    adapter_conv = bell_draw(splits[18], (9 * WIDTH, WIDTH), (9 * WIDTH) ** -0.5, 0.109375, ((0, 8),), jnp.float32)
    adapter_out = bell_draw(splits[19], (WIDTH, WIDTH), WIDTH ** -0.5, 0.3125, ((0, 8),), jnp.float32)
    adapter_bias = bell_draw(splits[20], (3 * WIDTH,), 0.05, 0.25, ((0, 8),), jnp.float32)
    first_in = bell_draw(splits[21], (9 * UNSHUF, WIDTH), (0.11 * 0.01 / (9 * UNSHUF * WIDTH + 10 * WIDTH * WIDTH + 3 * WIDTH) ** 0.5), 4.76837158203125e-06, ((0, 8),), jnp.float32)
    first_conv = bell_draw(splits[22], (9 * WIDTH, WIDTH), (0.11 * 0.01 / (9 * UNSHUF * WIDTH + 10 * WIDTH * WIDTH + 3 * WIDTH) ** 0.5), 4.76837158203125e-06, ((0, 8),), jnp.float32)
    first_out = bell_draw(splits[23], (WIDTH, WIDTH), (0.11 * 0.01 / (9 * UNSHUF * WIDTH + 10 * WIDTH * WIDTH + 3 * WIDTH) ** 0.5), 4.76837158203125e-06, ((0, 8),), jnp.float32)
    first_bias = bell_draw(splits[24], (3 * WIDTH,), (0.33 * 0.01 / (9 * UNSHUF * WIDTH + 10 * WIDTH * WIDTH + 3 * WIDTH) ** 0.5), 1.52587890625e-05, ((0, 8),), jnp.float32)
    second_in = jnp.clip(jnp.exp(math.log(2.5349828573079103e-13) - 1.3862944 * jax.random.uniform(splits[25], (9 * UNSHUF, WIDTH), jnp.float32) ** block_levels(splits[25], (9 * UNSHUF, WIDTH), ((0, 8),), -0.2, 0.2)), 6.337457143269776e-14, 2.5349828573079103e-13)
    second_conv = jnp.clip(jnp.exp(math.log(2.5349828573079103e-13) - 1.3862944 * jax.random.uniform(splits[26], (9 * WIDTH, WIDTH), jnp.float32) ** block_levels(splits[26], (9 * WIDTH, WIDTH), ((0, 8),), -0.2, 0.2)), 6.337457143269776e-14, 2.5349828573079103e-13)
    second_out = jnp.clip(jnp.exp(math.log(2.5349828573079103e-13) - 1.3862944 * jax.random.uniform(splits[27], (WIDTH, WIDTH), jnp.float32) ** block_levels(splits[27], (WIDTH, WIDTH), ((0, 8),), -0.2, 0.2)), 6.337457143269776e-14, 2.5349828573079103e-13)
    second_bias = jnp.clip(jnp.exp(math.log(2.281484463156902e-12) - 1.3862944 * jax.random.uniform(splits[28], (3 * WIDTH,), jnp.float32) ** block_levels(splits[28], (3 * WIDTH,), ((0, 8),), -0.2, 0.2)), 5.703711157892255e-13, 2.281484463156902e-12)
    return dict(conditions=conditions, clean_latents=clean_latents, noise_field=noise_field, timesteps=timesteps, text_states=text_states, text_lengths=text_lengths, item_valid=item_valid, unet_conv=unet_conv, res_conv=res_conv, time_mlp=time_mlp, time_proj=time_proj, query_proj=query_proj, keyvalue_proj=keyvalue_proj, output_proj=output_proj, geglu_in=geglu_in, geglu_out=geglu_out, velocity_proj=velocity_proj, adapter_in=adapter_in, adapter_conv=adapter_conv, adapter_out=adapter_out, adapter_bias=adapter_bias, first_in=first_in, first_conv=first_conv, first_out=first_out, first_bias=first_bias, second_in=second_in, second_conv=second_conv, second_out=second_out, second_bias=second_bias)


@jax.custom_vjp
def low(v):
    return lax.optimization_barrier(v.astype(jnp.bfloat16)).astype(jnp.float32)

@jax.custom_vjp
def low_back(v):
    return v

def low_keep(v):
    return (low(v), None)

def low_pass(kept, grad):
    return (grad,)

def back_keep(v):
    return (v, None)

def back_low(kept, grad):
    return (low(grad),)
low.defvjp(low_keep, low_pass)
low_back.defvjp(back_keep, back_low)
HIGH = lax.Precision.HIGHEST
LN_EPS = 1e-05
CLIP_MAX = 0.01
LEARN_RATE = 0.02
BETA_ONE = 0.9
BETA_TWO = 0.999
ADAM_EPS = 1e-08
WEIGHT_DECAY = 0.01

def plan():
    start = 0.00085 ** 0.5
    final = 0.012 ** 0.5
    places = jnp.arange(1000, dtype=jnp.int32).astype(jnp.float32)
    betas = (start + places * ((final - start) / 999.0)) ** 2
    return jnp.cumprod(1.0 - betas)

def lookup(table, index):
    places = jnp.arange(table.shape[0], dtype=jnp.int32)
    return jnp.sum(jnp.where(places == index, table, 0.0))

def shifted(field, tap_index, grid_side):
    chans = field.shape[-1]
    grid = field.reshape(grid_side, grid_side, chans)
    padded = jnp.pad(grid, ((1, 1), (1, 1), (0, 0)))
    row_off = tap_index // 3
    col_off = tap_index % 3
    return padded[row_off:row_off + grid_side, col_off:col_off + grid_side].reshape(grid_side * grid_side, chans)

def conv_three(field, kernel, grid_side):
    chans = field.shape[-1]
    total = jnp.zeros((field.shape[0], kernel.shape[1]), jnp.float32)
    for tap_index in range(9):
        part_rows = kernel[tap_index * chans:(tap_index + 1) * chans]
        total = total + jnp.dot(shifted(field, tap_index, grid_side), part_rows, precision=HIGH)
    return total

def unshuffle(image, grid_side):
    return image.reshape(3, grid_side, 8, grid_side, 8).transpose(1, 3, 0, 2, 4).reshape(grid_side * grid_side, 192)

def group_norm(field):
    pixels, chans = field.shape
    grouped = field.reshape(pixels, GROUPS, chans // GROUPS)
    centered = grouped - lax.optimization_barrier(jnp.mean(grouped, axis=(0, 2), keepdims=True))
    inv_std = lax.rsqrt(lax.optimization_barrier(jnp.mean(centered * centered, axis=(0, 2), keepdims=True)) + LN_EPS)
    return (centered * inv_std).reshape(pixels, chans)

def layer_norm(field):
    centered = field - lax.optimization_barrier(jnp.mean(field, axis=-1, keepdims=True))
    return centered * lax.rsqrt(lax.optimization_barrier(jnp.mean(centered * centered, axis=-1, keepdims=True)) + LN_EPS)

def item_loss(params, frozen, table, item):
    w_in, w_conv, w_out, biases = [low(entry) for entry in params]
    unet_conv, res_conv, time_mlp, time_proj, query_proj, keyvalue_proj, output_proj, geglu_in, geglu_out, velocity_proj = frozen
    image, clean, noise_field, tstep, text, length, item_flag = item
    grid_side = image.shape[-1] // 8
    width = w_in.shape[1]
    pixels = grid_side * grid_side
    base = unshuffle(image, grid_side)
    first = low_back(conv_three(base, w_in, grid_side) + biases[:width])
    inner = low_back(conv_three(low(first), w_conv, grid_side) + biases[width:2 * width])
    mixed = low(jax.nn.silu(inner))
    branch = low_back(jnp.dot(mixed, w_out, precision=HIGH) + biases[2 * width:])
    feature = first + branch
    half = width // 2
    freqs = jnp.exp(-math.log(10000.0) * jnp.arange(half, dtype=jnp.int32).astype(jnp.float32) / half)
    angles = tstep.astype(jnp.float32) * freqs
    emb = jnp.concatenate([jnp.cos(angles), jnp.sin(angles)])[None, :]
    temb = jnp.dot(low(emb), time_mlp, precision=HIGH)
    temb_add = jnp.dot(low(jax.nn.silu(temb)), time_proj, precision=HIGH)
    abar = lookup(table, tstep)
    alpha_t = jnp.sqrt(abar)
    sigma_t = jnp.sqrt(1.0 - abar)
    noisy = low(alpha_t * clean + sigma_t * noise_field)
    h_zero = conv_three(noisy.T, unet_conv, grid_side) + feature
    act_one = low(jax.nn.silu(group_norm(h_zero)))
    conv_one = low_back(conv_three(act_one, res_conv[0], grid_side) + temb_add)
    act_two = low(jax.nn.silu(group_norm(conv_one)))
    h_one = h_zero + low_back(conv_three(act_two, res_conv[1], grid_side))
    normed = low(layer_norm(h_one))
    queries = low(low_back(jnp.dot(normed, query_proj, precision=HIGH)))
    keyvals = low(jnp.dot(text, keyvalue_proj, precision=HIGH))
    query_heads = queries.reshape(pixels, HEADS, HEAD_D)
    key_heads = keyvals[:, :width].reshape(TEXT, HEADS, HEAD_D)
    value_heads = keyvals[:, width:].reshape(TEXT, HEADS, HEAD_D)
    scores = low_back(jnp.einsum('phd,thd->hpt', query_heads, key_heads, precision=HIGH) * HEAD_D ** (-0.5))
    allowed = jnp.arange(TEXT, dtype=jnp.int32) < length
    scores = jnp.where(allowed[None, None, :], scores, -1000000000.0)
    top_score = lax.optimization_barrier(jnp.max(scores, axis=-1, keepdims=True))
    expo = jnp.exp(scores - top_score)
    attend = low(expo / lax.optimization_barrier(jnp.sum(expo, axis=-1, keepdims=True)))
    heads_out = low(low_back(jnp.einsum('hpt,thd->phd', attend, value_heads, precision=HIGH).reshape(pixels, width)))
    h_two = h_one + low_back(jnp.dot(heads_out, output_proj, precision=HIGH))
    normed_two = low(layer_norm(h_two))
    proj = low_back(jnp.dot(normed_two, geglu_in, precision=HIGH))
    ff_width = geglu_out.shape[0]
    act = low(proj[:, :ff_width] * jax.nn.gelu(proj[:, ff_width:], approximate=False))
    h_three = h_two + low_back(jnp.dot(act, geglu_out, precision=HIGH))
    predicted = low_back(jnp.einsum('pc,cl->lp', low(h_three), velocity_proj, precision=HIGH))
    target = alpha_t * noise_field - sigma_t * clean
    diff = predicted - target
    return item_flag * jnp.sum(diff * diff)

def adamw(master, first, second, grad):
    new_first = BETA_ONE * first + (1.0 - BETA_ONE) * grad
    new_second = BETA_TWO * second + (1.0 - BETA_TWO) * grad * grad
    first_hat = new_first / (1.0 - BETA_ONE ** STEP)
    second_hat = new_second / (1.0 - BETA_TWO ** STEP)
    new_master = master - LEARN_RATE * (first_hat / (jnp.sqrt(second_hat) + ADAM_EPS) + WEIGHT_DECAY * master)
    return (new_first, new_second, new_master)

def reference(conditions, clean_latents, noise_field, timesteps, text_states, text_lengths, item_valid, unet_conv, res_conv, time_mlp, time_proj, query_proj, keyvalue_proj, output_proj, geglu_in, geglu_out, velocity_proj, adapter_in, adapter_conv, adapter_out, adapter_bias, first_in, first_conv, first_out, first_bias, second_in, second_conv, second_out, second_bias):
    frozen = tuple((entry.astype(jnp.float32) for entry in (unet_conv, res_conv, time_mlp, time_proj, query_proj, keyvalue_proj, output_proj, geglu_in, geglu_out, velocity_proj)))
    table = plan()
    pixels = clean_latents.shape[-1]
    channels = clean_latents.shape[1]
    count = jnp.maximum(jnp.sum(item_valid).astype(jnp.float32) * (pixels * channels), 1.0)
    items = (conditions.astype(jnp.float32), clean_latents, noise_field, timesteps, text_states.astype(jnp.float32), text_lengths, item_valid.astype(jnp.float32))
    masters = (adapter_in, adapter_conv, adapter_out, adapter_bias)

    def one_item(params, item):
        return item_loss(params, frozen, table, item)
    checked = jax.checkpoint(one_item)

    def total_loss(params):

        def scan_step(carry, item):
            return (carry + checked(params, item), None)
        total, unused = lax.scan(scan_step, jnp.zeros((), jnp.float32), items)
        return total
    loss_sum, pull_back = jax.vjp(total_loss, masters)
    grads = pull_back(jnp.ones((), jnp.float32) / count)[0]
    squares = jnp.zeros((), jnp.float32)
    for entry in grads:
        squares = squares + jnp.sum(entry * entry)
    grad_norm = jnp.sqrt(squares)
    factor = jnp.minimum(1.0, CLIP_MAX / (grad_norm + 1e-06))
    firsts = (first_in, first_conv, first_out, first_bias)
    seconds = (second_in, second_conv, second_out, second_bias)
    results = [adamw(masters[index], firsts[index], seconds[index], grads[index] * factor) for index in range(4)]
    return (loss_sum, count, grad_norm, results[0][0], results[1][0], results[2][0], results[3][0], results[0][1], results[1][1], results[2][1], results[3][1], results[0][2], results[1][2], results[2][2], results[3][2])
```

```python
import math

import jax
import jax.numpy as jnp
import numpy as np
from jax import lax
from jax.experimental import pallas as pl
from jax.experimental.pallas import tpu as pltpu
from jax.sharding import PartitionSpec as P

HEADS = 8
GROUPS = 32
STEP = 10

LN_EPS = 1e-05
CLIP_MAX = 0.01
LEARN_RATE = 0.02
BETA_ONE = 0.9
BETA_TWO = 0.999
ADAM_EPS = 1e-08
WEIGHT_DECAY = 0.01

BF = jnp.bfloat16
F32 = jnp.float32

SIDE = 64
PIX = SIDE * SIDE
LANES = 128
HALO = LANES
WIDE = PIX + 2 * HALO
CH = 320
UNS = 192
FF = 1280
TXT = 80
KEYS = HEADS * TXT
NT = (((1,), (1,)), ((), ()))
TN = (((0,), (0,)), ((), ()))
VMEM_LIMIT = 60 * 2**20


def schedule():
    start = 0.00085**0.5
    final = 0.012**0.5
    betas = (start + np.arange(1000, dtype=np.float64) * ((final - start) / 999.0)) ** 2
    return np.cumprod(1.0 - betas).astype(np.float32)


def dot(a, b):
    return jnp.dot(a, b, preferred_element_type=F32)


def dot_nt(a, b):
    return lax.dot_general(a, b, NT, preferred_element_type=F32)


def al(x):
    return pl.multiple_of(x, LANES)


def tiles(width, body):
    def step(i, carry):
        body(al(i * width))
        return carry

    lax.fori_loop(0, PIX // width, step, 0)


def put(dst, value, p0, chans):
    width = value.shape[1]
    low = value.astype(BF)
    for q in range(width // LANES):
        mid = low[:, q * LANES : (q + 1) * LANES]
        lane = lax.broadcasted_iota(jnp.int32, mid.shape, 1) & (SIDE - 1)
        up = jnp.where(lane == 0, jnp.zeros((), BF), pltpu.roll(mid, 1, 1))
        down = jnp.where(lane == SIDE - 1, jnp.zeros((), BF), pltpu.roll(mid, LANES - 1, 1))
        at = pl.ds(al(p0 + HALO + q * LANES), LANES)
        dst[0:chans, at] = up
        dst[chans : 2 * chans, at] = mid
        dst[2 * chans : 3 * chans, at] = down


def ends(dst, rows):
    last = dst[0:rows, PIX : PIX + LANES]
    head = dst[0:rows, HALO : HALO + LANES]
    lane = lax.broadcasted_iota(jnp.int32, last.shape, 1)
    zero = jnp.zeros((), BF)
    dst[0:rows, 0:LANES] = jnp.where(lane >= SIDE, pltpu.roll(last, SIDE, 1), zero)
    dst[0:rows, PIX + HALO : PIX + HALO + LANES] = jnp.where(lane < SIDE, pltpu.roll(head, SIDE, 1), zero)


def conv(weight, src, p0, width, rows):
    parts = [src[0:rows, pl.ds(al(p0 + b * LANES), width)] for b in range(3)]
    return dot(weight, jnp.concatenate(parts, axis=0))


def lane_sum(value):
    total = value[:, 0:LANES]
    for q in range(1, value.shape[1] // LANES):
        total = total + value[:, q * LANES : (q + 1) * LANES]
    return total


def group_mean(gm, sums):
    spread = jnp.dot(gm, sums, precision=lax.Precision.HIGHEST, preferred_element_type=F32)
    return jnp.sum(spread, axis=1, keepdims=True) * (1.0 / (PIX * (CH // GROUPS)))


def silu_slope(y):
    s = jax.nn.sigmoid(y)
    return s * (1.0 + y * (1.0 - s))


def layer_stats(field):
    mean = jnp.mean(field, axis=0, keepdims=True)
    centered = field - mean
    inv = lax.rsqrt(jnp.mean(centered * centered, axis=0, keepdims=True) + LN_EPS)
    return centered * inv, inv


def layer_back(grad, normed, inv):
    return inv * (
        grad
        - jnp.mean(grad, axis=0, keepdims=True)
        - normed * jnp.mean(grad * normed, axis=0, keepdims=True)
    )


def prologue_kernel(
    scal, cond, perm, clean, noise, text, kvproj, wq, wo, wot, gout_w, vel, velt, emb, tmlp, tproj,
    base, nz, target, kq, kqb, vo, vob, gvt, gvl, temb,
    zs, us,
):
    alpha = scal[0]
    sigma = scal[1]
    lane = lax.broadcasted_iota(jnp.int32, (32, 8, LANES), 2)
    for c in range(3):
        zs[...] = lax.dot_general(cond[c], perm[...], TN, preferred_element_type=F32).reshape(64, 8, 512)
        for k in range(4):
            one = zs[0:32, :, k * LANES : (k + 1) * LANES]
            two = zs[32:64, :, k * LANES : (k + 1) * LANES]
            even = jnp.where(lane < SIDE, one, pltpu.roll(two, SIDE, 2))
            odd = jnp.where(lane < SIDE, pltpu.roll(one, SIDE, 2), two)
            for m in range(32):
                us[16 * k : 16 * k + 8, m * LANES : (m + 1) * LANES] = even[m]
                us[16 * k + 8 : 16 * k + 16, m * LANES : (m + 1) * LANES] = odd[m]
        base[64 * c : 64 * (c + 1), :] = us[...].astype(BF)
    noisy = (alpha * clean[...] + sigma * noise[...]).astype(BF).astype(F32)
    target[...] = alpha * noise[...] - sigma * clean[...]
    lane = lax.broadcasted_iota(jnp.int32, (8, LANES), 1)
    slot = lane & (SIDE - 1)
    cols = [noisy[:, m * LANES : (m + 1) * LANES] for m in range(32)]
    left = jnp.where(lane >= SIDE, pltpu.roll(cols[31], SIDE, 1), 0.0)
    right = jnp.where(lane < SIDE, pltpu.roll(cols[0], SIDE, 1), 0.0)
    cols = [left] + cols + [right]
    for m in range(34):
        up = jnp.where(slot == 0, 0.0, pltpu.roll(cols[m], 1, 1))
        down = jnp.where(slot == SIDE - 1, 0.0, pltpu.roll(cols[m], LANES - 1, 1))
        for a, part in enumerate((up, cols[m], down)):
            for b in range(3):
                at = m - b
                if 0 <= at < 32:
                    row = (b * 3 + a) * 8
                    if row < 64:
                        us[row : row + 8, at * LANES : (at + 1) * LANES] = part
                    else:
                        zs[at, :, 0:LANES] = part
    nz[0:64, :] = us[...].astype(BF)
    for m in range(32):
        tail = jnp.concatenate([zs[m, :, 0:LANES], jnp.zeros((8, LANES), F32)], axis=0)
        nz[64:80, m * LANES : (m + 1) * LANES] = tail.astype(BF)
    kv = dot(text[...], kvproj[...]).astype(BF)
    keys = kv[:, 0:CH]
    values = kv[:, CH : 2 * CH]
    head_dim = CH // HEADS
    head = lax.broadcasted_iota(jnp.int32, (TXT, CH), 1)
    own = [jnp.logical_and(head >= h * head_dim, head < (h + 1) * head_dim) for h in range(HEADS)]
    zero = jnp.zeros((), BF)
    kbd = jnp.concatenate([jnp.where(own[h], keys, zero) for h in range(HEADS)], axis=0)
    vbd = jnp.concatenate([jnp.where(own[h], values, zero) for h in range(HEADS)], axis=0)
    scale = head_dim ** (-0.5)
    kq[...] = (dot_nt(kbd, wq[...]) * scale).astype(BF)
    kqb[...] = (dot_nt(wq[...], kbd) * scale).astype(BF)
    vo[...] = dot_nt(wot[...], vbd).astype(BF)
    vob[...] = dot(vbd, wo[...]).astype(BF)
    fold_t = dot_nt(velt[...], gout_w[...])
    high_t = fold_t.astype(BF)
    gvt[...] = jnp.concatenate([high_t, (fold_t - high_t.astype(F32)).astype(BF)], axis=0)
    fold = dot(gout_w[...], vel[...])
    high = fold.astype(BF)
    low = (fold - high.astype(F32)).astype(BF)
    gvl[0:FF, :] = jnp.concatenate([high[:, 0:8], low[:, 0:8]], axis=1)
    gvl[FF : FF + CH, :] = vel[:, 0:16]
    hidden = dot(emb[...], tmlp[...])
    row = dot(jax.nn.silu(hidden).astype(BF), tproj[...])
    rows_i = lax.broadcasted_iota(jnp.int32, (CH, CH), 0)
    cols_i = lax.broadcasted_iota(jnp.int32, (CH, CH), 1)
    eye = jnp.where(rows_i == cols_i, 1.0, 0.0)
    full = jnp.concatenate([row] * 16, axis=0)
    temb[...] = lax.dot_general(eye, full, NT, precision=lax.Precision.HIGHEST, preferred_element_type=F32)


def prologue(scal, cond, perm, clean, noise, text, kvproj, wq, wo, wot, gout_w, vel, velt, emb, tmlp, tproj):
    vm = pl.BlockSpec(memory_space=pltpu.VMEM)
    sm = pl.BlockSpec(memory_space=pltpu.SMEM)
    shapes = [
        ((UNS, PIX), BF), ((80, PIX), BF), ((8, PIX), F32),
        ((KEYS, CH), BF), ((CH, KEYS), BF), ((CH, KEYS), BF), ((KEYS, CH), BF),
        ((16, FF), BF), ((FF + CH, 16), BF), ((CH, LANES), F32),
    ]
    return pl.pallas_call(
        prologue_kernel,
        out_shape=[jax.ShapeDtypeStruct(*s) for s in shapes],
        in_specs=[sm] + [vm] * 15,
        out_specs=[vm] * len(shapes),
        scratch_shapes=[pltpu.VMEM((64, 8, 512), F32), pltpu.VMEM((64, PIX), F32)],
        compiler_params=pltpu.CompilerParams(vmem_limit_bytes=VMEM_LIMIT),
        cost_estimate=pl.CostEstimate(flops=4_000_000_000, bytes_accessed=10_000_000, transcendentals=0),
        name="prologue",
    )(scal, cond, perm, clean, noise, text, kvproj, wq, wo, wot, gout_w, vel, velt, emb, tmlp, tproj)


TILE = 512
WIN = 1792
TILE_D = 256
CHUNK = 256


def main_kernel(
    scal, ilen, target, kq, kqb, vo, vob, gvt, gvl, velt, temb, bcols, gm, wou, wout,
    base, nz, win, wcf, wf, wb, git_hbm, gi_hbm,
    loss, gconv, gout, gbias, ginner_hbm, gh_hbm,
    sa, sb, hg, cu, y1s, y2s, flow, mx, ds, wbuf, git, gi, acc, stat, sems,
):
    flag = scal[2]
    fetch = [
        pltpu.make_async_copy(wcf, wbuf.at[0], sems.at[0]),
        pltpu.make_async_copy(wf.at[0], wbuf.at[1], sems.at[1]),
        pltpu.make_async_copy(wf.at[1], wbuf.at[0], sems.at[2]),
        pltpu.make_async_copy(wb.at[1], wbuf.at[1], sems.at[3]),
        pltpu.make_async_copy(wb.at[0], wbuf.at[0], sems.at[4]),
    ]
    get_git = pltpu.make_async_copy(git_hbm, git, sems.at[5])
    get_gi = pltpu.make_async_copy(gi_hbm, gi, sems.at[6])
    get_base = pltpu.make_async_copy(base, flow.at[0:UNS, :], sems.at[9])
    get_nz = pltpu.make_async_copy(nz, mx.at[CH : CH + 80, :], sems.at[10])
    get_win = pltpu.make_async_copy(win, wbuf.at[1, :, 0:WIN], sems.at[11])
    get_base.start()
    get_win.start()
    fetch[0].start()
    get_nz.start()
    get_git.start()
    get_gi.start()
    get_base.wait()

    def body(p0):
        put(sa, flow[0:UNS, pl.ds(p0, TILE)], p0, UNS)

    tiles(TILE, body)
    ends(sa, 3 * UNS)
    get_win.wait()

    def body(p0):
        at = pl.ds(p0, TILE)
        first = conv(wbuf[1, :, 0 : 9 * UNS], sa, p0, TILE, 3 * UNS) + bcols[:, 0:1]
        hg[:, at] = first
        low = first.astype(BF)
        flow[:, at] = low
        put(sb, low, p0, CH)

    tiles(TILE, body)
    ends(sb, 3 * CH)

    get_nz.wait()
    fetch[1].start()
    acc[...] = jnp.zeros_like(acc)
    fetch[0].wait()

    def body(p0):
        at = pl.ds(p0, TILE)
        inner = conv(wbuf[0], sb, p0, TILE, 3 * CH) + bcols[:, 1:2]
        s = jax.nn.sigmoid(inner)
        m = inner * s
        mx[0:CH, at] = m.astype(BF)
        ds[:, at] = (s + m * (1.0 - s)).astype(BF)
        h0 = hg[:, at] + dot(wou[...], mx[:, at]) + bcols[:, 2:3]
        hg[:, at] = h0
        acc[0] += lane_sum(h0)

    tiles(TILE, body)

    def norm_silu(field, store, dst, which):
        mean = group_mean(gm[...], acc[0])
        acc[1] = jnp.zeros_like(acc[1])

        def body(p0):
            centered = field[:, pl.ds(p0, TILE)] - mean
            acc[1] += lane_sum(centered * centered)

        tiles(TILE, body)
        inv = lax.rsqrt(group_mean(gm[...], acc[1]) + LN_EPS)
        stat[which] = jnp.broadcast_to(inv, (CH, LANES))

        def body(p0):
            at = pl.ds(p0, TILE)
            y = (field[:, at] - mean) * inv
            store[:, at] = y.astype(BF)
            put(dst, y * jax.nn.sigmoid(y), p0, CH)

        tiles(TILE, body)
        ends(dst, 3 * CH)
        acc[...] = jnp.zeros_like(acc)

    fetch[2].start()
    norm_silu(hg, y1s, sa, 0)
    fetch[1].wait()

    def body(p0):
        at = pl.ds(p0, TILE)
        c1 = conv(wbuf[1], sa, p0, TILE, 3 * CH) + temb[:, 0:1]
        cu[:, at] = c1
        acc[0] += lane_sum(c1)

    tiles(TILE, body)
    fetch[3].start()
    norm_silu(cu, y2s, sb, 1)

    fetch[2].wait()
    get_git.wait()
    get_gi.wait()
    loss[...] = jnp.zeros_like(loss)
    length = ilen[0]
    token = lax.broadcasted_iota(jnp.int32, (1, TXT, 1), 1)
    bias = jnp.where(token < length, 0.0, -1000000000.0)

    def body(p0):
        at = pl.ds(p0, TILE_D)
        h1 = hg[:, at] + conv(wbuf[0], sb, p0, TILE_D, 3 * CH)
        normed, inv = layer_stats(h1)
        s = dot(kq[...], normed.astype(BF)).reshape(HEADS, TXT, TILE_D) + bias
        e = jnp.exp(s - jnp.max(s, axis=1, keepdims=True))
        attend = e * (1.0 / jnp.sum(e, axis=1, keepdims=True))
        h2 = h1 + dot(vo[...], attend.reshape(KEYS, TILE_D).astype(BF))
        normed2, inv2 = layer_stats(h2)
        n2 = normed2.astype(BF)
        parts = []
        pred = dot(velt[...], h2.astype(BF))
        for f in range(0, FF, CHUNK):
            val = dot(git[f : f + CHUNK, :], n2)
            gate = dot(git[FF + f : FF + f + CHUNK, :], n2)
            phi = 0.5 + 0.5 * lax.erf(gate * 0.5**0.5)
            u = gate * phi
            slope = phi + gate * (jnp.exp(-0.5 * gate * gate) * (2.0 * math.pi) ** (-0.5))
            act = (val * u).astype(BF)
            both = dot(gvt[:, f : f + CHUNK], act)
            pred = pred + (both[0:8] + both[8:16])
            parts.append((u, val * slope))
        diff = pred - target[:, at]
        loss[...] += lane_sum(diff * diff) * flag
        gp = (diff * (2.0 * flag)).astype(BF)
        gp = jnp.concatenate([gp, gp], axis=0)
        pieces = []
        for k in (0, 1):
            for n, f in enumerate(range(0, FF, CHUNK)):
                g_act = dot(gvl[f : f + CHUNK, :], gp)
                pieces.append((g_act * parts[n][k]).astype(BF))
        g3 = dot(gvl[FF : FF + CH, :], gp)
        g_n2 = dot(gi[...], jnp.concatenate(pieces, axis=0))
        g2 = g3 + layer_back(g_n2, normed2, inv2)
        g_att = dot(vob[...], g2.astype(BF)).reshape(HEADS, TXT, TILE_D)
        prod = attend * g_att
        g_s = prod - attend * jnp.sum(prod, axis=1, keepdims=True)
        g_n = dot(kqb[...], g_s.reshape(KEYS, TILE_D).astype(BF))
        g1 = g2 + layer_back(g_n, normed, inv)
        hg[:, at] = g1
        put(sa, g1, p0, CH)

    tiles(TILE_D, body)
    ends(sa, 3 * CH)

    def conv_back(weight, src, ys):
        def body(p0):
            at = pl.ds(p0, TILE)
            y = ys[:, at].astype(F32)
            u = conv(weight[...], src, p0, TILE, 3 * CH) * silu_slope(y)
            cu[:, at] = u
            acc[0] += lane_sum(u)
            acc[1] += lane_sum(u * y)

        acc[...] = jnp.zeros_like(acc)
        tiles(TILE, body)
        return group_mean(gm[...], acc[0]), group_mean(gm[...], acc[1])

    fetch[4].start()
    fetch[3].wait()
    mean, cross = conv_back(wbuf.at[1], sa, y2s)
    inv = stat[1][:, 0:1]

    def body(p0):
        at = pl.ds(p0, TILE)
        put(sb, inv * (cu[:, at] - mean - y2s[:, at].astype(F32) * cross), p0, CH)

    tiles(TILE, body)
    ends(sb, 3 * CH)
    fetch[4].wait()
    mean, cross = conv_back(wbuf.at[0], sb, y1s)
    inv = stat[0][:, 0:1]

    gout[...] = jnp.zeros_like(gout)
    gbias[...] = jnp.zeros_like(gbias)

    def body(p0):
        at = pl.ds(p0, TILE)
        g0 = hg[:, at] + inv * (cu[:, at] - mean - y1s[:, at].astype(F32) * cross)
        hg[:, at] = g0
        branch = g0.astype(BF)
        g_inner = (dot(wout[...], branch) * ds[:, at].astype(F32)).astype(BF)
        put(sa, g_inner, p0, CH)
        gout[...] += dot_nt(mx[0:CH, at], branch)
        gbias[0] += lane_sum(g_inner.astype(F32))
        gbias[1] += lane_sum(branch.astype(F32))

    tiles(TILE, body)
    send_h = pltpu.make_async_copy(hg, gh_hbm, sems.at[7])
    send_g = pltpu.make_async_copy(sa.at[CH : 2 * CH, HALO : HALO + PIX], ginner_hbm, sems.at[8])
    send_h.start()
    send_g.start()
    ends(sa, 3 * CH)

    for b in range(3):
        grad = dot_nt(flow[...], sa[0 : 3 * CH, b * LANES : b * LANES + PIX])
        for a in range(3):
            t = 8 - 3 * a - b
            gconv[t * CH : (t + 1) * CH, :] = grad[:, a * CH : (a + 1) * CH].astype(BF)
    send_h.wait()
    send_g.wait()


def main_call(scal, ilen, *rest):
    vm = pl.BlockSpec(memory_space=pltpu.VMEM)
    sm = pl.BlockSpec(memory_space=pltpu.SMEM)
    hb = pl.BlockSpec(memory_space=pl.ANY)
    shapes = [
        ((8, LANES), F32), ((9 * CH, CH), BF), ((CH, CH), F32), ((2, CH, LANES), F32),
        ((CH, PIX), BF), ((CH, PIX), F32),
    ]
    return pl.pallas_call(
        main_kernel,
        out_shape=[jax.ShapeDtypeStruct(*s) for s in shapes],
        in_specs=[sm, sm] + [vm] * 13 + [hb] * 8,
        out_specs=[vm] * 4 + [hb] * 2,
        scratch_shapes=[
            pltpu.VMEM((3 * CH, WIDE), BF),
            pltpu.VMEM((3 * CH, WIDE), BF),
            pltpu.VMEM((CH, PIX), F32),
            pltpu.VMEM((CH, PIX), F32),
            pltpu.VMEM((CH, PIX), BF),
            pltpu.VMEM((CH, PIX), BF),
            pltpu.VMEM((CH, PIX), BF),
            pltpu.VMEM((CH + 80, PIX), BF),
            pltpu.VMEM((CH, PIX), BF),
            pltpu.VMEM((2, CH, 9 * CH), BF),
            pltpu.VMEM((2 * FF, CH), BF),
            pltpu.VMEM((CH, 2 * FF), BF),
            pltpu.VMEM((2, CH, LANES), F32),
            pltpu.VMEM((2, CH, LANES), F32),
            pltpu.SemaphoreType.DMA((12,)),
        ],
        compiler_params=pltpu.CompilerParams(vmem_limit_bytes=VMEM_LIMIT),
        cost_estimate=pl.CostEstimate(flops=80_000_000_000, bytes_accessed=40_000_000, transcendentals=0),
        name="main",
    )(scal, ilen, *rest)


def tail_kernel(ginner, base, wcb, gh_hbm, gin, gbias, sa, sb, gh, sem):
    fetch = pltpu.make_async_copy(gh_hbm, gh, sem)
    fetch.start()

    def body(p0):
        put(sa, ginner[:, pl.ds(p0, TILE)], p0, CH)

    tiles(TILE, body)
    ends(sa, 3 * CH)
    gbias[...] = jnp.zeros_like(gbias)
    fetch.wait()

    def body(p0):
        at = pl.ds(p0, TILE)
        g_first = (gh[:, at] + conv(wcb[...], sa, p0, TILE, 3 * CH)).astype(BF)
        put(sb, g_first, p0, CH)
        gbias[...] += lane_sum(g_first.astype(F32))

    tiles(TILE, body)
    ends(sb, 3 * CH)
    for b in range(3):
        grad = dot_nt(base[...], sb[0 : 3 * CH, b * LANES : b * LANES + PIX])
        for a in range(3):
            t = 8 - 3 * a - b
            gin[t * UNS : (t + 1) * UNS, :] = grad[:, a * CH : (a + 1) * CH].astype(BF)


def tail_call(ginner, base, wcb, gh):
    vm = pl.BlockSpec(memory_space=pltpu.VMEM)
    hb = pl.BlockSpec(memory_space=pl.ANY)
    return pl.pallas_call(
        tail_kernel,
        out_shape=[jax.ShapeDtypeStruct((9 * UNS, CH), BF), jax.ShapeDtypeStruct((CH, LANES), F32)],
        in_specs=[vm, vm, vm, hb],
        out_specs=[vm, vm],
        scratch_shapes=[
            pltpu.VMEM((3 * CH, WIDE), BF),
            pltpu.VMEM((3 * CH, WIDE), BF),
            pltpu.VMEM((CH, PIX), F32),
            pltpu.SemaphoreType.DMA(()),
        ],
        compiler_params=pltpu.CompilerParams(vmem_limit_bytes=VMEM_LIMIT),
        cost_estimate=pl.CostEstimate(flops=12_000_000_000, bytes_accessed=12_000_000, transcendentals=0),
        name="tail",
    )(ginner, base, wcb, gh)


def pixel_order(field):
    grid = field.reshape(4, SIDE, 2, SIDE // 2).transpose(0, 3, 2, 1).reshape(4, PIX)
    return jnp.pad(grid, ((0, 4), (0, 0)))


def forward_rows(weight, chans):
    return weight.reshape(3, 3, chans, CH).transpose(3, 1, 0, 2).reshape(CH, 9 * chans)


def backward_rows(weight):
    return weight.reshape(3, 3, CH, CH)[::-1, ::-1].transpose(2, 1, 0, 3).reshape(CH, 9 * CH)


def unshuffle_order():
    perm = np.zeros((512, 512), np.float32)
    for i in range(SIDE):
        for u in range(8):
            perm[i * 8 + u, u * SIDE + i] = 1.0
    return perm


def group_matrix():
    ids = np.arange(CH) // (CH // GROUPS)
    return (ids[:, None] == ids[None, :]).astype(np.float32)


def early(item, frozen):
    cond, clean, noise, tstep, text, length, flag = item
    unet_conv, res_conv, time_mlp, time_proj, wq, kvproj, wo, geglu_in, geglu_out, vel = frozen
    abar = jnp.asarray(schedule())[tstep]
    scal = jnp.stack([jnp.sqrt(abar), jnp.sqrt(1.0 - abar), flag, flag])
    half = CH // 2
    freqs = jnp.exp(-math.log(10000.0) * jnp.arange(half, dtype=jnp.int32).astype(F32) / half)
    angles = tstep.astype(F32) * freqs
    emb = jnp.concatenate([jnp.cos(angles), jnp.sin(angles)])[None, :].astype(BF)
    emb = jnp.broadcast_to(emb, (8, CH))
    perm = jnp.asarray(unshuffle_order(), BF)
    velt = jnp.pad(vel.T, ((0, 4), (0, 0)))
    velp = jnp.pad(vel, ((0, 0), (0, 12)))
    outs = prologue(
        scal, cond, perm, pixel_order(clean), pixel_order(noise), jnp.pad(text, ((0, TXT - text.shape[0]), (0, 0))),
        kvproj, wq, wo, wo.T, geglu_out, velp, velt, emb, time_mlp, time_proj,
    )
    wut = jnp.pad(unet_conv.reshape(3, 3, 4, CH).transpose(1, 0, 2, 3), ((0, 0), (0, 0), (0, 4), (0, 0)))
    wut = jnp.pad(wut.reshape(72, CH).T, ((0, 0), (0, 8)))
    wf = jnp.stack([forward_rows(res_conv[0], CH), forward_rows(res_conv[1], CH)])
    wb = jnp.stack([backward_rows(res_conv[0]), backward_rows(res_conv[1])])
    return scal, length.reshape(1), outs, velt, wut, wf, wb, geglu_in.T, geglu_in


def late(state, weights):
    scal, ilen, outs, velt, wut, wf, wb, git, gi = state
    base, nz, target, kq, kqb, vo, vob, gvt, gvl, temb = outs
    w_in, w_conv, w_out, biases = weights
    bcols = biases.astype(F32).reshape(3, CH).T
    wou = jnp.concatenate([w_out.T, wut], axis=1)
    gm = jnp.asarray(group_matrix())
    loss, gconv, gout, gbias, ginner, gh = main_call(
        scal, ilen, target, kq, kqb, vo, vob, gvt, gvl, velt, temb, bcols, gm, wou, w_out,
        base, nz, jnp.pad(forward_rows(w_in, UNS), ((0, 0), (0, WIN - 9 * UNS))), forward_rows(w_conv, CH), wf, wb, git, gi,
    )
    gin, gbin = tail_call(ginner, base, backward_rows(w_conv), gh)
    grad_bias = jnp.concatenate([jnp.sum(gbin, axis=1), jnp.sum(gbias, axis=2).reshape(-1)])
    return jnp.sum(loss), (gin, gconv, gout.astype(BF), grad_bias.astype(BF))


def adamw(master, first, second, grad):
    new_first = BETA_ONE * first + (1.0 - BETA_ONE) * grad
    new_second = BETA_TWO * second + (1.0 - BETA_TWO) * grad * grad
    first_hat = new_first / (1.0 - BETA_ONE**STEP)
    second_hat = new_second / (1.0 - BETA_TWO**STEP)
    new_master = master - LEARN_RATE * (
        first_hat / (jnp.sqrt(second_hat) + ADAM_EPS) + WEIGHT_DECAY * master
    )
    return (new_first, new_second, new_master)


def per_device(*args):
    conditions, clean, noise, tsteps, text, lengths, valid = args[:7]
    frozen = args[7:17]
    masters, firsts, seconds = args[17:21], args[21:25], args[25:29]
    weights = tuple(lax.all_gather(entry.astype(BF), "shard", axis=0, tiled=True) for entry in masters)
    item = (conditions[0], clean[0], noise[0], tsteps[0], text[0], lengths[0], valid[0].astype(F32))
    state = early(item, frozen)
    loss, grads = late(state, weights)
    owned = []
    for grad in grads:
        part = lax.psum_scatter(grad, "shard", scatter_dimension=0, tiled=True)
        owned.append(lax.psum(part, "dp").astype(F32))
    squares = jnp.zeros((), F32)
    for entry in owned:
        squares = squares + jnp.sum(entry * entry)
    pixels, channels = clean.shape[-1], clean.shape[1]
    local_count = jnp.sum(valid).astype(F32) * (pixels * channels)
    loss_sum, squares, count = lax.psum((loss, squares, local_count), ("dp", "shard"))
    count = jnp.maximum(count, 1.0)
    grad_norm = jnp.sqrt(squares / lax.axis_size("dp")) / count
    factor = jnp.minimum(1.0, CLIP_MAX / (grad_norm + 1e-06)) / count
    results = [adamw(masters[k], firsts[k], seconds[k], owned[k] * factor) for k in range(4)]
    return (loss_sum, count, grad_norm, *[results[k][n] for n in range(3) for k in range(4)])


def solution(mesh):
    both = ("dp", "shard")
    placed = (
        (P(both, None, None, None), P(both, None, None), P(both, None, None), P(both), P(both, None, None), P(both), P(both))
        + (P(),) * 10
        + (P("shard", None), P("shard", None), P("shard", None), P("shard")) * 3
    )
    return jax.shard_map(
        per_device,
        mesh=mesh,
        in_specs=placed,
        out_specs=(P(), P(), P()) + (P("shard", None), P("shard", None), P("shard", None), P("shard")) * 3,
        check_vma=False,
    )
```

```python
import math

import jax
import jax.numpy as jnp
import numpy as np
from jax import lax
from jax.experimental import pallas as pl
from jax.experimental.pallas import tpu as pltpu
from jax.sharding import PartitionSpec as P

HEADS = 8
GROUPS = 32
STEP = 10

LN_EPS = 1e-05
CLIP_MAX = 0.01
LEARN_RATE = 0.02
BETA_ONE = 0.9
BETA_TWO = 0.999
ADAM_EPS = 1e-08
WEIGHT_DECAY = 0.01

BF = jnp.bfloat16
F32 = jnp.float32

SIDE = 64
PIX = SIDE * SIDE
LANES = 128
HALO = LANES
WIDE = PIX + 2 * HALO
CH = 320
UNS = 192
FF = 1280
TXT = 80
KEYS = HEADS * TXT
NZ = 48
NT = (((1,), (1,)), ((), ()))
TN = (((0,), (0,)), ((), ()))
VMEM_LIMIT = 60 * 2**20

TILE = 512
TILE_D = 512
CHAINS = 1
SPAN_D = TILE_D * CHAINS
CHUNK = 320


def schedule():
    start = 0.00085**0.5
    final = 0.012**0.5
    betas = (start + np.arange(1000, dtype=np.float64) * ((final - start) / 999.0)) ** 2
    table = np.zeros(1024, np.float32)
    table[:1000] = np.cumprod(1.0 - betas)
    return table.reshape(8, LANES)


def dot(a, b):
    return jnp.dot(a, b, preferred_element_type=F32)


def dot_nt(a, b):
    return lax.dot_general(a, b, NT, preferred_element_type=F32)


def al(x):
    return pl.multiple_of(x, LANES)


def tiles(width, body):
    def step(i, carry):
        body(al(i * width))
        return carry

    lax.fori_loop(0, PIX // width, step, 0)


def put(dst, value, p0, chans):
    width = value.shape[1]
    low = value.astype(BF)
    for q in range(width // LANES):
        mid = low[:, q * LANES : (q + 1) * LANES]
        lane = lax.broadcasted_iota(jnp.int32, mid.shape, 1) & (SIDE - 1)
        up = jnp.where(lane == 0, jnp.zeros((), BF), pltpu.roll(mid, 1, 1))
        down = jnp.where(lane == SIDE - 1, jnp.zeros((), BF), pltpu.roll(mid, LANES - 1, 1))
        at = pl.ds(al(p0 + HALO + q * LANES), LANES)
        dst[0:chans, at] = up
        dst[chans : 2 * chans, at] = mid
        dst[2 * chans : 3 * chans, at] = down


def ends(dst, rows):
    last = dst[0:rows, PIX : PIX + LANES]
    head = dst[0:rows, HALO : HALO + LANES]
    lane = lax.broadcasted_iota(jnp.int32, last.shape, 1)
    zero = jnp.zeros((), BF)
    dst[0:rows, 0:LANES] = jnp.where(lane >= SIDE, pltpu.roll(last, SIDE, 1), zero)
    dst[0:rows, PIX + HALO : PIX + HALO + LANES] = jnp.where(lane < SIDE, pltpu.roll(head, SIDE, 1), zero)


def conv(weight, src, p0, width, chans):
    parts = []
    for a in range(3):
        for b in range(3):
            parts.append(src[a * chans : (a + 1) * chans, pl.ds(al(p0 + b * LANES), width)])
    return dot(weight, jnp.concatenate(parts, axis=0))


def backward_weight(weight, natural):
    natural[...] = weight.T
    blocks = [natural[(8 - t) * CH : (9 - t) * CH, :] for t in range(9)]
    return jnp.concatenate(blocks, axis=1)


def lane_sum(value):
    total = value[:, 0:LANES]
    for q in range(1, value.shape[1] // LANES):
        total = total + value[:, q * LANES : (q + 1) * LANES]
    return total


def group_mean(gm, sums):
    spread = jnp.dot(gm, sums, precision=lax.Precision.HIGHEST, preferred_element_type=F32)
    return jnp.sum(spread, axis=1, keepdims=True) * (1.0 / (PIX * (CH // GROUPS)))


def silu_slope(y):
    s = jax.nn.sigmoid(y)
    return s * (1.0 + y * (1.0 - s))


def layer_stats(field):
    mean = jnp.mean(field, axis=0, keepdims=True)
    centered = field - mean
    inv = lax.rsqrt(jnp.mean(centered * centered, axis=0, keepdims=True) + LN_EPS)
    return centered * inv, inv


def layer_back(grad, normed, inv):
    return inv * (
        grad
        - jnp.mean(grad, axis=0, keepdims=True)
        - normed * jnp.mean(grad * normed, axis=0, keepdims=True)
    )


def slot(owner, me, count):
    rel = jnp.bitwise_xor(owner, me)
    return (rel & 1) * (count // 2) + lax.shift_right_logical(rel, 1)


def scatter(dst, value, start, width, lane0, me, count):
    stop = start + value.shape[1]
    for owner in range(count):
        lo, hi = max(start, owner * width), min(stop, (owner + 1) * width)
        if lo < hi:
            at = lane0 + lo - owner * width
            dst[slot(owner, me, count), 0:CH, at : at + hi - lo] = value[:, lo - start : hi - start].astype(BF)


def prologue_kernel(
    steps, table, cond, lat, text, kvproj, wq, wo, gi, got, velt_in, emb, tmlp, tprojt, unet, res,
    base, nz, target, kq, kqb, vo, vob, gvt, gvl, velt, temb, wut, git, wb,
    zs, us, kvs, nat, wsrc, sems,
):
    fetch = [pltpu.make_async_copy(res.at[k], wsrc.at[k], sems.at[k]) for k in range(2)]
    for copy in fetch:
        copy.start()
    index = lax.broadcasted_iota(jnp.int32, (8, LANES), 0) * LANES + lax.broadcasted_iota(jnp.int32, (8, LANES), 1)
    picked = jnp.where(index == steps[0], table[...], 0.0)
    abar = jnp.sum(jnp.sum(picked, axis=1, keepdims=True), axis=0, keepdims=True)
    alpha = jnp.sqrt(abar)
    sigma = jnp.sqrt(1.0 - abar)
    row = lax.broadcasted_iota(jnp.int32, (512, 512), 0)
    col = lax.broadcasted_iota(jnp.int32, (512, 512), 1)
    same = jnp.logical_and((row & 7) == (col >> 6), (row >> 3) == (col & 63))
    perm = jnp.where(same, 1.0, 0.0).astype(BF)
    lane = lax.broadcasted_iota(jnp.int32, (32, 8, LANES), 2)
    for c in range(3):
        zs[...] = lax.dot_general(cond[c], perm, TN, preferred_element_type=F32).reshape(64, 8, 512)
        for k in range(4):
            one = zs[0:32, :, k * LANES : (k + 1) * LANES]
            two = zs[32:64, :, k * LANES : (k + 1) * LANES]
            even = jnp.where(lane < SIDE, one, pltpu.roll(two, SIDE, 2))
            odd = jnp.where(lane < SIDE, pltpu.roll(one, SIDE, 2), two)
            for m in range(32):
                us[16 * k : 16 * k + 8, m * LANES : (m + 1) * LANES] = even[m]
                us[16 * k + 8 : 16 * k + 16, m * LANES : (m + 1) * LANES] = odd[m]
        base[64 * c : 64 * (c + 1), :] = us[...].astype(BF)
    clean = lat[0]
    noise = lat[1]
    noisy = (alpha * clean + sigma * noise).astype(BF).astype(F32)
    target[4:8, :] = jnp.zeros((4, PIX), F32)
    target[0:4, :] = alpha * noise - sigma * clean
    lane = lax.broadcasted_iota(jnp.int32, (4, LANES), 1)
    inside = lane & (SIDE - 1)
    cols = [noisy[:, m * LANES : (m + 1) * LANES] for m in range(32)]
    left = jnp.where(lane >= SIDE, pltpu.roll(cols[31], SIDE, 1), 0.0)
    right = jnp.where(lane < SIDE, pltpu.roll(cols[0], SIDE, 1), 0.0)
    cols = [left] + cols + [right]
    us[0:NZ, :] = jnp.zeros((NZ, PIX), F32)
    for m in range(34):
        up = jnp.where(inside == 0, 0.0, pltpu.roll(cols[m], 1, 1))
        down = jnp.where(inside == SIDE - 1, 0.0, pltpu.roll(cols[m], LANES - 1, 1))
        for a, part in enumerate((up, cols[m], down)):
            for b in range(3):
                at = m - b
                if 0 <= at < 32:
                    r = (3 * a + b) * 4
                    us[r : r + 4, at * LANES : (at + 1) * LANES] = part
    nz[...] = us[0:NZ, :].astype(BF)
    us[0:LANES // 2, 0:CH] = jnp.zeros((LANES // 2, CH), F32)
    us[0:36, 0:CH] = unet[...].astype(F32)
    wide = jnp.concatenate([us[0:64, 0:CH], jnp.zeros((64, CH), F32)], axis=0)
    wut[...] = wide.T.astype(BF)
    kvs[...] = jnp.zeros_like(kvs)
    kvs[0 : text.shape[0], :] = dot(text[...], kvproj[...])
    keys = kvs[:, 0:CH].astype(BF)
    values = kvs[:, CH : 2 * CH].astype(BF)
    head_dim = CH // HEADS
    head = lax.broadcasted_iota(jnp.int32, (TXT, CH), 1)
    own = [jnp.logical_and(head >= h * head_dim, head < (h + 1) * head_dim) for h in range(HEADS)]
    zero = jnp.zeros((), BF)
    kbd = jnp.concatenate([jnp.where(own[h], keys, zero) for h in range(HEADS)], axis=0)
    vbd = jnp.concatenate([jnp.where(own[h], values, zero) for h in range(HEADS)], axis=0)
    scale = head_dim ** (-0.5)
    fold = dot_nt(kbd, wq[...]) * scale
    kq[...] = fold.astype(BF)
    kqb[...] = fold.T.astype(BF)
    fold = dot(vbd, wo[...])
    vob[...] = fold.astype(BF)
    vo[...] = fold.T.astype(BF)
    us[0:8, 0:CH] = jnp.zeros((8, CH), F32)
    us[0:4, 0:CH] = velt_in[...].astype(F32)
    velf = us[0:8, 0:CH]
    velt[...] = velf.astype(BF)
    fold = dot(velf.astype(BF), got[...])
    high = fold.astype(BF).astype(F32)
    both = jnp.concatenate([high, fold - high], axis=0)
    gvt[...] = both.astype(BF)
    wide = jnp.concatenate([both, jnp.zeros((LANES - 16, FF), F32)], axis=0)
    gvl[0:FF, :] = wide.T[:, 0:16].astype(BF)
    wide = jnp.concatenate([velf, jnp.zeros((LANES - 8, CH), F32)], axis=0)
    gvl[FF : FF + CH, :] = wide.T[:, 0:16].astype(BF)
    git[...] = gi[...].T
    hidden = jax.nn.silu(dot(emb[...], tmlp[...])).astype(BF)
    temb[...] = dot_nt(tprojt[...], jnp.concatenate([hidden] * 8, axis=0))
    for k in range(2):
        fetch[k].wait()
        wb[k] = backward_weight(wsrc[k], nat)


def prologue(*args):
    vm = pl.BlockSpec(memory_space=pltpu.VMEM)
    sm = pl.BlockSpec(memory_space=pltpu.SMEM)
    hb = pl.BlockSpec(memory_space=pl.ANY)
    shapes = [
        ((UNS, PIX), BF), ((NZ, PIX), BF), ((8, PIX), F32),
        ((KEYS, CH), BF), ((CH, KEYS), BF), ((CH, KEYS), BF), ((KEYS, CH), BF),
        ((16, FF), BF), ((FF + CH, 16), BF), ((8, CH), BF), ((CH, LANES), F32), ((CH, LANES), BF),
        ((2 * FF, CH), BF), ((2, CH, 9 * CH), BF),
    ]
    return pl.pallas_call(
        prologue_kernel,
        out_shape=[jax.ShapeDtypeStruct(*s) for s in shapes],
        in_specs=[sm] + [vm] * 14 + [hb],
        out_specs=[vm] * len(shapes),
        scratch_shapes=[
            pltpu.VMEM((64, 8, 512), F32),
            pltpu.VMEM((64, PIX), F32),
            pltpu.VMEM((TXT, 2 * CH), F32),
            pltpu.VMEM((9 * CH, CH), BF),
            pltpu.VMEM((2, CH, 9 * CH), BF),
            pltpu.SemaphoreType.DMA((2,)),
        ],
        compiler_params=pltpu.CompilerParams(vmem_limit_bytes=VMEM_LIMIT),
        cost_estimate=pl.CostEstimate(flops=12_000_000_000, bytes_accessed=20_000_000, transcendentals=0),
        name="prologue",
    )(*args)


def main_kernel(
    ints, target, kq, kqb, vo, vob, gvt, gvl, velt, temb, wut,
    mine_one, theirs_one, mine_two, theirs_two, base, nz, wf, wb, git_hbm, gi_hbm,
    loss, gout, gbias, keep_hbm, send_hbm, ginner_hbm, gh_hbm, wcf_hbm, sf_hbm, mx_hbm, ds_hbm,
    sa, sb, hg, cu, y1s, y2s, wbuf, git, gi, acc, stat, gm, bcols, wou, sems, wsems,
):
    length = ints[0]
    flag = ints[1].astype(F32)
    me = ints[2]
    half, _, wide_one = mine_one.shape
    count = 2 * half
    w_conv = mine_two.shape[2]
    w_in = 9 * UNS // count
    w_out = CH // count
    w_bias = 3 * CH // count
    fetch = [
        pltpu.make_async_copy(wf.at[0], wbuf.at[1], sems.at[1]),
        pltpu.make_async_copy(wf.at[1], wbuf.at[0], sems.at[2]),
        pltpu.make_async_copy(wb.at[1], wbuf.at[1], sems.at[3]),
        pltpu.make_async_copy(wb.at[0], wbuf.at[0], sems.at[4]),
    ]
    get_git = pltpu.make_async_copy(git_hbm, git, sems.at[5])
    get_gi = pltpu.make_async_copy(gi_hbm, gi, sems.at[6])
    keep_first = pltpu.make_async_copy(sb, sf_hbm, sems.at[12])

    row = lax.broadcasted_iota(jnp.int32, (CH, CH), 0)
    col = lax.broadcasted_iota(jnp.int32, (CH, CH), 1)
    gm[...] = jnp.where((row * 6554) >> 16 == (col * 6554) >> 16, 1.0, 0.0)

    def norm_silu(field, store, dst, which):
        mean = group_mean(gm[...], acc[0])
        acc[1] = jnp.zeros_like(acc[1])

        def body(p0):
            centered = field[:, pl.ds(p0, TILE)] - mean
            acc[1] += lane_sum(centered * centered)

        tiles(TILE, body)
        inv = lax.rsqrt(group_mean(gm[...], acc[1]) + LN_EPS)
        stat[which] = jnp.broadcast_to(inv, (CH, LANES))

        def body(p0):
            at = pl.ds(p0, TILE)
            y = (field[:, at] - mean) * inv
            store[:, at] = y.astype(BF)
            put(dst, y * jax.nn.sigmoid(y), p0, CH)

        tiles(TILE, body)
        ends(dst, 3 * CH)
        acc[...] = jnp.zeros_like(acc)

    def head(mx, ds, one, two):
        loads = []
        for j in range(half):
            for core, (src_one, src_two) in enumerate(((mine_one, mine_two), (theirs_one, theirs_two))):
                owner = jnp.bitwise_xor(me, 2 * j + core)
                loads.append((
                    pltpu.make_async_copy(src_one.at[j], one.at[owner], wsems.at[0, 2 * j + core]),
                    pltpu.make_async_copy(src_two.at[j], two.at[owner], wsems.at[1, 2 * j + core]),
                ))
        get_base = pltpu.make_async_copy(base, ds.at[0:UNS, :], sems.at[9])
        get_nz = pltpu.make_async_copy(nz, mx.at[CH : CH + NZ, :], sems.at[10])
        get_base.start()
        for pair in loads:
            pair[0].start()
        get_nz.start()
        for pair in loads:
            pair[1].start()
        get_git.start()
        get_gi.start()
        get_base.wait()

        def body(p0):
            put(sa, ds[0:UNS, pl.ds(p0, TILE)], p0, UNS)

        tiles(TILE, body)
        ends(sa, 3 * UNS)
        for pair in loads:
            pair[0].wait()
        wbuf[1, :, 0 : 9 * UNS] = jnp.concatenate([one[d, 0:CH, 0:w_in] for d in range(count)], axis=1)
        out_t = jnp.concatenate([one[d, 0:CH, w_in : w_in + w_out] for d in range(count)], axis=1)
        wou[...] = jnp.concatenate([out_t, wut[:, 0:NZ]], axis=1)
        bias = jnp.concatenate([one[d, CH : CH + 8, 0:w_bias].astype(F32) for d in range(count)], axis=1)
        for k in range(3):
            part = jnp.concatenate([bias[:, k * CH : (k + 1) * CH]] * 16, axis=0)
            bcols[k] = part.T

        def body(p0):
            at = pl.ds(p0, TILE)
            first = conv(wbuf[1, :, 0 : 9 * UNS], sa, p0, TILE, UNS) + bcols[0, :, 0:1]
            hg[:, at] = first
            put(sb, first, p0, CH)

        tiles(TILE, body)
        ends(sb, 3 * CH)
        keep_first.start()

        get_nz.wait()
        fetch[0].start()
        acc[...] = jnp.zeros_like(acc)
        for pair in loads:
            pair[1].wait()
        wbuf[0] = jnp.concatenate([two[d] for d in range(count)], axis=1)
        keep_w = pltpu.make_async_copy(wbuf.at[0], wcf_hbm, sems.at[0])
        keep_w.start()

        def body(p0):
            at = pl.ds(p0, TILE)
            inner = conv(wbuf[0], sb, p0, TILE, CH) + bcols[1, :, 0:1]
            s = jax.nn.sigmoid(inner)
            m = inner * s
            mx[0:CH, at] = m.astype(BF)
            ds[:, at] = (s + m * (1.0 - s)).astype(BF)
            h0 = hg[:, at] + dot(wou[...], mx[:, at]) + bcols[2, :, 0:1]
            hg[:, at] = h0
            acc[0] += lane_sum(h0)

        tiles(TILE, body)
        keep_mx = pltpu.make_async_copy(mx, mx_hbm, sems.at[13])
        keep_ds = pltpu.make_async_copy(ds, ds_hbm, sems.at[14])
        keep_mx.start()
        keep_ds.start()
        keep_w.wait()
        fetch[1].start()
        norm_silu(hg, y1s, sa, 0)
        keep_mx.wait()
        keep_ds.wait()

    held = (pltpu.VMEM((CH + NZ, PIX), BF), pltpu.VMEM((CH, PIX), BF))
    gathered = (pltpu.VMEM((count, CH + 8, wide_one), BF), pltpu.VMEM((count, CH, w_conv), BF))
    pl.run_scoped(head, *held, *gathered)
    fetch[0].wait()

    def body(p0):
        at = pl.ds(p0, TILE)
        c1 = conv(wbuf[1], sa, p0, TILE, CH) + temb[:, 0:1]
        cu[:, at] = c1
        acc[0] += lane_sum(c1)

    tiles(TILE, body)
    fetch[2].start()
    keep_first.wait()
    norm_silu(cu, y2s, sb, 1)

    fetch[1].wait()
    get_git.wait()
    get_gi.wait()
    loss[...] = jnp.zeros_like(loss)
    token = lax.broadcasted_iota(jnp.int32, (1, TXT, 1), 1)
    bias = jnp.where(token < length, 0.0, -1000000000.0)

    def body(p0):
        spots = [al(p0 + k * TILE_D) for k in range(CHAINS)]
        run = range(CHAINS)
        at = [pl.ds(spot, TILE_D) for spot in spots]
        h1 = [hg[:, at[k]] + conv(wbuf[0], sb, spots[k], TILE_D, CH) for k in run]
        normed, inv = zip(*[layer_stats(h1[k]) for k in run])
        s = [dot(kq[...], normed[k].astype(BF)).reshape(HEADS, TXT, TILE_D) + bias for k in run]
        e = [jnp.exp(s[k] - jnp.max(s[k], axis=1, keepdims=True)) for k in run]
        attend = [e[k] * (1.0 / jnp.sum(e[k], axis=1, keepdims=True)) for k in run]
        h2 = [h1[k] + dot(vo[...], attend[k].reshape(KEYS, TILE_D).astype(BF)) for k in run]
        normed2, inv2 = zip(*[layer_stats(h2[k]) for k in run])
        n2 = [normed2[k].astype(BF) for k in run]
        pred = [dot(velt[...], h2[k].astype(BF)) for k in run]
        for n in range(FF // CHUNK):
            f = n * CHUNK
            for k in run:
                val = dot(git[f : f + CHUNK, :], n2[k])
                gate = dot(git[FF + f : FF + f + CHUNK, :], n2[k])
                phi = 0.5 + 0.5 * lax.erf(gate * 0.5**0.5)
                u = gate * phi
                slope = phi + gate * (jnp.exp(-0.5 * gate * gate) * (2.0 * math.pi) ** (-0.5))
                act = (val * u).astype(BF)
                both = dot(gvt[:, f : f + CHUNK], act)
                pred[k] = pred[k] + (both[0:8] + both[8:16])
                col = (n * CHAINS + k) * TILE_D
                cu[:, col : col + TILE_D] = u
                cu[:, PIX // 2 + col : PIX // 2 + col + TILE_D] = val * slope
        diff = [pred[k] - target[:, at[k]] for k in run]
        for k in run:
            loss[...] += lane_sum(diff[k] * diff[k]) * flag
        gp = [(diff[k] * (2.0 * flag)).astype(BF) for k in run]
        gp = [jnp.concatenate([gp[k], gp[k]], axis=0) for k in run]
        pieces = [[] for k in run]
        for n in range(FF // CHUNK):
            for k in run:
                g_act = dot(gvl[n * CHUNK : (n + 1) * CHUNK, :], gp[k])
                col = (n * CHAINS + k) * TILE_D
                pieces[k].insert(n, (g_act * cu[:, col : col + TILE_D]).astype(BF))
                pieces[k].append((g_act * cu[:, PIX // 2 + col : PIX // 2 + col + TILE_D]).astype(BF))
        g3 = [dot(gvl[FF : FF + CH, :], gp[k]) for k in run]
        g_n2 = [dot(gi[...], jnp.concatenate(pieces[k], axis=0)) for k in run]
        g2 = [g3[k] + layer_back(g_n2[k], normed2[k], inv2[k]) for k in run]
        g_att = [dot(vob[...], g2[k].astype(BF)).reshape(HEADS, TXT, TILE_D) for k in run]
        prod = [attend[k] * g_att[k] for k in run]
        g_s = [prod[k] - attend[k] * jnp.sum(prod[k], axis=1, keepdims=True) for k in run]
        g_n = [dot(kqb[...], g_s[k].reshape(KEYS, TILE_D).astype(BF)) for k in run]
        for k in run:
            g1 = g2[k] + layer_back(g_n[k], normed[k], inv[k])
            hg[:, at[k]] = g1
            put(sa, g1, spots[k], CH)

    tiles(SPAN_D, body)
    ends(sa, 3 * CH)

    def conv_back(weight, src, ys):
        def body(p0):
            at = pl.ds(p0, TILE)
            y = ys[:, at].astype(F32)
            u = conv(weight[...], src, p0, TILE, CH) * silu_slope(y)
            cu[:, at] = u
            acc[0] += lane_sum(u)
            acc[1] += lane_sum(u * y)

        acc[...] = jnp.zeros_like(acc)
        tiles(TILE, body)
        return group_mean(gm[...], acc[0]), group_mean(gm[...], acc[1])

    fetch[3].start()
    fetch[2].wait()
    mean, cross = conv_back(wbuf.at[1], sa, y2s)
    inv = stat[1][:, 0:1]

    def body(p0):
        at = pl.ds(p0, TILE)
        put(sb, inv * (cu[:, at] - mean - y2s[:, at].astype(F32) * cross), p0, CH)

    tiles(TILE, body)
    ends(sb, 3 * CH)

    def foot(mx, ds):
        back = [
            pltpu.make_async_copy(mx_hbm, mx, sems.at[13]),
            pltpu.make_async_copy(ds_hbm, ds, sems.at[14]),
        ]
        for copy in back:
            copy.start()
        fetch[3].wait()
        mean, cross = conv_back(wbuf.at[0], sb, y1s)
        inv = stat[0][:, 0:1]
        get_first = pltpu.make_async_copy(sf_hbm, sb, sems.at[12])
        get_first.start()
        for copy in back:
            copy.wait()
        gout[...] = jnp.zeros_like(gout)
        gbias[...] = jnp.zeros_like(gbias)
        wout = wou[:, 0:CH].T

        def body(p0):
            at = pl.ds(p0, TILE)
            g0 = hg[:, at] + inv * (cu[:, at] - mean - y1s[:, at].astype(F32) * cross)
            hg[:, at] = g0
            branch = g0.astype(BF)
            g_inner = (dot(wout, branch) * ds[:, at].astype(F32)).astype(BF)
            sa[0:CH, at] = g_inner
            gout[...] += dot_nt(branch, mx[0:CH, at])
            gbias[0] += lane_sum(g_inner.astype(F32))
            gbias[1] += lane_sum(branch.astype(F32))

        tiles(TILE, body)
        get_first.wait()

    pl.run_scoped(foot, *held)
    send_h = pltpu.make_async_copy(hg, gh_hbm, sems.at[7])
    send_g = pltpu.make_async_copy(sa.at[0:CH, 0:PIX], ginner_hbm, sems.at[8])
    send_h.start()
    send_g.start()

    def last(grads):
        for b in range(3):
            grad = dot_nt(sa[0:CH, 0:PIX], sb[:, b * LANES : b * LANES + PIX])
            for a in range(3):
                scatter(grads, grad[:, a * CH : (a + 1) * CH], (3 * a + b) * CH, w_conv, 0, me, count)
        keep = pltpu.make_async_copy(grads.at[0:half], keep_hbm, sems.at[9])
        send = pltpu.make_async_copy(grads.at[half:count], send_hbm, sems.at[10])
        keep.start()
        send.start()
        keep.wait()
        send.wait()

    pl.run_scoped(last, gathered[1])
    send_h.wait()
    send_g.wait()


def main_call(ints, outs, pieces, wf, gi):
    base, nz, target, kq, kqb, vo, vob, gvt, gvl, velt, temb, wut, git, wb = outs
    half, _, w_conv = pieces[2].shape
    vm = pl.BlockSpec(memory_space=pltpu.VMEM)
    sm = pl.BlockSpec(memory_space=pltpu.SMEM)
    hb = pl.BlockSpec(memory_space=pl.ANY)
    shapes = [
        ((8, LANES), F32), ((CH, CH), F32), ((2, CH, LANES), F32),
        ((half, CH, w_conv), BF), ((half, CH, w_conv), BF),
        ((CH, PIX), BF), ((CH, PIX), F32), ((CH, 9 * CH), BF),
        ((3 * CH, WIDE), BF), ((CH + NZ, PIX), BF), ((CH, PIX), BF),
    ]
    return pl.pallas_call(
        main_kernel,
        out_shape=[jax.ShapeDtypeStruct(*s) for s in shapes],
        in_specs=[sm] + [vm] * 10 + [hb] * 10,
        out_specs=[vm] * 3 + [hb] * 8,
        scratch_shapes=[
            pltpu.VMEM((3 * CH, WIDE), BF),
            pltpu.VMEM((3 * CH, WIDE), BF),
            pltpu.VMEM((CH, PIX), F32),
            pltpu.VMEM((CH, PIX), F32),
            pltpu.VMEM((CH, PIX), BF),
            pltpu.VMEM((CH, PIX), BF),
            pltpu.VMEM((2, CH, 9 * CH), BF),
            pltpu.VMEM((2 * FF, CH), BF),
            pltpu.VMEM((CH, 2 * FF), BF),
            pltpu.VMEM((2, CH, LANES), F32),
            pltpu.VMEM((2, CH, LANES), F32),
            pltpu.VMEM((CH, CH), F32),
            pltpu.VMEM((3, CH, LANES), F32),
            pltpu.VMEM((CH, CH + NZ), BF),
            pltpu.SemaphoreType.DMA((15,)),
            pltpu.SemaphoreType.DMA((2, 2 * half)),
        ],
        compiler_params=pltpu.CompilerParams(vmem_limit_bytes=VMEM_LIMIT),
        cost_estimate=pl.CostEstimate(flops=80_000_000_000, bytes_accessed=60_000_000, transcendentals=0),
        name="main",
    )(ints, target, kq, kqb, vo, vob, gvt, gvl, velt, temb, wut, *pieces, base, nz, wf, wb, git, gi)


def tail_kernel(
    ints, ginner, base, wcf, gout, gbias, gh_hbm, keep_hbm, send_hbm,
    sa, sb, gh, gf, nat, wcb, grads, acc, sems,
):
    me = ints[2]
    half = keep_hbm.shape[0]
    count = 2 * half
    w_in = 9 * UNS // count
    w_out = CH // count
    w_bias = 3 * CH // count
    fetch = pltpu.make_async_copy(gh_hbm, gh, sems.at[0])
    fetch.start()
    wcb[...] = backward_weight(wcf[...], nat)

    def body(p0):
        at = pl.ds(p0, TILE)
        put(sa, ginner[:, at], p0, CH)
        put(sb, base[:, at], p0, UNS)

    tiles(TILE, body)
    ends(sa, 3 * CH)
    ends(sb, 3 * UNS)
    acc[...] = jnp.zeros_like(acc)
    fetch.wait()

    def body(p0):
        at = pl.ds(p0, TILE)
        g_first = (gh[:, at] + conv(wcb[...], sa, p0, TILE, CH)).astype(BF)
        gf[:, at] = g_first
        acc[...] += lane_sum(g_first.astype(F32))

    tiles(TILE, body)
    for b in range(3):
        grad = dot_nt(gf[...], sb[:, b * LANES : b * LANES + PIX])
        for a in range(3):
            scatter(grads, grad[:, a * UNS : (a + 1) * UNS], (3 * a + b) * UNS, w_in, 0, me, count)
    scatter(grads, gout[...], 0, w_out, w_in, me, count)
    rows = [jnp.sum(part.T, axis=0, keepdims=True) for part in (acc[...], gbias[0], gbias[1])]
    bias = jnp.concatenate(rows, axis=1)
    first_row = lax.broadcasted_iota(jnp.int32, (8, w_in + w_out), 0) == 0
    for owner in range(count):
        part = bias[:, owner * w_bias : (owner + 1) * w_bias]
        part = jnp.concatenate([part, jnp.zeros((1, w_in + w_out - w_bias), F32)], axis=1)
        grads[slot(owner, me, count), CH : CH + 8, :] = jnp.where(first_row, part, 0.0).astype(BF)
    keep = pltpu.make_async_copy(grads.at[0:half], keep_hbm, sems.at[1])
    send = pltpu.make_async_copy(grads.at[half:count], send_hbm, sems.at[2])
    keep.start()
    send.start()
    keep.wait()
    send.wait()


def tail_call(ints, ginner, base, wcf, gout, gbias, gh, half):
    vm = pl.BlockSpec(memory_space=pltpu.VMEM)
    sm = pl.BlockSpec(memory_space=pltpu.SMEM)
    hb = pl.BlockSpec(memory_space=pl.ANY)
    wide = (9 * UNS + CH) // (2 * half)
    return pl.pallas_call(
        tail_kernel,
        out_shape=[jax.ShapeDtypeStruct((half, CH + 8, wide), BF)] * 2,
        in_specs=[sm] + [vm] * 5 + [hb],
        out_specs=[hb, hb],
        scratch_shapes=[
            pltpu.VMEM((3 * CH, WIDE), BF),
            pltpu.VMEM((3 * UNS, WIDE), BF),
            pltpu.VMEM((CH, PIX), F32),
            pltpu.VMEM((CH, PIX), BF),
            pltpu.VMEM((9 * CH, CH), BF),
            pltpu.VMEM((CH, 9 * CH), BF),
            pltpu.VMEM((2 * half, CH + 8, wide), BF),
            pltpu.VMEM((CH, LANES), F32),
            pltpu.SemaphoreType.DMA((3,)),
        ],
        compiler_params=pltpu.CompilerParams(vmem_limit_bytes=VMEM_LIMIT),
        cost_estimate=pl.CostEstimate(flops=14_000_000_000, bytes_accessed=16_000_000, transcendentals=0),
        name="tail",
    )(ints, ginner, base, wcf, gout, gbias, gh)


def update(master, first, second, grad):
    new_first = BETA_ONE * first + (1.0 - BETA_ONE) * grad
    new_second = BETA_TWO * second + (1.0 - BETA_TWO) * grad * grad
    first_hat = new_first / (1.0 - BETA_ONE**STEP)
    second_hat = new_second / (1.0 - BETA_TWO**STEP)
    new_master = master - LEARN_RATE * (
        first_hat / (jnp.sqrt(second_hat) + ADAM_EPS) + WEIGHT_DECAY * master
    )
    return new_first, new_second, new_master


def adam_kernel(factor, g_one, g_two, *refs):
    ins, outs = refs[:12], refs[12:]
    w_in, w_out, w_bias = ins[0].shape[1], ins[2].shape[0], ins[3].shape[1]
    scale = factor[0]
    one = g_one[...].astype(F32) * scale
    tail = one[0:CH, one.shape[1] // LANES * LANES - LANES if one.shape[1] >= LANES else 0 :]
    offset = w_in - (one.shape[1] - tail.shape[1])
    grads = (
        one[0:CH, 0:w_in],
        g_two[...].astype(F32) * scale,
        tail.T[offset : offset + w_out, :],
        one[CH : CH + 1, 0:w_bias],
    )
    for k in range(4):
        values = update(ins[k][...], ins[4 + k][...], ins[8 + k][...], grads[k])
        for n in range(3):
            outs[4 * n + k][...] = values[n]


def adam_call(factor, g_one, g_two, states):
    vm = pl.BlockSpec(memory_space=pltpu.VMEM)
    sm = pl.BlockSpec(memory_space=pltpu.SMEM)
    return pl.pallas_call(
        adam_kernel,
        out_shape=[jax.ShapeDtypeStruct(s.shape, F32) for s in states],
        in_specs=[sm] + [vm] * 14,
        out_specs=[vm] * 12,
        compiler_params=pltpu.CompilerParams(vmem_limit_bytes=32 * 2**20),
        cost_estimate=pl.CostEstimate(flops=10_000_000, bytes_accessed=6_000_000, transcendentals=0),
        name="adamw",
    )(factor, g_one, g_two, *states)


def swap(value, axis, bit):
    return lax.ppermute(value, axis, [(i, i ^ bit) for i in range(lax.axis_size(axis))])


def from_chips(piece):
    return [swap(piece, "shard", 2 * j) for j in range(1, lax.axis_size("shard") // 2)]


def add_low(*parts):
    total = parts[0].astype(F32)
    for part in parts[1:]:
        total = total + part.astype(F32)
    return total.astype(BF)


def reduce_cores(keep, send):
    return add_low(keep, swap(send, "shard", 1))


def between_chips(part):
    return [part[0]] + [swap(part[j], "shard", 2 * j) for j in range(1, part.shape[0])]


def reduce_replicas(part):
    bit = 1
    while bit < lax.axis_size("dp"):
        part = add_low(part, swap(part, "dp", bit))
        bit *= 2
    return part


def sum_over(value, axes):
    for axis in axes:
        bit = 1
        while bit < lax.axis_size(axis):
            value = value + swap(value, axis, bit)
            bit *= 2
    return value


def early(item, frozen):
    cond, clean, noise, tstep, text = item
    unet_conv, res_conv, time_mlp, time_proj, wq, kvproj, wo, geglu_in, geglu_out, vel = frozen
    half = CH // 2
    freqs = jnp.exp(-math.log(10000.0) * jnp.arange(half, dtype=jnp.int32).astype(F32) / half)
    angles = tstep[0].astype(F32) * freqs
    emb = jnp.concatenate([jnp.cos(angles), jnp.sin(angles)])[None, :].astype(BF)
    lat = jnp.stack([clean, noise]).reshape(2, 4, SIDE, 2, SIDE // 2).transpose(0, 1, 4, 3, 2).reshape(2, 4, PIX)
    wf = res_conv.transpose(0, 2, 1)
    outs = prologue(
        tstep, jnp.asarray(schedule()), cond, lat, text, kvproj, wq, wo, geglu_in, geglu_out.T, vel.T,
        jnp.broadcast_to(emb, (16, CH)), time_mlp, time_proj.T, unet_conv, wf,
    )
    return outs, wf, geglu_in


def pieces_of(masters):
    w_in, w_conv, w_out, bias = [entry.astype(BF) for entry in masters]
    one = jnp.concatenate([w_in.T, w_out.T], axis=1)
    row = jnp.pad(bias[None, :], ((0, 7), (0, one.shape[1] - bias.shape[0])))
    return jnp.concatenate([one, row], axis=0), w_conv.T


def per_device(*args):
    conditions, clean, noise, tsteps, text, lengths, valid = args[:7]
    frozen = args[7:17]
    masters, firsts, seconds = args[17:21], args[21:25], args[25:29]
    one, two = pieces_of(masters)
    ones = [one] + from_chips(one)
    twos = [two] + from_chips(two)
    me = lax.axis_index("shard").astype(jnp.int32)
    ints = jnp.stack([lengths[0], valid[0], me])
    outs, wf, gi = early((conditions[0], clean[0], noise[0], tsteps, text[0]), frozen)
    ones, twos, outs = lax.optimization_barrier((ones, twos, outs))
    mine_one, mine_two = jnp.stack(ones), jnp.stack(twos)
    theirs_one, theirs_two = swap(mine_one, "shard", 1), swap(mine_two, "shard", 1)
    loss, gout, gbias, keep_two, send_two, ginner, gh, wcf, *_ = main_call(
        ints, outs, (mine_one, theirs_one, mine_two, theirs_two), wf, gi
    )
    two, ginner = lax.optimization_barrier((reduce_cores(keep_two, send_two), ginner))
    twos = between_chips(two)
    keep_one, send_one = tail_call(ints, ginner, outs[0], wcf, gout, gbias, gh, mine_one.shape[0])
    twos, keep_one, send_one = lax.optimization_barrier((twos, keep_one, send_one))
    two = reduce_replicas(add_low(*twos))
    one = reduce_replicas(add_low(*between_chips(reduce_cores(keep_one, send_one))))
    pixels, channels = clean.shape[-1], clean.shape[1]
    local_count = jnp.sum(valid).astype(F32) * (pixels * channels)
    lane = lax.broadcasted_iota(jnp.int32, (8, LANES), 1)
    sums = sum_over(jnp.where(lane == 0, jnp.sum(loss), jnp.where(lane == 1, local_count, 0.0)), ("shard", "dp"))
    loss_sum = sums[0, 0]
    count = jnp.maximum(sums[0, 1], 1.0)
    squares = jnp.sum(jnp.square(one.astype(F32))) + jnp.sum(jnp.square(two.astype(F32)))
    squares = sum_over(jnp.full((8, LANES), squares), ("shard",))[0, 0]
    grad_norm = jnp.sqrt(squares) / count
    factor = jnp.minimum(1.0, CLIP_MAX / (grad_norm + 1e-06)) / count
    states = []
    for group in (masters, firsts, seconds):
        states += [group[0].T, group[1].T, group[2], group[3][None, :]]
    new = adam_call(factor.reshape(1), one, two, states)
    results = []
    for n in range(3):
        results += [new[4 * n].T, new[4 * n + 1].T, new[4 * n + 2], new[4 * n + 3][0]]
    return (loss_sum, count, grad_norm, *results)


def solution(mesh):
    both = ("dp", "shard")
    placed = (
        (P(both, None, None, None), P(both, None, None), P(both, None, None), P(both), P(both, None, None), P(both), P(both))
        + (P(),) * 10
        + (P("shard", None), P("shard", None), P("shard", None), P("shard")) * 3
    )
    return jax.shard_map(
        per_device,
        mesh=mesh,
        in_specs=placed,
        out_specs=(P(), P(), P()) + (P("shard", None), P("shard", None), P("shard", None), P("shard")) * 3,
        check_vma=False,
    )
```

```python
import math

import jax
import jax.numpy as jnp
import numpy as np
from jax import lax
from jax.experimental import pallas as pl
from jax.experimental.pallas import tpu as pltpu
from jax.sharding import PartitionSpec as P

HEADS = 8
GROUPS = 32
STEP = 10

LN_EPS = 1e-05
CLIP_MAX = 0.01
LEARN_RATE = 0.02
BETA_ONE = 0.9
BETA_TWO = 0.999
ADAM_EPS = 1e-08
WEIGHT_DECAY = 0.01

BF = jnp.bfloat16
F32 = jnp.float32

SIDE = 64
PIX = SIDE * SIDE
LANES = 128
HALO = LANES
WIDE = PIX + 2 * HALO
CH = 320
UNS = 192
FF = 1280
TXT = 80
KEYS = HEADS * TXT
NZ = 48
NT = (((1,), (1,)), ((), ()))
TN = (((0,), (0,)), ((), ()))
VMEM_LIMIT = 62 * 2**20

TILE = 512
TILE_C = 512
TILE_D = 512
CHUNK = 320


def schedule():
    start = 0.00085**0.5
    final = 0.012**0.5
    betas = (start + np.arange(1000, dtype=np.float64) * ((final - start) / 999.0)) ** 2
    table = np.zeros(1024, np.float32)
    table[:1000] = np.cumprod(1.0 - betas)
    return table.reshape(8, LANES)


def dot(a, b):
    return jnp.dot(a, b, preferred_element_type=F32)


def dot_nt(a, b):
    return lax.dot_general(a, b, NT, preferred_element_type=F32)


def al(x):
    return x if isinstance(x, int) else pl.multiple_of(x, LANES)


def tiles(width, body, go):
    @pl.when(go)
    def _():
        for p0 in range(0, PIX, width):
            body(p0)


def stream(width, make, ends, use, go):
    @pl.when(go)
    def _():
        make(0)
        make(PIX - width)
        ends()
        for p0 in range(0, PIX, width):
            if p0 + 2 * width < PIX:
                make(p0 + width)
            use(p0)


def put(dst, value, p0, chans):
    width = value.shape[1]
    low = value.astype(BF)
    for q in range(width // LANES):
        mid = low[:, q * LANES : (q + 1) * LANES]
        lane = lax.broadcasted_iota(jnp.int32, mid.shape, 1) & (SIDE - 1)
        up = jnp.where(lane == 0, jnp.zeros((), BF), pltpu.roll(mid, 1, 1))
        down = jnp.where(lane == SIDE - 1, jnp.zeros((), BF), pltpu.roll(mid, LANES - 1, 1))
        at = pl.ds(al(p0 + HALO + q * LANES), LANES)
        dst[0:chans, at] = up
        dst[chans : 2 * chans, at] = mid
        dst[2 * chans : 3 * chans, at] = down


def ends(dst, rows):
    last = dst[0:rows, PIX : PIX + LANES]
    head = dst[0:rows, HALO : HALO + LANES]
    lane = lax.broadcasted_iota(jnp.int32, last.shape, 1)
    zero = jnp.zeros((), BF)
    dst[0:rows, 0:LANES] = jnp.where(lane >= SIDE, pltpu.roll(last, SIDE, 1), zero)
    dst[0:rows, PIX + HALO : PIX + HALO + LANES] = jnp.where(lane < SIDE, pltpu.roll(head, SIDE, 1), zero)


def conv(weight, src, p0, width, chans):
    parts = []
    for a in range(3):
        for b in range(3):
            parts.append(src[a * chans : (a + 1) * chans, pl.ds(al(p0 + b * LANES), width)])
    return dot(weight, jnp.concatenate(parts, axis=0))


def backward_weight(weight, natural):
    natural[...] = weight.T
    blocks = [natural[(8 - t) * CH : (9 - t) * CH, :] for t in range(9)]
    return jnp.concatenate(blocks, axis=1)


def lane_sum(value):
    total = value[:, 0:LANES]
    for q in range(1, value.shape[1] // LANES):
        total = total + value[:, q * LANES : (q + 1) * LANES]
    return total


def group_mean(gm, sums):
    spread = jnp.dot(gm, sums, precision=lax.Precision.HIGHEST, preferred_element_type=F32)
    return jnp.sum(spread, axis=1, keepdims=True) * (1.0 / (PIX * (CH // GROUPS)))


def silu_slope(y):
    s = jax.nn.sigmoid(y)
    return s * (1.0 + y * (1.0 - s))


def layer_stats(field):
    mean = jnp.mean(field, axis=0, keepdims=True)
    centered = field - mean
    inv = lax.rsqrt(jnp.mean(centered * centered, axis=0, keepdims=True) + LN_EPS)
    return centered * inv, inv


def layer_back(grad, normed, inv):
    return inv * (
        grad
        - jnp.mean(grad, axis=0, keepdims=True)
        - normed * jnp.mean(grad * normed, axis=0, keepdims=True)
    )


def split(value):
    high = value.astype(BF)
    rest = value - high.astype(F32)
    mid = rest.astype(BF)
    return high, mid, (rest - mid.astype(F32)).astype(BF)


def slot(owner, me, count):
    rel = jnp.bitwise_xor(owner, me)
    return (rel & 1) * (count // 2) + lax.shift_right_logical(rel, 1)


def scatter(dst, value, start, width, lane0, me, count):
    stop = start + value.shape[1]
    for owner in range(count):
        lo, hi = max(start, owner * width), min(stop, (owner + 1) * width)
        if lo < hi:
            at = lane0 + lo - owner * width
            dst[slot(owner, me, count), 0:CH, at : at + hi - lo] = value[:, lo - start : hi - start].astype(BF)


def prologue_kernel(
    steps, table, cond, lat, text, kvproj, wq, wo, gi, got, velt_in, emb, tmlp, tprojt, unet, res,
    base, nz, target, kq, kqb, vo, vob, gvt, gvl, velt, temb, wut, git, wb,
    zs, us, kvs, nat, wsrc, sems,
):
    fetch = [pltpu.make_async_copy(res.at[k], wsrc.at[k], sems.at[k]) for k in range(2)]
    for copy in fetch:
        copy.start()
    index = lax.broadcasted_iota(jnp.int32, (8, LANES), 0) * LANES + lax.broadcasted_iota(jnp.int32, (8, LANES), 1)
    picked = jnp.where(index == steps[0], table[...], 0.0)
    abar = jnp.sum(jnp.sum(picked, axis=1, keepdims=True), axis=0, keepdims=True)
    alpha = jnp.sqrt(abar)
    sigma = jnp.sqrt(1.0 - abar)
    row = lax.broadcasted_iota(jnp.int32, (512, 512), 0)
    col = lax.broadcasted_iota(jnp.int32, (512, 512), 1)
    same = jnp.logical_and((row & 7) == (col >> 6), (row >> 3) == (col & 63))
    perm = jnp.where(same, 1.0, 0.0).astype(BF)
    lane = lax.broadcasted_iota(jnp.int32, (32, 8, LANES), 2)
    for c in range(3):
        zs[...] = lax.dot_general(cond[c], perm, TN, preferred_element_type=F32).reshape(64, 8, 512)
        for k in range(4):
            one = zs[0:32, :, k * LANES : (k + 1) * LANES]
            two = zs[32:64, :, k * LANES : (k + 1) * LANES]
            even = jnp.where(lane < SIDE, one, pltpu.roll(two, SIDE, 2))
            odd = jnp.where(lane < SIDE, pltpu.roll(one, SIDE, 2), two)
            for m in range(32):
                us[16 * k : 16 * k + 8, m * LANES : (m + 1) * LANES] = even[m]
                us[16 * k + 8 : 16 * k + 16, m * LANES : (m + 1) * LANES] = odd[m]
        base[64 * c : 64 * (c + 1), :] = us[...].astype(BF)
    clean = lat[0]
    noise = lat[1]
    noisy = (alpha * clean + sigma * noise).astype(BF).astype(F32)
    target[4:8, :] = jnp.zeros((4, PIX), F32)
    target[0:4, :] = alpha * noise - sigma * clean
    lane = lax.broadcasted_iota(jnp.int32, (4, LANES), 1)
    inside = lane & (SIDE - 1)
    cols = [noisy[:, m * LANES : (m + 1) * LANES] for m in range(32)]
    left = jnp.where(lane >= SIDE, pltpu.roll(cols[31], SIDE, 1), 0.0)
    right = jnp.where(lane < SIDE, pltpu.roll(cols[0], SIDE, 1), 0.0)
    cols = [left] + cols + [right]
    us[0:NZ, :] = jnp.zeros((NZ, PIX), F32)
    for m in range(34):
        up = jnp.where(inside == 0, 0.0, pltpu.roll(cols[m], 1, 1))
        down = jnp.where(inside == SIDE - 1, 0.0, pltpu.roll(cols[m], LANES - 1, 1))
        for a, part in enumerate((up, cols[m], down)):
            for b in range(3):
                at = m - b
                if 0 <= at < 32:
                    r = (3 * a + b) * 4
                    us[r : r + 4, at * LANES : (at + 1) * LANES] = part
    nz[...] = us[0:NZ, :].astype(BF)
    us[0:LANES // 2, 0:CH] = jnp.zeros((LANES // 2, CH), F32)
    us[0:36, 0:CH] = unet[...].astype(F32)
    wide = jnp.concatenate([us[0:64, 0:CH], jnp.zeros((64, CH), F32)], axis=0)
    wut[...] = wide.T.astype(BF)
    kvs[...] = jnp.zeros_like(kvs)
    kvs[0 : text.shape[0], :] = dot(text[...], kvproj[...])
    keys = kvs[:, 0:CH].astype(BF)
    values = kvs[:, CH : 2 * CH].astype(BF)
    head_dim = CH // HEADS
    head = lax.broadcasted_iota(jnp.int32, (TXT, CH), 1)
    own = [jnp.logical_and(head >= h * head_dim, head < (h + 1) * head_dim) for h in range(HEADS)]
    zero = jnp.zeros((), BF)
    kbd = jnp.concatenate([jnp.where(own[h], keys, zero) for h in range(HEADS)], axis=0)
    vbd = jnp.concatenate([jnp.where(own[h], values, zero) for h in range(HEADS)], axis=0)
    scale = head_dim ** (-0.5)
    fold = dot_nt(kbd, wq[...]) * scale
    kq[...] = fold.astype(BF)
    kqb[...] = fold.T.astype(BF)
    fold = dot(vbd, wo[...])
    vob[...] = fold.astype(BF)
    vo[...] = fold.T.astype(BF)
    us[0:8, 0:CH] = jnp.zeros((8, CH), F32)
    us[0:4, 0:CH] = velt_in[...].astype(F32)
    velf = us[0:8, 0:CH]
    velt[...] = velf.astype(BF)
    fold = dot(velf.astype(BF), got[...])
    high = fold.astype(BF).astype(F32)
    both = jnp.concatenate([high, fold - high], axis=0)
    gvt[...] = both.astype(BF)
    wide = jnp.concatenate([both, jnp.zeros((LANES - 16, FF), F32)], axis=0)
    gvl[0:FF, :] = wide.T[:, 0:16].astype(BF)
    wide = jnp.concatenate([velf, jnp.zeros((LANES - 8, CH), F32)], axis=0)
    gvl[FF : FF + CH, :] = wide.T[:, 0:16].astype(BF)
    git[...] = gi[...].T
    hidden = jax.nn.silu(dot(emb[...], tmlp[...])).astype(BF)
    temb[...] = dot_nt(tprojt[...], jnp.concatenate([hidden] * 8, axis=0))
    for k in range(2):
        fetch[k].wait()
        wb[k] = backward_weight(wsrc[k], nat)


def prologue(*args):
    vm = pl.BlockSpec(memory_space=pltpu.VMEM)
    sm = pl.BlockSpec(memory_space=pltpu.SMEM)
    hb = pl.BlockSpec(memory_space=pl.ANY)
    shapes = [
        ((UNS, PIX), BF), ((NZ, PIX), BF), ((8, PIX), F32),
        ((KEYS, CH), BF), ((CH, KEYS), BF), ((CH, KEYS), BF), ((KEYS, CH), BF),
        ((16, FF), BF), ((FF + CH, 16), BF), ((8, CH), BF), ((CH, LANES), F32), ((CH, LANES), BF),
        ((2 * FF, CH), BF), ((2, CH, 9 * CH), BF),
    ]
    return pl.pallas_call(
        prologue_kernel,
        out_shape=[jax.ShapeDtypeStruct(*s) for s in shapes],
        in_specs=[sm] + [vm] * 14 + [hb],
        out_specs=[vm] * len(shapes),
        scratch_shapes=[
            pltpu.VMEM((64, 8, 512), F32),
            pltpu.VMEM((64, PIX), F32),
            pltpu.VMEM((TXT, 2 * CH), F32),
            pltpu.VMEM((9 * CH, CH), BF),
            pltpu.VMEM((2, CH, 9 * CH), BF),
            pltpu.SemaphoreType.DMA((2,)),
        ],
        compiler_params=pltpu.CompilerParams(vmem_limit_bytes=VMEM_LIMIT),
        cost_estimate=pl.CostEstimate(flops=12_000_000_000, bytes_accessed=20_000_000, transcendentals=0),
        name="prologue",
    )(*args)


def main_kernel(
    ints, target, kq, kqb, vo, vob, gvt, gvl, velt, temb, wut, base, nz, wf, wb, git_hbm, gi_hbm, *rest,
):
    count = len(rest) - 27
    pieces = rest[:count]
    (
    gout, gbias, keep_hbm, send_hbm, ginner_hbm, gh_hbm, wcf_hbm, sf_hbm, mx_hbm, ds_hbm, y1_hbm,
    sa, sb, hg, cu, y2s, wbuf, git, gi, acc, stat, gm, bcols, wou, loss, sems, wsems,
    ) = rest[count:]
    length = ints[0]
    flag = ints[1].astype(F32)
    me = ints[2]
    go = me >= 0
    half = count // 2
    w_conv = 9 * CH // count
    w_in = 9 * UNS // count
    w_out = CH // count
    w_bias = 3 * CH // count
    fetch = [
        pltpu.make_async_copy(wf.at[0], wbuf.at[1], sems.at[1]),
        pltpu.make_async_copy(wf.at[1], wbuf.at[0], sems.at[2]),
        pltpu.make_async_copy(wb.at[1], wbuf.at[1], sems.at[3]),
        pltpu.make_async_copy(wb.at[0], wbuf.at[0], sems.at[4]),
    ]
    get_git = pltpu.make_async_copy(git_hbm, git, sems.at[5])
    get_gi = pltpu.make_async_copy(gi_hbm, gi, sems.at[6])
    keep_first = pltpu.make_async_copy(sb, sf_hbm, sems.at[12])

    row = lax.broadcasted_iota(jnp.int32, (CH, CH), 0)
    col = lax.broadcasted_iota(jnp.int32, (CH, CH), 1)
    gm[...] = jnp.where((row * 6554) >> 16 == (col * 6554) >> 16, 1.0, 0.0)

    def norm_silu(field, store, dst, which):
        mean = group_mean(gm[...], acc[0])
        acc[1] = jnp.zeros_like(acc[1])

        def body(p0):
            centered = field[:, pl.ds(p0, TILE)] - mean
            acc[1] += lane_sum(centered * centered)

        tiles(TILE, body, go)
        inv = lax.rsqrt(group_mean(gm[...], acc[1]) + LN_EPS)
        stat[which] = jnp.broadcast_to(inv, (CH, LANES))
        acc[...] = jnp.zeros_like(acc)

        def make(p0):
            at = pl.ds(p0, TILE)
            y = (field[:, at] - mean) * inv
            store[:, at] = y.astype(BF)
            put(dst, y * jax.nn.sigmoid(y), p0, CH)

        return make

    def head(mx, ds, y1s, got):
        loads = [
            pltpu.make_async_copy(pieces[rel], got.at[jnp.bitwise_xor(me, rel)], wsems.at[rel]) for rel in range(count)
        ]
        get_base = pltpu.make_async_copy(base, ds.at[0:UNS, :], sems.at[9])
        get_nz = pltpu.make_async_copy(nz, mx.at[CH : CH + NZ, :], sems.at[10])
        get_base.start()
        for copy in loads:
            copy.start()
        get_nz.start()
        get_git.start()
        get_gi.start()
        get_base.wait()

        def make_base(p0):
            put(sa, ds[0:UNS, pl.ds(p0, TILE)], p0, UNS)

        for copy in loads:
            copy.wait()
        wbuf[1, :, 0 : 9 * UNS] = jnp.concatenate([got[d, 0:CH, 0:w_in] for d in range(count)], axis=1)
        out_t = jnp.concatenate([got[d, 0:CH, w_in : w_in + w_out] for d in range(count)], axis=1)
        wou[...] = jnp.concatenate([out_t, wut[:, 0:NZ]], axis=1)
        bias = jnp.concatenate([got[d, CH : CH + 8, 0:w_bias].astype(F32) for d in range(count)], axis=1)
        for k in range(3):
            part = jnp.concatenate([bias[:, k * CH : (k + 1) * CH]] * 16, axis=0)
            bcols[k] = part.T

        def body(p0):
            at = pl.ds(p0, TILE)
            first = conv(wbuf[1, :, 0 : 9 * UNS], sa, p0, TILE, UNS) + bcols[0, :, 0:1]
            hg[:, at] = first
            put(sb, first, p0, CH)

        stream(TILE, make_base, lambda: ends(sa, 3 * UNS), body, go)
        ends(sb, 3 * CH)
        keep_first.start()

        get_nz.wait()
        fetch[0].start()
        acc[...] = jnp.zeros_like(acc)
        skip = w_in + w_out
        wbuf[0] = jnp.concatenate([got[d, 0:CH, skip : skip + w_conv] for d in range(count)], axis=1)
        keep_w = pltpu.make_async_copy(wbuf.at[0], wcf_hbm, sems.at[0])
        keep_w.start()

        def body(p0):
            at = pl.ds(p0, TILE)
            inner = conv(wbuf[0], sb, p0, TILE, CH) + bcols[1, :, 0:1]
            s = jax.nn.sigmoid(inner)
            m = inner * s
            mx[0:CH, at] = m.astype(BF)
            ds[:, at] = (s + m * (1.0 - s)).astype(BF)
            h0 = hg[:, at] + dot(wou[...], mx[:, at]) + bcols[2, :, 0:1]
            hg[:, at] = h0
            acc[0] += lane_sum(h0)

        tiles(TILE, body, go)
        keep_mx = pltpu.make_async_copy(mx, mx_hbm, sems.at[13])
        keep_ds = pltpu.make_async_copy(ds, ds_hbm, sems.at[14])
        keep_mx.start()
        keep_ds.start()
        keep_w.wait()
        fetch[1].start()
        make = norm_silu(hg, y1s, sa, 0)
        fetch[0].wait()

        def body(p0):
            at = pl.ds(p0, TILE_C)
            c1 = conv(wbuf[1], sa, p0, TILE_C, CH) + temb[:, 0:1]
            cu[:, at] = c1
            acc[0] += lane_sum(c1)

        stream(TILE, make, lambda: ends(sa, 3 * CH), body, go)
        keep_y1 = pltpu.make_async_copy(y1s, y1_hbm, sems.at[11])
        keep_y1.start()
        keep_mx.wait()
        keep_ds.wait()
        keep_y1.wait()

    held = (pltpu.VMEM((CH + NZ, PIX), BF), pltpu.VMEM((CH, PIX), BF), pltpu.VMEM((CH, PIX), BF))
    pl.run_scoped(head, *held, pltpu.VMEM((count,) + pieces[0].shape, BF))
    fetch[2].start()
    keep_first.wait()
    make = norm_silu(cu, y2s, sb, 1)
    tiles(TILE, make, go)
    ends(sb, 3 * CH)

    fetch[1].wait()
    get_git.wait()
    get_gi.wait()
    loss[...] = jnp.zeros_like(loss)
    token = lax.broadcasted_iota(jnp.int32, (1, TXT, 1), 1)
    bias = jnp.where(token < length, 0.0, -1000000000.0)

    def front(p0, keep):
        uw, attend_k, normed_k, normed2_k, inv_k, gp_k = keep
        at = pl.ds(p0, TILE_D)
        h1 = hg[:, at] + conv(wbuf[0], sb, p0, TILE_D, CH)
        yield
        normed, inv = layer_stats(h1)
        low = normed.astype(BF)
        normed_k[...] = low
        inv_k[0:1] = inv
        s = dot(kq[...], low).reshape(HEADS, TXT, TILE_D) + bias
        yield
        e = jnp.exp(s - jnp.max(s, axis=1, keepdims=True))
        attend = (e * (1.0 / jnp.sum(e, axis=1, keepdims=True))).reshape(KEYS, TILE_D).astype(BF)
        attend_k[...] = attend
        yield
        h2 = h1 + dot(vo[...], attend)
        normed2, inv2 = layer_stats(h2)
        n2 = normed2.astype(BF)
        normed2_k[...] = n2
        inv_k[1:2] = inv2
        yield
        acts = []
        for n in range(FF // CHUNK):
            f = n * CHUNK
            val = dot(git[f : f + CHUNK, :], n2)
            gate = dot(git[FF + f : FF + f + CHUNK, :], n2)
            phi = 0.5 + 0.5 * lax.erf(gate * 0.5**0.5)
            u = gate * phi
            slope = phi + gate * (jnp.exp(-0.5 * gate * gate) * (2.0 * math.pi) ** (-0.5))
            acts.append((val * u).astype(BF))
            col = n * TILE_D
            uw[:, col : col + TILE_D] = u
            uw[:, PIX // 2 + col : PIX // 2 + col + TILE_D] = val * slope
            yield
        both = dot(gvt[...], jnp.concatenate(acts, axis=0))
        diff = both[0:8] + both[8:16] + dot(velt[...], h2.astype(BF)) - target[:, at]
        loss[...] += lane_sum(diff * diff) * flag
        gp = (diff * (2.0 * flag)).astype(BF)
        gp_k[...] = jnp.concatenate([gp, gp], axis=0)
        yield

    def back(p0, keep):
        uw, attend_k, normed_k, normed2_k, inv_k, gp_k = keep
        at = pl.ds(p0, TILE_D)
        gp = gp_k[...]
        pieces = []
        for n in range(FF // CHUNK):
            g_act = dot(gvl[n * CHUNK : (n + 1) * CHUNK, :], gp)
            col = n * TILE_D
            pieces.insert(n, (g_act * uw[:, col : col + TILE_D]).astype(BF))
            pieces.append((g_act * uw[:, PIX // 2 + col : PIX // 2 + col + TILE_D]).astype(BF))
        yield
        g_n2 = dot(gi[...], jnp.concatenate(pieces, axis=0))
        yield
        g2 = dot(gvl[FF : FF + CH, :], gp) + layer_back(g_n2, normed2_k[...].astype(F32), inv_k[1:2])
        yield
        attend = attend_k[...].astype(F32).reshape(HEADS, TXT, TILE_D)
        prod = attend * dot(vob[...], g2.astype(BF)).reshape(HEADS, TXT, TILE_D)
        yield
        g_s = prod - attend * jnp.sum(prod, axis=1, keepdims=True)
        g_n = dot(kqb[...], g_s.reshape(KEYS, TILE_D).astype(BF))
        yield
        g1 = g2 + layer_back(g_n, normed_k[...].astype(F32), inv_k[0:1])
        hg[:, at] = g1
        put(sa, g1, p0, CH)
        yield

    def weave(*parts):
        parts = list(parts)
        while parts:
            parts = [part for part in parts if next(part, True) is None]

    def stages(uw, *states):
        one, two = (cu,) + states[0:5], (uw,) + states[5:10]
        weave(front(0, one))

        def pair(i, carry):
            p0 = al(i * (2 * TILE_D))
            weave(back(p0, one), front(al(p0 + TILE_D), two))
            weave(back(al(p0 + TILE_D), two), front(al(p0 + 2 * TILE_D), one))
            return carry

        lax.fori_loop(0, PIX // (2 * TILE_D) - 1, pair, 0)
        weave(back(PIX - 2 * TILE_D, one), front(PIX - TILE_D, two))
        weave(back(PIX - TILE_D, two))

    state = (
        pltpu.VMEM((KEYS, TILE_D), BF),
        pltpu.VMEM((CH, TILE_D), BF),
        pltpu.VMEM((CH, TILE_D), BF),
        pltpu.VMEM((8, TILE_D), F32),
        pltpu.VMEM((16, TILE_D), BF),
    )
    pl.run_scoped(stages, pltpu.VMEM((CH, PIX), F32), *state, *state)
    ends(sa, 3 * CH)

    def conv_back(weight, src, ys, make=None):
        def body(p0):
            at = pl.ds(p0, TILE_C)
            y = ys[:, at].astype(F32)
            u = conv(weight[...], src, p0, TILE_C, CH) * silu_slope(y)
            cu[:, at] = u
            acc[0] += lane_sum(u)
            acc[1] += lane_sum(u * y)

        acc[...] = jnp.zeros_like(acc)
        if make is None:
            tiles(TILE_C, body, go)
        else:
            stream(TILE_C, make, lambda: ends(src, 3 * CH), body, go)
        return group_mean(gm[...], acc[0]), group_mean(gm[...], acc[1])

    fetch[3].start()
    fetch[2].wait()
    mean, cross = conv_back(wbuf.at[1], sa, y2s)
    inv = stat[1][:, 0:1]

    mean_two, cross_two, inv_two = mean, cross, inv

    def make_c1(p0):
        at = pl.ds(p0, TILE_C)
        put(sb, inv_two * (cu[:, at] - mean_two - y2s[:, at].astype(F32) * cross_two), p0, CH)

    def foot(mx, ds, y1s):
        back = [
            pltpu.make_async_copy(mx_hbm, mx, sems.at[13]),
            pltpu.make_async_copy(ds_hbm, ds, sems.at[14]),
        ]
        get_y1 = pltpu.make_async_copy(y1_hbm, y1s, sems.at[11])
        get_y1.start()
        for copy in back:
            copy.start()
        fetch[3].wait()
        get_y1.wait()
        mean, cross = conv_back(wbuf.at[0], sb, y1s, make_c1)
        inv = stat[0][:, 0:1]
        get_first = pltpu.make_async_copy(sf_hbm, sb, sems.at[12])
        get_first.start()
        for copy in back:
            copy.wait()
        gout[...] = jnp.zeros_like(gout)
        gbias[...] = jnp.zeros_like(gbias)
        wout = wou[:, 0:CH].T

        def body(p0):
            at = pl.ds(p0, TILE)
            g0 = hg[:, at] + inv * (cu[:, at] - mean - y1s[:, at].astype(F32) * cross)
            hg[:, at] = g0
            branch = g0.astype(BF)
            g_inner = (dot(wout, branch) * ds[:, at].astype(F32)).astype(BF)
            sa[0:CH, at] = g_inner
            gout[...] += dot_nt(branch, mx[0:CH, at])
            gbias[0] += lane_sum(g_inner.astype(F32))
            gbias[1] += lane_sum(branch.astype(F32))

        tiles(TILE, body, go)
        get_first.wait()

    pl.run_scoped(foot, *held)
    send_h = pltpu.make_async_copy(hg, gh_hbm, sems.at[7])
    send_g = pltpu.make_async_copy(sa.at[0:CH, 0:PIX], ginner_hbm, sems.at[8])
    send_h.start()
    send_g.start()

    def last(grads):
        for b in range(3):
            grad = dot_nt(sa[0:CH, 0:PIX], sb[:, b * LANES : b * LANES + PIX])
            for a in range(3):
                scatter(grads, grad[:, a * CH : (a + 1) * CH], (3 * a + b) * CH, w_conv, 0, me, count)
        total = jnp.sum(jnp.sum(loss[...], axis=1, keepdims=True), axis=0, keepdims=True)
        row = lax.broadcasted_iota(jnp.int32, (CH, 1), 0)
        value = jnp.where(row == 0, total, jnp.where(row == 1, flag * float(4 * PIX), 0.0))
        triple = jnp.concatenate(split(value), axis=1)
        for k in range(count):
            grads[k, :, w_conv : w_conv + 3] = triple
        keep = pltpu.make_async_copy(grads.at[0:half], keep_hbm, sems.at[9])
        send = pltpu.make_async_copy(grads.at[half:count], send_hbm, sems.at[10])
        keep.start()
        send.start()
        keep.wait()
        send.wait()

    pl.run_scoped(last, pltpu.VMEM((count, CH, w_conv + 3), BF))
    send_h.wait()
    send_g.wait()


def main_call(ints, outs, pieces, wf, gi):
    base, nz, target, kq, kqb, vo, vob, gvt, gvl, velt, temb, wut, git, wb = outs
    count = len(pieces)
    half = count // 2
    w_grad = 9 * CH // count + 3
    vm = pl.BlockSpec(memory_space=pltpu.VMEM)
    sm = pl.BlockSpec(memory_space=pltpu.SMEM)
    hb = pl.BlockSpec(memory_space=pl.ANY)
    shapes = [
        ((CH, CH), F32), ((2, CH, LANES), F32),
        ((half, CH, w_grad), BF), ((half, CH, w_grad), BF),
        ((CH, PIX), BF), ((CH, PIX), F32), ((CH, 9 * CH), BF),
        ((3 * CH, WIDE), BF), ((CH + NZ, PIX), BF), ((CH, PIX), BF), ((CH, PIX), BF),
    ]
    return pl.pallas_call(
        main_kernel,
        out_shape=[jax.ShapeDtypeStruct(*s) for s in shapes],
        in_specs=[sm] + [vm] * 10 + [hb] * (6 + count),
        out_specs=[vm] * 2 + [hb] * 9,
        scratch_shapes=[
            pltpu.VMEM((3 * CH, WIDE), BF),
            pltpu.VMEM((3 * CH, WIDE), BF),
            pltpu.VMEM((CH, PIX), F32),
            pltpu.VMEM((CH, PIX), F32),
            pltpu.VMEM((CH, PIX), BF),
            pltpu.VMEM((2, CH, 9 * CH), BF),
            pltpu.VMEM((2 * FF, CH), BF),
            pltpu.VMEM((CH, 2 * FF), BF),
            pltpu.VMEM((2, CH, LANES), F32),
            pltpu.VMEM((2, CH, LANES), F32),
            pltpu.VMEM((CH, CH), F32),
            pltpu.VMEM((3, CH, LANES), F32),
            pltpu.VMEM((CH, CH + NZ), BF),
            pltpu.VMEM((8, LANES), F32),
            pltpu.SemaphoreType.DMA((15,)),
            pltpu.SemaphoreType.DMA((count,)),
        ],
        compiler_params=pltpu.CompilerParams(vmem_limit_bytes=VMEM_LIMIT),
        cost_estimate=pl.CostEstimate(flops=80_000_000_000, bytes_accessed=60_000_000, transcendentals=0),
        name="main",
    )(ints, target, kq, kqb, vo, vob, gvt, gvl, velt, temb, wut, base, nz, wf, wb, git, gi, *pieces)


def tail_kernel(
    ints, ginner, base, wcf, gout, gbias, gh_hbm, keep_hbm, send_hbm,
    sa, sb, gh, gf, nat, wcb, grads, acc, sems,
):
    me = ints[2]
    go = me >= 0
    half = keep_hbm.shape[0]
    count = 2 * half
    w_in = 9 * UNS // count
    w_out = CH // count
    w_bias = 3 * CH // count
    fetch = pltpu.make_async_copy(gh_hbm, gh, sems.at[0])
    fetch.start()
    wcb[...] = backward_weight(wcf[...], nat)

    def make(p0):
        at = pl.ds(p0, TILE)
        put(sa, ginner[:, at], p0, CH)
        put(sb, base[:, at], p0, UNS)

    acc[...] = jnp.zeros_like(acc)
    fetch.wait()

    def body(p0):
        at = pl.ds(p0, TILE)
        g_first = (gh[:, at] + conv(wcb[...], sa, p0, TILE, CH)).astype(BF)
        gf[:, at] = g_first
        acc[...] += lane_sum(g_first.astype(F32))

    stream(TILE, make, lambda: ends(sa, 3 * CH), body, go)
    ends(sb, 3 * UNS)
    for b in range(3):
        grad = dot_nt(gf[...], sb[:, b * LANES : b * LANES + PIX])
        for a in range(3):
            scatter(grads, grad[:, a * UNS : (a + 1) * UNS], (3 * a + b) * UNS, w_in, 0, me, count)
    scatter(grads, gout[...], 0, w_out, w_in, me, count)
    rows = [jnp.sum(part.T, axis=0, keepdims=True) for part in (acc[...], gbias[0], gbias[1])]
    bias = jnp.concatenate(rows, axis=1)
    first_row = lax.broadcasted_iota(jnp.int32, (8, w_in + w_out), 0) == 0
    for owner in range(count):
        part = bias[:, owner * w_bias : (owner + 1) * w_bias]
        part = jnp.concatenate([part, jnp.zeros((1, w_in + w_out - w_bias), F32)], axis=1)
        grads[slot(owner, me, count), CH : CH + 8, :] = jnp.where(first_row, part, 0.0).astype(BF)
    keep = pltpu.make_async_copy(grads.at[0:half], keep_hbm, sems.at[1])
    send = pltpu.make_async_copy(grads.at[half:count], send_hbm, sems.at[2])
    keep.start()
    send.start()
    keep.wait()
    send.wait()


def tail_call(ints, ginner, base, wcf, gout, gbias, gh, half):
    vm = pl.BlockSpec(memory_space=pltpu.VMEM)
    sm = pl.BlockSpec(memory_space=pltpu.SMEM)
    hb = pl.BlockSpec(memory_space=pl.ANY)
    wide = (9 * UNS + CH) // (2 * half)
    return pl.pallas_call(
        tail_kernel,
        out_shape=[jax.ShapeDtypeStruct((half, CH + 8, wide), BF)] * 2,
        in_specs=[sm] + [vm] * 5 + [hb],
        out_specs=[hb, hb],
        scratch_shapes=[
            pltpu.VMEM((3 * CH, WIDE), BF),
            pltpu.VMEM((3 * UNS, WIDE), BF),
            pltpu.VMEM((CH, PIX), F32),
            pltpu.VMEM((CH, PIX), BF),
            pltpu.VMEM((9 * CH, CH), BF),
            pltpu.VMEM((CH, 9 * CH), BF),
            pltpu.VMEM((2 * half, CH + 8, wide), BF),
            pltpu.VMEM((CH, LANES), F32),
            pltpu.SemaphoreType.DMA((3,)),
        ],
        compiler_params=pltpu.CompilerParams(vmem_limit_bytes=VMEM_LIMIT),
        cost_estimate=pl.CostEstimate(flops=14_000_000_000, bytes_accessed=16_000_000, transcendentals=0),
        name="tail",
    )(ints, ginner, base, wcf, gout, gbias, gh)


def update(master, first, second, grad):
    new_first = BETA_ONE * first + (1.0 - BETA_ONE) * grad
    new_second = BETA_TWO * second + (1.0 - BETA_TWO) * grad * grad
    first_hat = new_first / (1.0 - BETA_ONE**STEP)
    second_hat = new_second / (1.0 - BETA_TWO**STEP)
    new_master = master - LEARN_RATE * (
        first_hat / (jnp.sqrt(second_hat) + ADAM_EPS) + WEIGHT_DECAY * master
    )
    return new_first, new_second, new_master


def adam_kernel(sums, g_one, g_two, *refs):
    ins, outs, (loss, items, norm) = refs[:12], refs[12:24], refs[24:]
    w_in, w_conv, w_out, w_bias = ins[0].shape[1], ins[1].shape[1], ins[2].shape[0], ins[3].shape[1]
    two = g_two[...].astype(F32)
    spare = two[0:8, w_conv : w_conv + 1] + two[0:8, w_conv + 1 : w_conv + 2] + two[0:8, w_conv + 2 : w_conv + 3]
    loss[...] = spare[0:1]
    count = jnp.maximum(spare[1:2], 1.0)
    items[...] = count
    grad_norm = jnp.sqrt(sums[0:1, 0:1]) / count
    norm[...] = grad_norm
    scale = jnp.minimum(1.0, CLIP_MAX / (grad_norm + 1e-06)) / count
    one = g_one[...].astype(F32) * scale
    first = max((one.shape[1] // LANES - 1) * LANES, 0)
    grads = (
        one[0:CH, 0:w_in],
        two[:, 0:w_conv] * scale,
        one[0:CH, first:].T[w_in - first : w_in - first + w_out, :],
        one[CH : CH + 1, 0:w_bias],
    )
    for k in range(4):
        values = update(ins[k][...], ins[4 + k][...], ins[8 + k][...], grads[k])
        for n in range(3):
            outs[4 * n + k][...] = values[n]


def adam_call(sums, g_one, g_two, states):
    vm = pl.BlockSpec(memory_space=pltpu.VMEM)
    return pl.pallas_call(
        adam_kernel,
        out_shape=[jax.ShapeDtypeStruct(s.shape, F32) for s in states] + [jax.ShapeDtypeStruct((1, 1), F32)] * 3,
        in_specs=[vm] * 15,
        out_specs=[vm] * 15,
        compiler_params=pltpu.CompilerParams(vmem_limit_bytes=32 * 2**20),
        cost_estimate=pl.CostEstimate(flops=10_000_000, bytes_accessed=6_000_000, transcendentals=0),
        name="adamw",
    )(sums, g_one, g_two, *states)


def swap(value, axis, bit):
    return lax.ppermute(value, axis, [(i, i ^ bit) for i in range(lax.axis_size(axis))])


def from_chips(piece):
    return [swap(piece, "shard", 2 * j) for j in range(1, lax.axis_size("shard") // 2)]


def tree(parts):
    while len(parts) > 1:
        parts = [parts[k] + parts[k + 1] for k in range(0, len(parts), 2)]
    return parts[0]


def add_low(parts, spare):
    wide = [part.astype(F32) for part in parts]
    total = tree(wide).astype(BF)
    if not spare:
        return total
    at = total.shape[-1] - spare
    triple = split(tree([part[..., at : at + 1] + part[..., at + 1 : at + 2] + part[..., at + 2 : at + 3] for part in wide]))
    column = lax.broadcasted_iota(jnp.int32, total.shape, total.ndim - 1)
    for k in range(3):
        total = jnp.where(column == at + k, triple[k], total)
    return total


def between_chips(part):
    return [part[0]] + [swap(part[j], "shard", 2 * j) for j in range(1, part.shape[0])]


def early(item, frozen):
    cond, clean, noise, tstep, text = item
    unet_conv, res_conv, time_mlp, time_proj, wq, kvproj, wo, geglu_in, geglu_out, vel = frozen
    half = CH // 2
    freqs = jnp.exp(-math.log(10000.0) * jnp.arange(half, dtype=jnp.int32).astype(F32) / half)
    angles = tstep[0].astype(F32) * freqs
    emb = jnp.concatenate([jnp.cos(angles), jnp.sin(angles)])[None, :].astype(BF)
    lat = jnp.stack([clean, noise]).reshape(2, 4, SIDE, 2, SIDE // 2).transpose(0, 1, 4, 3, 2).reshape(2, 4, PIX)
    wf = res_conv.transpose(0, 2, 1)
    outs = prologue(
        tstep, jnp.asarray(schedule()), cond, lat, text, kvproj, wq, wo, geglu_in, geglu_out.T, vel.T,
        jnp.broadcast_to(emb, (16, CH)), time_mlp, time_proj.T, unet_conv, wf,
    )
    return outs, wf, geglu_in


def piece_of(masters):
    w_in, w_conv, w_out, bias = [entry.astype(BF) for entry in masters]
    piece = jnp.concatenate([w_in.T, w_out.T, w_conv.T], axis=1)
    row = jnp.pad(bias[None, :], ((0, 7), (0, piece.shape[1] - bias.shape[0])))
    return jnp.concatenate([piece, row], axis=0)


def per_device(*args):
    conditions, clean, noise, tsteps, text, lengths, valid = args[:7]
    frozen = args[7:17]
    masters, firsts, seconds = args[17:21], args[21:25], args[25:29]
    piece = piece_of(masters)
    even = [piece] + from_chips(piece)
    me = lax.axis_index("shard").astype(jnp.int32)
    ints = jnp.stack([lengths[0], valid[0], me])
    outs, wf, gi = early((conditions[0], clean[0], noise[0], tsteps, text[0]), frozen)
    even, outs, ints = lax.optimization_barrier((even, outs, ints))
    pieces = []
    for part in even:
        pieces += [part, swap(part, "shard", 1)]
    gout, gbias, keep_two, send_two, ginner, gh, wcf, *_ = main_call(ints, outs, pieces, wf, gi)
    two, ginner = lax.optimization_barrier((add_low([keep_two, swap(send_two, "shard", 1)], 3), ginner))
    twos = between_chips(two)
    keep_one, send_one = tail_call(ints, ginner, outs[0], wcf, gout, gbias, gh, len(pieces) // 2)
    twos, keep_one, send_one = lax.optimization_barrier((twos, keep_one, send_one))
    one = add_low([keep_one, swap(send_one, "shard", 1)], 0)
    two = add_low(twos, 3)
    bits = [1 << k for k in reversed(range((lax.axis_size("dp") - 1).bit_length()))]
    ones = between_chips(one)
    for bit in bits:
        twos = [two, swap(two, "dp", bit)]
        ones, twos = lax.optimization_barrier((ones, twos))
        two, one = add_low(twos, 3), add_low(ones, 0)
        ones = [one, swap(one, "dp", bit)]
    one = add_low(ones, 0)
    squares = jnp.sum(jnp.square(one.astype(F32))) + jnp.sum(jnp.square(two[:, :-3].astype(F32)))
    sums = jnp.full((8, LANES), squares)
    sums = sums + swap(sums, "shard", 1)
    sums = tree([sums] + from_chips(sums))
    states = []
    for group in (masters, firsts, seconds):
        states += [group[0].T, group[1].T, group[2], group[3][None, :]]
    new = adam_call(sums, one, two, states)
    results = []
    for n in range(3):
        results += [new[4 * n].T, new[4 * n + 1].T, new[4 * n + 2], new[4 * n + 3][0]]
    return (*[entry[0, 0] for entry in new[12:]], *results)


def solution(mesh):
    both = ("dp", "shard")
    placed = (
        (P(both, None, None, None), P(both, None, None), P(both, None, None), P(both), P(both, None, None), P(both), P(both))
        + (P(),) * 10
        + (P("shard", None), P("shard", None), P("shard", None), P("shard")) * 3
    )
    return jax.shard_map(
        per_device,
        mesh=mesh,
        in_specs=placed,
        out_specs=(P(), P(), P()) + (P("shard", None), P("shard", None), P("shard", None), P("shard")) * 3,
        check_vma=False,
    )
```

```python
import math

import jax
import jax.numpy as jnp
import numpy as np
from jax import lax
from jax.experimental import pallas as pl
from jax.experimental.pallas import tpu as pltpu
from jax.sharding import PartitionSpec as P

HEADS = 8
GROUPS = 32
STEP = 10

LN_EPS = 1e-05
CLIP_MAX = 0.01
LEARN_RATE = 0.02
BETA_ONE = 0.9
BETA_TWO = 0.999
ADAM_EPS = 1e-08
WEIGHT_DECAY = 0.01

BF = jnp.bfloat16
F32 = jnp.float32

SIDE = 64
PIX = SIDE * SIDE
LANES = 128
HALO = LANES
WIDE = PIX + 2 * HALO
CH = 320
UNS = 192
FF = 1280
TXT = 80
KEYS = HEADS * TXT
NZ = 48
NT = (((1,), (1,)), ((), ()))
TN = (((0,), (0,)), ((), ()))
VMEM_LIMIT = 62 * 2**20

TILE = 512
TILE_C = 512
TILE_D = 512
CHUNK = 320


def schedule():
    start = 0.00085**0.5
    final = 0.012**0.5
    betas = (start + np.arange(1000, dtype=np.float64) * ((final - start) / 999.0)) ** 2
    table = np.zeros(1024, np.float32)
    table[:1000] = np.cumprod(1.0 - betas)
    return table.reshape(8, LANES)


def dot(a, b):
    return jnp.dot(a, b, preferred_element_type=F32)


def dot_nt(a, b):
    return lax.dot_general(a, b, NT, preferred_element_type=F32)


def al(x):
    return x if isinstance(x, int) else pl.multiple_of(x, LANES)


def tiles(width, *bodies):
    for p0 in range(0, PIX, width):
        for body in bodies:
            body(p0)


def stream(width, make, ends, use):
    make(0)
    make(PIX - width)
    ends()
    for p0 in range(0, PIX, width):
        if p0 + 2 * width < PIX:
            make(p0 + width)
        use(p0)


def put(dst, value, p0, chans):
    width = value.shape[1]
    low = value.astype(BF)
    for q in range(width // LANES):
        mid = low[:, q * LANES : (q + 1) * LANES]
        lane = lax.broadcasted_iota(jnp.int32, mid.shape, 1) & (SIDE - 1)
        up = jnp.where(lane == 0, jnp.zeros((), BF), pltpu.roll(mid, 1, 1))
        down = jnp.where(lane == SIDE - 1, jnp.zeros((), BF), pltpu.roll(mid, LANES - 1, 1))
        at = pl.ds(al(p0 + HALO + q * LANES), LANES)
        dst[0:chans, at] = up
        dst[chans : 2 * chans, at] = mid
        dst[2 * chans : 3 * chans, at] = down


def ends(dst, rows):
    last = dst[0:rows, PIX : PIX + LANES]
    head = dst[0:rows, HALO : HALO + LANES]
    lane = lax.broadcasted_iota(jnp.int32, last.shape, 1)
    zero = jnp.zeros((), BF)
    dst[0:rows, 0:LANES] = jnp.where(lane >= SIDE, pltpu.roll(last, SIDE, 1), zero)
    dst[0:rows, PIX + HALO : PIX + HALO + LANES] = jnp.where(lane < SIDE, pltpu.roll(head, SIDE, 1), zero)


def conv(weight, src, p0, width, chans):
    parts = []
    for a in range(3):
        for b in range(3):
            parts.append(src[a * chans : (a + 1) * chans, pl.ds(al(p0 + b * LANES), width)])
    return dot(weight, jnp.concatenate(parts, axis=0))


def backward_weight(weight, natural):
    natural[...] = weight.T
    blocks = [natural[(8 - t) * CH : (9 - t) * CH, :] for t in range(9)]
    return jnp.concatenate(blocks, axis=1)


def lane_sum(value):
    total = value[:, 0:LANES]
    for q in range(1, value.shape[1] // LANES):
        total = total + value[:, q * LANES : (q + 1) * LANES]
    return total


def group_mean(gm, *sums):
    joined = sums[0] if len(sums) == 1 else jnp.concatenate(sums, axis=1)
    spread = jnp.dot(gm, joined, precision=lax.Precision.HIGHEST, preferred_element_type=F32)
    share = 1.0 / (PIX * (CH // GROUPS))
    means = [jnp.sum(spread[:, k * LANES : (k + 1) * LANES], axis=1, keepdims=True) * share for k in range(len(sums))]
    return means[0] if len(sums) == 1 else means


def silu_slope(y):
    s = jax.nn.sigmoid(y)
    return s * (1.0 + y * (1.0 - s))


def layer_stats(field):
    mean = jnp.mean(field, axis=0, keepdims=True)
    centered = field - mean
    inv = lax.rsqrt(jnp.mean(centered * centered, axis=0, keepdims=True) + LN_EPS)
    return centered * inv, inv


def layer_back(grad, normed, inv):
    return inv * (
        grad
        - jnp.mean(grad, axis=0, keepdims=True)
        - normed * jnp.mean(grad * normed, axis=0, keepdims=True)
    )


def split(value):
    high = value.astype(BF)
    rest = value - high.astype(F32)
    mid = rest.astype(BF)
    return high, mid, (rest - mid.astype(F32)).astype(BF)


def slot(owner, me, count):
    rel = jnp.bitwise_xor(owner, me)
    return (rel & 1) * (count // 2) + lax.shift_right_logical(rel, 1)


def scatter(dst, value, start, width, lane0, me, count):
    stop = start + value.shape[1]
    for owner in range(count):
        lo, hi = max(start, owner * width), min(stop, (owner + 1) * width)
        if lo < hi:
            at = lane0 + lo - owner * width
            dst[slot(owner, me, count), 0:CH, at : at + hi - lo] = value[:, lo - start : hi - start].astype(BF)


def prologue_kernel(
    steps, table, cond, lat, text, kvproj, wq, wo, gi, got, velt_in, emb, tmlp, tprojt, unet, res,
    base, nz, target, kq, kqb, vo, vob, gvt, gvl, velt, temb, wut, git, wb,
    zs, us, kvs, nat, wsrc, sems,
):
    fetch = [pltpu.make_async_copy(res.at[k], wsrc.at[k], sems.at[k]) for k in range(2)]
    for copy in fetch:
        copy.start()
    index = lax.broadcasted_iota(jnp.int32, (8, LANES), 0) * LANES + lax.broadcasted_iota(jnp.int32, (8, LANES), 1)
    picked = jnp.where(index == steps[0], table[...], 0.0)
    abar = jnp.sum(jnp.sum(picked, axis=1, keepdims=True), axis=0, keepdims=True)
    alpha = jnp.sqrt(abar)
    sigma = jnp.sqrt(1.0 - abar)
    row = lax.broadcasted_iota(jnp.int32, (512, 512), 0)
    col = lax.broadcasted_iota(jnp.int32, (512, 512), 1)
    same = jnp.logical_and((row & 7) == (col >> 6), (row >> 3) == (col & 63))
    perm = jnp.where(same, 1.0, 0.0).astype(BF)
    lane = lax.broadcasted_iota(jnp.int32, (32, 8, LANES), 2)
    for c in range(3):
        zs[...] = lax.dot_general(cond[c], perm, TN, preferred_element_type=F32).reshape(64, 8, 512)
        for k in range(4):
            one = zs[0:32, :, k * LANES : (k + 1) * LANES]
            two = zs[32:64, :, k * LANES : (k + 1) * LANES]
            even = jnp.where(lane < SIDE, one, pltpu.roll(two, SIDE, 2))
            odd = jnp.where(lane < SIDE, pltpu.roll(one, SIDE, 2), two)
            for m in range(32):
                us[16 * k : 16 * k + 8, m * LANES : (m + 1) * LANES] = even[m]
                us[16 * k + 8 : 16 * k + 16, m * LANES : (m + 1) * LANES] = odd[m]
        base[64 * c : 64 * (c + 1), :] = us[...].astype(BF)
    clean = lat[0]
    noise = lat[1]
    noisy = (alpha * clean + sigma * noise).astype(BF).astype(F32)
    target[4:8, :] = jnp.zeros((4, PIX), F32)
    target[0:4, :] = alpha * noise - sigma * clean
    lane = lax.broadcasted_iota(jnp.int32, (4, LANES), 1)
    inside = lane & (SIDE - 1)
    cols = [noisy[:, m * LANES : (m + 1) * LANES] for m in range(32)]
    left = jnp.where(lane >= SIDE, pltpu.roll(cols[31], SIDE, 1), 0.0)
    right = jnp.where(lane < SIDE, pltpu.roll(cols[0], SIDE, 1), 0.0)
    cols = [left] + cols + [right]
    us[0:NZ, :] = jnp.zeros((NZ, PIX), F32)
    for m in range(34):
        up = jnp.where(inside == 0, 0.0, pltpu.roll(cols[m], 1, 1))
        down = jnp.where(inside == SIDE - 1, 0.0, pltpu.roll(cols[m], LANES - 1, 1))
        for a, part in enumerate((up, cols[m], down)):
            for b in range(3):
                at = m - b
                if 0 <= at < 32:
                    r = (3 * a + b) * 4
                    us[r : r + 4, at * LANES : (at + 1) * LANES] = part
    nz[...] = us[0:NZ, :].astype(BF)
    us[0:LANES // 2, 0:CH] = jnp.zeros((LANES // 2, CH), F32)
    us[0:36, 0:CH] = unet[...].astype(F32)
    wide = jnp.concatenate([us[0:64, 0:CH], jnp.zeros((64, CH), F32)], axis=0)
    wut[...] = wide.T.astype(BF)
    kvs[...] = jnp.zeros_like(kvs)
    kvs[0 : text.shape[0], :] = dot(text[...], kvproj[...])
    keys = kvs[:, 0:CH].astype(BF)
    values = kvs[:, CH : 2 * CH].astype(BF)
    head_dim = CH // HEADS
    head = lax.broadcasted_iota(jnp.int32, (TXT, CH), 1)
    own = [jnp.logical_and(head >= h * head_dim, head < (h + 1) * head_dim) for h in range(HEADS)]
    zero = jnp.zeros((), BF)
    kbd = jnp.concatenate([jnp.where(own[h], keys, zero) for h in range(HEADS)], axis=0)
    vbd = jnp.concatenate([jnp.where(own[h], values, zero) for h in range(HEADS)], axis=0)
    scale = head_dim ** (-0.5)
    fold = dot_nt(kbd, wq[...]) * scale
    kq[...] = fold.astype(BF)
    kqb[...] = fold.T.astype(BF)
    fold = dot(vbd, wo[...])
    vob[...] = fold.astype(BF)
    vo[...] = fold.T.astype(BF)
    us[0:8, 0:CH] = jnp.zeros((8, CH), F32)
    us[0:4, 0:CH] = velt_in[...].astype(F32)
    velf = us[0:8, 0:CH]
    velt[...] = velf.astype(BF)
    fold = dot(velf.astype(BF), got[...])
    high = fold.astype(BF).astype(F32)
    both = jnp.concatenate([high, fold - high], axis=0)
    gvt[...] = both.astype(BF)
    wide = jnp.concatenate([both, jnp.zeros((LANES - 16, FF), F32)], axis=0)
    gvl[0:FF, :] = wide.T[:, 0:16].astype(BF)
    wide = jnp.concatenate([velf, jnp.zeros((LANES - 8, CH), F32)], axis=0)
    gvl[FF : FF + CH, :] = wide.T[:, 0:16].astype(BF)
    git[...] = gi[...].T
    hidden = jax.nn.silu(dot(emb[...], tmlp[...])).astype(BF)
    temb[...] = dot_nt(tprojt[...], jnp.concatenate([hidden] * 8, axis=0))
    for k in range(2):
        fetch[k].wait()
        wb[k] = backward_weight(wsrc[k], nat)


def prologue(*args):
    vm = pl.BlockSpec(memory_space=pltpu.VMEM)
    sm = pl.BlockSpec(memory_space=pltpu.SMEM)
    hb = pl.BlockSpec(memory_space=pl.ANY)
    shapes = [
        ((UNS, PIX), BF), ((NZ, PIX), BF), ((8, PIX), F32),
        ((KEYS, CH), BF), ((CH, KEYS), BF), ((CH, KEYS), BF), ((KEYS, CH), BF),
        ((16, FF), BF), ((FF + CH, 16), BF), ((8, CH), BF), ((CH, LANES), F32), ((CH, LANES), BF),
        ((2 * FF, CH), BF), ((2, CH, 9 * CH), BF),
    ]
    return pl.pallas_call(
        prologue_kernel,
        out_shape=[jax.ShapeDtypeStruct(*s) for s in shapes],
        in_specs=[sm] + [vm] * 14 + [hb],
        out_specs=[vm] * len(shapes),
        scratch_shapes=[
            pltpu.VMEM((64, 8, 512), F32),
            pltpu.VMEM((64, PIX), F32),
            pltpu.VMEM((TXT, 2 * CH), F32),
            pltpu.VMEM((9 * CH, CH), BF),
            pltpu.VMEM((2, CH, 9 * CH), BF),
            pltpu.SemaphoreType.DMA((2,)),
        ],
        compiler_params=pltpu.CompilerParams(vmem_limit_bytes=VMEM_LIMIT),
        cost_estimate=pl.CostEstimate(flops=12_000_000_000, bytes_accessed=20_000_000, transcendentals=0),
        name="prologue",
    )(*args)


def main_kernel(
    ints, target, kq, kqb, vo, vob, gvt, gvl, velt, temb, wut, base, nz, wf, wb, git_hbm, gi_hbm, *rest,
):
    count = len(rest) - 27
    pieces = rest[:count]
    (
    gout, gbias, keep_hbm, send_hbm, ginner_hbm, gh_hbm, wcf_hbm, sf_hbm, mx_hbm, ds_hbm, y1_hbm,
    sa, sb, hg, cu, y2s, wbuf, git, gi, acc, stat, gm, bcols, wou, loss, sems, wsems,
    ) = rest[count:]
    length = ints[0]
    flag = ints[1].astype(F32)
    me = ints[2]
    half = count // 2
    w_conv = 9 * CH // count
    w_in = 9 * UNS // count
    w_out = CH // count
    w_bias = 3 * CH // count
    fetch = [
        pltpu.make_async_copy(wf.at[0], wbuf.at[1], sems.at[1]),
        pltpu.make_async_copy(wf.at[1], wbuf.at[0], sems.at[2]),
        pltpu.make_async_copy(wb.at[1], wbuf.at[1], sems.at[3]),
        pltpu.make_async_copy(wb.at[0], wbuf.at[0], sems.at[4]),
    ]
    get_git = pltpu.make_async_copy(git_hbm, git, sems.at[5])
    get_gi = pltpu.make_async_copy(gi_hbm, gi, sems.at[6])
    keep_first = pltpu.make_async_copy(sb, sf_hbm, sems.at[12])

    row = lax.broadcasted_iota(jnp.int32, (CH, CH), 0)
    col = lax.broadcasted_iota(jnp.int32, (CH, CH), 1)
    gm[...] = jnp.where((row * 6554) >> 16 == (col * 6554) >> 16, 1.0, 0.0)

    def norm_silu(field, store, dst, which):
        mean = group_mean(gm[...], acc[0])
        acc[1] = jnp.zeros_like(acc[1])

        def body(p0):
            centered = field[:, pl.ds(p0, TILE)] - mean
            acc[1] += lane_sum(centered * centered)

        tiles(TILE, body)
        inv = lax.rsqrt(group_mean(gm[...], acc[1]) + LN_EPS)
        stat[which] = jnp.broadcast_to(inv, (CH, LANES))
        acc[...] = jnp.zeros_like(acc)

        def make(p0):
            at = pl.ds(p0, TILE)
            y = (field[:, at] - mean) * inv
            store[:, at] = y.astype(BF)
            put(dst, y * jax.nn.sigmoid(y), p0, CH)

        return make

    def head(mx, ds, y1s, got):
        loads = [
            pltpu.make_async_copy(pieces[rel], got.at[jnp.bitwise_xor(me, rel)], wsems.at[rel]) for rel in range(count)
        ]
        get_base = pltpu.make_async_copy(base, ds.at[0:UNS, :], sems.at[9])
        get_nz = pltpu.make_async_copy(nz, mx.at[CH : CH + NZ, :], sems.at[10])
        get_base.start()
        for copy in loads:
            copy.start()
        get_nz.start()
        get_git.start()
        get_gi.start()
        get_base.wait()

        def make_base(p0):
            put(sa, ds[0:UNS, pl.ds(p0, TILE)], p0, UNS)

        for copy in loads:
            copy.wait()
        wbuf[1, :, 0 : 9 * UNS] = jnp.concatenate([got[d, 0:CH, 0:w_in] for d in range(count)], axis=1)
        out_t = jnp.concatenate([got[d, 0:CH, w_in : w_in + w_out] for d in range(count)], axis=1)
        wou[...] = jnp.concatenate([out_t, wut[:, 0:NZ]], axis=1)
        bias = jnp.concatenate([got[d, CH : CH + 8, 0:w_bias].astype(F32) for d in range(count)], axis=1)
        for k in range(3):
            part = jnp.concatenate([bias[:, k * CH : (k + 1) * CH]] * 16, axis=0)
            bcols[k] = part.T

        def body(p0):
            at = pl.ds(p0, TILE)
            first = conv(wbuf[1, :, 0 : 9 * UNS], sa, p0, TILE, UNS) + bcols[0, :, 0:1]
            hg[:, at] = first
            put(sb, first, p0, CH)

        stream(TILE, make_base, lambda: ends(sa, 3 * UNS), body)
        ends(sb, 3 * CH)
        keep_first.start()

        get_nz.wait()
        fetch[0].start()
        acc[...] = jnp.zeros_like(acc)
        skip = w_in + w_out
        wbuf[0] = jnp.concatenate([got[d, 0:CH, skip : skip + w_conv] for d in range(count)], axis=1)
        keep_w = pltpu.make_async_copy(wbuf.at[0], wcf_hbm, sems.at[0])
        keep_w.start()

        def body(p0):
            at = pl.ds(p0, TILE)
            inner = conv(wbuf[0], sb, p0, TILE, CH) + bcols[1, :, 0:1]
            s = jax.nn.sigmoid(inner)
            m = inner * s
            mx[0:CH, at] = m.astype(BF)
            ds[:, at] = (s + m * (1.0 - s)).astype(BF)
            h0 = hg[:, at] + dot(wou[...], mx[:, at]) + bcols[2, :, 0:1]
            hg[:, at] = h0
            acc[0] += lane_sum(h0)

        tiles(TILE, body)
        keep_mx = pltpu.make_async_copy(mx, mx_hbm, sems.at[13])
        keep_ds = pltpu.make_async_copy(ds, ds_hbm, sems.at[14])
        keep_mx.start()
        keep_ds.start()
        keep_w.wait()
        fetch[1].start()
        make = norm_silu(hg, y1s, sa, 0)
        fetch[0].wait()

        def body(p0):
            at = pl.ds(p0, TILE_C)
            c1 = conv(wbuf[1], sa, p0, TILE_C, CH) + temb[:, 0:1]
            cu[:, at] = c1
            acc[0] += lane_sum(c1)

        stream(TILE, make, lambda: ends(sa, 3 * CH), body)
        keep_y1 = pltpu.make_async_copy(y1s, y1_hbm, sems.at[11])
        keep_y1.start()
        keep_mx.wait()
        keep_ds.wait()
        keep_y1.wait()

    held = (pltpu.VMEM((CH + NZ, PIX), BF), pltpu.VMEM((CH, PIX), BF), pltpu.VMEM((CH, PIX), BF))
    pl.run_scoped(head, *held, pltpu.VMEM((count,) + pieces[0].shape, BF))
    fetch[2].start()
    keep_first.wait()
    make = norm_silu(cu, y2s, sb, 1)
    tiles(TILE, make)
    ends(sb, 3 * CH)

    fetch[1].wait()
    get_git.wait()
    get_gi.wait()
    loss[...] = jnp.zeros_like(loss)
    token = lax.broadcasted_iota(jnp.int32, (1, TXT, 1), 1)
    bias = jnp.where(token < length, 0.0, -1000000000.0)

    def front(p0, keep):
        uw, attend_k, normed_k, normed2_k, inv_k, gp_k = keep
        at = pl.ds(p0, TILE_D)
        h1 = hg[:, at] + conv(wbuf[0], sb, p0, TILE_D, CH)
        yield
        normed, inv = layer_stats(h1)
        low = normed.astype(BF)
        normed_k[...] = low
        inv_k[0:1] = inv
        s = dot(kq[...], low).reshape(HEADS, TXT, TILE_D) + bias
        yield
        e = jnp.exp(s - jnp.max(s, axis=1, keepdims=True))
        attend = (e * (1.0 / jnp.sum(e, axis=1, keepdims=True))).reshape(KEYS, TILE_D).astype(BF)
        attend_k[...] = attend
        yield
        h2 = h1 + dot(vo[...], attend)
        normed2, inv2 = layer_stats(h2)
        n2 = normed2.astype(BF)
        normed2_k[...] = n2
        inv_k[1:2] = inv2
        yield
        acts = []
        for n in range(FF // CHUNK):
            f = n * CHUNK
            val = dot(git[f : f + CHUNK, :], n2)
            gate = dot(git[FF + f : FF + f + CHUNK, :], n2)
            phi = 0.5 + 0.5 * lax.erf(gate * 0.5**0.5)
            u = gate * phi
            slope = phi + gate * (jnp.exp(-0.5 * gate * gate) * (2.0 * math.pi) ** (-0.5))
            acts.append((val * u).astype(BF))
            col = n * TILE_D
            uw[:, col : col + TILE_D] = u.astype(BF)
            uw[:, PIX // 2 + col : PIX // 2 + col + TILE_D] = (val * slope).astype(BF)
            yield
        both = dot(gvt[...], jnp.concatenate(acts, axis=0))
        diff = both[0:8] + both[8:16] + dot(velt[...], h2.astype(BF)) - target[:, at]
        loss[...] += lane_sum(diff * diff) * flag
        gp = (diff * (2.0 * flag)).astype(BF)
        gp_k[...] = jnp.concatenate([gp, gp], axis=0)
        yield

    def back(p0, keep):
        uw, attend_k, normed_k, normed2_k, inv_k, gp_k = keep
        at = pl.ds(p0, TILE_D)
        gp = gp_k[...]
        pieces = []
        for n in range(FF // CHUNK):
            g_act = dot(gvl[n * CHUNK : (n + 1) * CHUNK, :], gp).astype(BF)
            col = n * TILE_D
            pieces.insert(n, g_act * uw[:, col : col + TILE_D])
            pieces.append(g_act * uw[:, PIX // 2 + col : PIX // 2 + col + TILE_D])
        yield
        g_n2 = dot(gi[...], jnp.concatenate(pieces, axis=0))
        yield
        g2 = dot(gvl[FF : FF + CH, :], gp) + layer_back(g_n2, normed2_k[...].astype(F32), inv_k[1:2])
        yield
        attend = attend_k[...].astype(F32).reshape(HEADS, TXT, TILE_D)
        prod = attend * dot(vob[...], g2.astype(BF)).reshape(HEADS, TXT, TILE_D)
        yield
        g_s = prod - attend * jnp.sum(prod, axis=1, keepdims=True)
        g_n = dot(kqb[...], g_s.reshape(KEYS, TILE_D).astype(BF))
        yield
        g1 = g2 + layer_back(g_n, normed_k[...].astype(F32), inv_k[0:1])
        hg[:, at] = g1
        put(sa, g1, p0, CH)
        yield

    def weave(*parts):
        parts = list(parts)
        while parts:
            parts = [part for part in parts if next(part, True) is None]

    def stages(*states):
        one, two = states[0:6], states[6:12]
        weave(front(0, one))

        def pair(i, carry):
            p0 = al(i * (2 * TILE_D))
            weave(back(p0, one), front(al(p0 + TILE_D), two))
            weave(back(al(p0 + TILE_D), two), front(al(p0 + 2 * TILE_D), one))
            return carry

        lax.fori_loop(0, PIX // (2 * TILE_D) - 1, pair, 0)
        weave(back(PIX - 2 * TILE_D, one), front(PIX - TILE_D, two))
        weave(back(PIX - TILE_D, two))

    state = (
        pltpu.VMEM((CH, PIX), BF),
        pltpu.VMEM((KEYS, TILE_D), BF),
        pltpu.VMEM((CH, TILE_D), BF),
        pltpu.VMEM((CH, TILE_D), BF),
        pltpu.VMEM((8, TILE_D), F32),
        pltpu.VMEM((16, TILE_D), BF),
    )
    pl.run_scoped(stages, *state, *state)
    ends(sa, 3 * CH)

    def conv_back(weight, src, ys, make=None):
        def body(p0):
            at = pl.ds(p0, TILE_C)
            y = ys[:, at].astype(F32)
            u = conv(weight[...], src, p0, TILE_C, CH) * silu_slope(y)
            cu[:, at] = u
            acc[0] += lane_sum(u)
            acc[1] += lane_sum(u * y)

        acc[...] = jnp.zeros_like(acc)
        if make is None:
            tiles(TILE_C, body)
        else:
            stream(TILE_C, make, lambda: ends(src, 3 * CH), body)
        return group_mean(gm[...], acc[0], acc[1])

    fetch[3].start()
    fetch[2].wait()
    mean, cross = conv_back(wbuf.at[1], sa, y2s)
    inv = stat[1][:, 0:1]

    mean_two, cross_two, inv_two = mean, cross, inv

    def make_c1(p0):
        at = pl.ds(p0, TILE_C)
        put(sb, inv_two * (cu[:, at] - mean_two - y2s[:, at].astype(F32) * cross_two), p0, CH)

    def foot(mx, ds, y1s):
        back = [
            pltpu.make_async_copy(mx_hbm, mx, sems.at[13]),
            pltpu.make_async_copy(ds_hbm, ds, sems.at[14]),
        ]
        get_y1 = pltpu.make_async_copy(y1_hbm, y1s, sems.at[11])
        get_y1.start()
        for copy in back:
            copy.start()
        fetch[3].wait()
        get_y1.wait()
        mean, cross = conv_back(wbuf.at[0], sb, y1s, make_c1)
        inv = stat[0][:, 0:1]
        get_first = pltpu.make_async_copy(sf_hbm, sb, sems.at[12])
        get_first.start()
        for copy in back:
            copy.wait()
        gbias[...] = jnp.zeros_like(gbias)
        wout = wou[:, 0:CH].T

        def body(p0):
            at = pl.ds(p0, TILE)
            g0 = hg[:, at] + inv * (cu[:, at] - mean - y1s[:, at].astype(F32) * cross)
            hg[:, at] = g0
            branch = g0.astype(BF)
            g_inner = (dot(wout, branch) * ds[:, at].astype(F32)).astype(BF)
            sa[0:CH, at] = g_inner
            y1s[:, at] = branch
            gbias[0] += lane_sum(g_inner.astype(F32))
            gbias[1] += lane_sum(branch.astype(F32))

        tiles(TILE, body)
        gout[...] = dot_nt(y1s[...], mx[0:CH, :])
        get_first.wait()

    pl.run_scoped(foot, *held)
    send_h = pltpu.make_async_copy(hg, gh_hbm, sems.at[7])
    send_g = pltpu.make_async_copy(sa.at[0:CH, 0:PIX], ginner_hbm, sems.at[8])
    send_h.start()
    send_g.start()

    def last(grads):
        for b in range(3):
            grad = dot_nt(sa[0:CH, 0:PIX], sb[:, b * LANES : b * LANES + PIX])
            for a in range(3):
                scatter(grads, grad[:, a * CH : (a + 1) * CH], (3 * a + b) * CH, w_conv, 0, me, count)
        total = jnp.sum(jnp.sum(loss[...], axis=1, keepdims=True), axis=0, keepdims=True)
        lane = lax.broadcasted_iota(jnp.int32, (8, w_conv), 1)
        row = lax.broadcasted_iota(jnp.int32, (8, w_conv), 0)
        value = jnp.where(lane == 0, total, jnp.where(lane == 1, flag * float(4 * PIX), 0.0))
        high, mid, low = [part.astype(F32) for part in split(value)]
        triple = jnp.where(row == 0, high, jnp.where(row == 1, mid, jnp.where(row == 2, low, 0.0))).astype(BF)
        for k in range(count):
            grads[k, CH : CH + 8, :] = triple
        keep = pltpu.make_async_copy(grads.at[0:half], keep_hbm, sems.at[9])
        send = pltpu.make_async_copy(grads.at[half:count], send_hbm, sems.at[10])
        keep.start()
        send.start()
        keep.wait()
        send.wait()

    pl.run_scoped(last, pltpu.VMEM((count, CH + 8, w_conv), BF))
    send_h.wait()
    send_g.wait()


def main_call(ints, outs, pieces, wf, gi):
    base, nz, target, kq, kqb, vo, vob, gvt, gvl, velt, temb, wut, git, wb = outs
    count = len(pieces)
    half = count // 2
    w_grad = 9 * CH // count
    vm = pl.BlockSpec(memory_space=pltpu.VMEM)
    sm = pl.BlockSpec(memory_space=pltpu.SMEM)
    hb = pl.BlockSpec(memory_space=pl.ANY)
    shapes = [
        ((CH, CH), F32), ((2, CH, LANES), F32),
        ((half, CH + 8, w_grad), BF), ((half, CH + 8, w_grad), BF),
        ((CH, PIX), BF), ((CH, PIX), F32), ((CH, 9 * CH), BF),
        ((3 * CH, WIDE), BF), ((CH + NZ, PIX), BF), ((CH, PIX), BF), ((CH, PIX), BF),
    ]
    return pl.pallas_call(
        main_kernel,
        out_shape=[jax.ShapeDtypeStruct(*s) for s in shapes],
        in_specs=[sm] + [vm] * 10 + [hb] * (6 + count),
        out_specs=[vm] * 2 + [hb] * 9,
        scratch_shapes=[
            pltpu.VMEM((3 * CH, WIDE), BF),
            pltpu.VMEM((3 * CH, WIDE), BF),
            pltpu.VMEM((CH, PIX), F32),
            pltpu.VMEM((CH, PIX), F32),
            pltpu.VMEM((CH, PIX), BF),
            pltpu.VMEM((2, CH, 9 * CH), BF),
            pltpu.VMEM((2 * FF, CH), BF),
            pltpu.VMEM((CH, 2 * FF), BF),
            pltpu.VMEM((2, CH, LANES), F32),
            pltpu.VMEM((2, CH, LANES), F32),
            pltpu.VMEM((CH, CH), F32),
            pltpu.VMEM((3, CH, LANES), F32),
            pltpu.VMEM((CH, CH + NZ), BF),
            pltpu.VMEM((8, LANES), F32),
            pltpu.SemaphoreType.DMA((15,)),
            pltpu.SemaphoreType.DMA((count,)),
        ],
        compiler_params=pltpu.CompilerParams(vmem_limit_bytes=VMEM_LIMIT),
        cost_estimate=pl.CostEstimate(flops=80_000_000_000, bytes_accessed=60_000_000, transcendentals=0),
        name="main",
    )(ints, target, kq, kqb, vo, vob, gvt, gvl, velt, temb, wut, base, nz, wf, wb, git, gi, *pieces)


def tail_kernel(
    ints, ginner, base, wcf, gout, gbias, gh_hbm, keep_hbm, send_hbm,
    sa, sb, gh, gf, nat, wcb, grads, acc, sems,
):
    me = ints[2]
    half = keep_hbm.shape[0]
    count = 2 * half
    w_in = 9 * UNS // count
    w_out = CH // count
    w_bias = 3 * CH // count
    fetch = pltpu.make_async_copy(gh_hbm, gh, sems.at[0])
    fetch.start()
    wcb[...] = backward_weight(wcf[...], nat)

    def make(p0):
        at = pl.ds(p0, TILE)
        put(sa, ginner[:, at], p0, CH)
        put(sb, base[:, at], p0, UNS)

    acc[...] = jnp.zeros_like(acc)
    fetch.wait()

    def body(p0):
        at = pl.ds(p0, TILE)
        g_first = (gh[:, at] + conv(wcb[...], sa, p0, TILE, CH)).astype(BF)
        gf[:, at] = g_first
        acc[...] += lane_sum(g_first.astype(F32))

    stream(TILE, make, lambda: ends(sa, 3 * CH), body)
    ends(sb, 3 * UNS)
    for b in range(3):
        grad = dot_nt(gf[...], sb[:, b * LANES : b * LANES + PIX])
        for a in range(3):
            scatter(grads, grad[:, a * UNS : (a + 1) * UNS], (3 * a + b) * UNS, w_in, 0, me, count)
    scatter(grads, gout[...], 0, w_out, w_in, me, count)
    rows = [jnp.sum(part.T, axis=0, keepdims=True) for part in (acc[...], gbias[0], gbias[1])]
    bias = jnp.concatenate(rows, axis=1)
    first_row = lax.broadcasted_iota(jnp.int32, (8, w_in + w_out), 0) == 0
    for owner in range(count):
        part = bias[:, owner * w_bias : (owner + 1) * w_bias]
        part = jnp.concatenate([part, jnp.zeros((1, w_in + w_out - w_bias), F32)], axis=1)
        grads[slot(owner, me, count), CH : CH + 8, :] = jnp.where(first_row, part, 0.0).astype(BF)
    keep = pltpu.make_async_copy(grads.at[0:half], keep_hbm, sems.at[1])
    send = pltpu.make_async_copy(grads.at[half:count], send_hbm, sems.at[2])
    keep.start()
    send.start()
    keep.wait()
    send.wait()


def tail_call(ints, ginner, base, wcf, gout, gbias, gh, half):
    vm = pl.BlockSpec(memory_space=pltpu.VMEM)
    sm = pl.BlockSpec(memory_space=pltpu.SMEM)
    hb = pl.BlockSpec(memory_space=pl.ANY)
    wide = (9 * UNS + CH) // (2 * half)
    return pl.pallas_call(
        tail_kernel,
        out_shape=[jax.ShapeDtypeStruct((half, CH + 8, wide), BF)] * 2,
        in_specs=[sm] + [vm] * 5 + [hb],
        out_specs=[hb, hb],
        scratch_shapes=[
            pltpu.VMEM((3 * CH, WIDE), BF),
            pltpu.VMEM((3 * UNS, WIDE), BF),
            pltpu.VMEM((CH, PIX), F32),
            pltpu.VMEM((CH, PIX), BF),
            pltpu.VMEM((9 * CH, CH), BF),
            pltpu.VMEM((CH, 9 * CH), BF),
            pltpu.VMEM((2 * half, CH + 8, wide), BF),
            pltpu.VMEM((CH, LANES), F32),
            pltpu.SemaphoreType.DMA((3,)),
        ],
        compiler_params=pltpu.CompilerParams(vmem_limit_bytes=VMEM_LIMIT),
        cost_estimate=pl.CostEstimate(flops=14_000_000_000, bytes_accessed=16_000_000, transcendentals=0),
        name="tail",
    )(ints, ginner, base, wcf, gout, gbias, gh)


def update(master, first, second, grad):
    new_first = BETA_ONE * first + (1.0 - BETA_ONE) * grad
    new_second = BETA_TWO * second + (1.0 - BETA_TWO) * grad * grad
    first_hat = new_first / (1.0 - BETA_ONE**STEP)
    second_hat = new_second / (1.0 - BETA_TWO**STEP)
    new_master = master - LEARN_RATE * (
        first_hat / (jnp.sqrt(second_hat) + ADAM_EPS) + WEIGHT_DECAY * master
    )
    return new_first, new_second, new_master


def adam_kernel(sums, g_one, g_two, *refs):
    ins, outs, (loss, items, norm) = refs[:12], refs[12:24], refs[24:]
    w_in, w_conv, w_out, w_bias = ins[0].shape[1], ins[1].shape[1], ins[2].shape[0], ins[3].shape[1]
    two = g_two[...].astype(F32)
    spare = two[CH : CH + 1] + two[CH + 1 : CH + 2] + two[CH + 2 : CH + 3]
    loss[...] = spare[:, 0:1]
    count = jnp.maximum(spare[:, 1:2], 1.0)
    items[...] = count
    grad_norm = jnp.sqrt(sums[0:1, 0:1]) / count
    norm[...] = grad_norm
    scale = jnp.minimum(1.0, CLIP_MAX / (grad_norm + 1e-06)) / count
    one = g_one[...].astype(F32) * scale
    first = max((one.shape[1] // LANES - 1) * LANES, 0)
    grads = (
        one[0:CH, 0:w_in],
        two[0:CH] * scale,
        one[0:CH, first:].T[w_in - first : w_in - first + w_out, :],
        one[CH : CH + 1, 0:w_bias],
    )
    for k in range(4):
        values = update(ins[k][...], ins[4 + k][...], ins[8 + k][...], grads[k])
        for n in range(3):
            outs[4 * n + k][...] = values[n]


def adam_call(sums, g_one, g_two, states):
    vm = pl.BlockSpec(memory_space=pltpu.VMEM)
    return pl.pallas_call(
        adam_kernel,
        out_shape=[jax.ShapeDtypeStruct(s.shape, F32) for s in states] + [jax.ShapeDtypeStruct((1, 1), F32)] * 3,
        in_specs=[vm] * 15,
        out_specs=[vm] * 15,
        compiler_params=pltpu.CompilerParams(vmem_limit_bytes=32 * 2**20),
        cost_estimate=pl.CostEstimate(flops=10_000_000, bytes_accessed=6_000_000, transcendentals=0),
        name="adamw",
    )(sums, g_one, g_two, *states)


def swap(value, axis, bit):
    return lax.ppermute(value, axis, [(i, i ^ bit) for i in range(lax.axis_size(axis))])


def from_chips(piece):
    return [swap(piece, "shard", 2 * j) for j in range(1, lax.axis_size("shard") // 2)]


def tree(parts):
    while len(parts) > 1:
        parts = [parts[k] + parts[k + 1] for k in range(0, len(parts), 2)]
    return parts[0]


def add_low(parts, spare):
    wide = [part.astype(F32) for part in parts]
    total = tree(wide).astype(BF)
    if not spare:
        return total
    at = total.shape[-2] - 8
    rows = [part[..., at:, :] for part in wide]
    value = tree([part[..., 0:1, :] + part[..., 1:2, :] + part[..., 2:3, :] for part in rows])
    row = lax.broadcasted_iota(jnp.int32, total.shape, total.ndim - 2)
    for k, part in enumerate(split(value)):
        total = jnp.where(row == at + k, part, total)
    return total


def between_chips(part):
    return [part[0]] + [swap(part[j], "shard", 2 * j) for j in range(1, part.shape[0])]


def early(item, frozen):
    cond, clean, noise, tstep, text = item
    unet_conv, res_conv, time_mlp, time_proj, wq, kvproj, wo, geglu_in, geglu_out, vel = frozen
    half = CH // 2
    freqs = jnp.exp(-math.log(10000.0) * jnp.arange(half, dtype=jnp.int32).astype(F32) / half)
    angles = tstep[0].astype(F32) * freqs
    emb = jnp.concatenate([jnp.cos(angles), jnp.sin(angles)])[None, :].astype(BF)
    lat = jnp.stack([clean, noise]).reshape(2, 4, SIDE, 2, SIDE // 2).transpose(0, 1, 4, 3, 2).reshape(2, 4, PIX)
    wf = res_conv.transpose(0, 2, 1)
    outs = prologue(
        tstep, jnp.asarray(schedule()), cond, lat, text, kvproj, wq, wo, geglu_in, geglu_out.T, vel.T,
        jnp.broadcast_to(emb, (16, CH)), time_mlp, time_proj.T, unet_conv, wf,
    )
    return outs, wf, geglu_in


def piece_kernel(w_in, w_conv, w_out, bias, piece):
    rows = w_out.shape[0]
    tall = jnp.concatenate([w_out[...], jnp.zeros((LANES - rows, CH), F32)], axis=0) if rows % 8 == 0 else None
    out_t = tall.T[:, 0:rows] if rows % 8 == 0 else w_out[...].T
    piece[0:CH, :] = jnp.concatenate([w_in[...], out_t, w_conv[...]], axis=1).astype(BF)
    pad = piece.shape[1] - bias.shape[1]
    row = jnp.concatenate([bias[...], jnp.zeros((1, pad), F32)], axis=1)
    first_row = lax.broadcasted_iota(jnp.int32, (8, piece.shape[1]), 0) == 0
    piece[CH : CH + 8, :] = jnp.where(first_row, row, 0.0).astype(BF)


def piece_of(masters):
    w_in, w_conv, w_out, bias = masters
    vm = pl.BlockSpec(memory_space=pltpu.VMEM)
    width = w_in.shape[0] + w_out.shape[0] + w_conv.shape[0]
    return pl.pallas_call(
        piece_kernel,
        out_shape=jax.ShapeDtypeStruct((CH + 8, width), BF),
        in_specs=[vm] * 4,
        out_specs=vm,
        compiler_params=pltpu.CompilerParams(vmem_limit_bytes=16 * 2**20),
        name="piece",
    )(w_in.T, w_conv.T, w_out, bias[None, :])


def per_device(*args):
    conditions, clean, noise, tsteps, text, lengths, valid = args[:7]
    frozen = args[7:17]
    masters, firsts, seconds = args[17:21], args[21:25], args[25:29]
    piece = piece_of(masters)
    even = [piece] + from_chips(piece)
    me = lax.axis_index("shard").astype(jnp.int32)
    ints = jnp.stack([lengths[0], valid[0], me])
    outs, wf, gi = early((conditions[0], clean[0], noise[0], tsteps, text[0]), frozen)
    even, outs, ints = lax.optimization_barrier((even, outs, ints))
    pieces = []
    for part in even:
        pieces += [part, swap(part, "shard", 1)]
    gout, gbias, keep_two, send_two, ginner, gh, wcf, *_ = main_call(ints, outs, pieces, wf, gi)
    two, ginner = lax.optimization_barrier((add_low([keep_two, swap(send_two, "shard", 1)], True), ginner))
    twos = between_chips(two)
    keep_one, send_one = tail_call(ints, ginner, outs[0], wcf, gout, gbias, gh, len(pieces) // 2)
    twos, keep_one, send_one = lax.optimization_barrier((twos, keep_one, send_one))
    one = add_low([keep_one, swap(send_one, "shard", 1)], False)
    two = add_low(twos, True)
    bits = [1 << k for k in reversed(range((lax.axis_size("dp") - 1).bit_length()))]
    ones = between_chips(one)
    for bit in bits:
        twos = [two, swap(two, "dp", bit)]
        ones, twos = lax.optimization_barrier((ones, twos))
        two, one = add_low(twos, True), add_low(ones, False)
        ones = [one, swap(one, "dp", bit)]
    one = add_low(ones, False)
    squares = jnp.sum(jnp.square(one.astype(F32))) + jnp.sum(jnp.square(two[:CH].astype(F32)))
    sums = jnp.full((8, LANES), squares)
    sums = sums + swap(sums, "shard", 1)
    sums = tree([sums] + from_chips(sums))
    states = []
    for group in (masters, firsts, seconds):
        states += [group[0].T, group[1].T, group[2], group[3][None, :]]
    new = adam_call(sums, one, two, states)
    results = []
    for n in range(3):
        results += [new[4 * n].T, new[4 * n + 1].T, new[4 * n + 2], new[4 * n + 3][0]]
    return (*[entry[0, 0] for entry in new[12:]], *results)


def solution(mesh):
    both = ("dp", "shard")
    placed = (
        (P(both, None, None, None), P(both, None, None), P(both, None, None), P(both), P(both, None, None), P(both), P(both))
        + (P(),) * 10
        + (P("shard", None), P("shard", None), P("shard", None), P("shard")) * 3
    )
    return jax.shard_map(
        per_device,
        mesh=mesh,
        in_specs=placed,
        out_specs=(P(), P(), P()) + (P("shard", None), P("shard", None), P("shard", None), P("shard")) * 3,
        check_vma=False,
    )
```

```python
import math

import jax
import jax.numpy as jnp
import numpy as np
from jax import lax
from jax.experimental import pallas as pl
from jax.experimental.pallas import tpu as pltpu
from jax.sharding import PartitionSpec as P

HEADS = 8
GROUPS = 32
STEP = 10

LN_EPS = 1e-05
CLIP_MAX = 0.01
LEARN_RATE = 0.02
BETA_ONE = 0.9
BETA_TWO = 0.999
ADAM_EPS = 1e-08
WEIGHT_DECAY = 0.01

BF = jnp.bfloat16
F32 = jnp.float32

SIDE = 64
PIX = SIDE * SIDE
LANES = 128
HALO = LANES
WIDE = PIX + 2 * HALO
CH = 320
UNS = 192
FF = 1280
TXT = 80
KEYS = HEADS * TXT
NZ = 48
NT = (((1,), (1,)), ((), ()))
TN = (((0,), (0,)), ((), ()))
VMEM_LIMIT = 62 * 2**20

TILE = 512
TILE_C = 512
TILE_D = 512
W_PAD = 2944
DEPTH = 1024
CHUNK = 320


def schedule():
    start = 0.00085**0.5
    final = 0.012**0.5
    betas = (start + np.arange(1000, dtype=np.float64) * ((final - start) / 999.0)) ** 2
    table = np.zeros(1024, np.float32)
    table[:1000] = np.cumprod(1.0 - betas)
    return table.reshape(8, LANES)


def dot(a, b):
    return jnp.dot(a, b, preferred_element_type=F32)


def dot_nt(a, b):
    return lax.dot_general(a, b, NT, preferred_element_type=F32)


def al(x):
    return x if isinstance(x, int) else pl.multiple_of(x, LANES)


def tiles(width, *bodies):
    for p0 in range(0, PIX, width):
        for body in bodies:
            body(p0)


def stream(width, make, ends, use):
    make(0)
    make(PIX - width)
    ends()
    for p0 in range(0, PIX, width):
        if p0 + 2 * width < PIX:
            make(p0 + width)
        use(p0)


def put(dst, value, p0, chans):
    width = value.shape[1]
    low = value.astype(BF)
    for q in range(width // LANES):
        mid = low[:, q * LANES : (q + 1) * LANES]
        lane = lax.broadcasted_iota(jnp.int32, mid.shape, 1) & (SIDE - 1)
        up = jnp.where(lane == 0, jnp.zeros((), BF), pltpu.roll(mid, 1, 1))
        down = jnp.where(lane == SIDE - 1, jnp.zeros((), BF), pltpu.roll(mid, LANES - 1, 1))
        at = pl.ds(al(p0 + HALO + q * LANES), LANES)
        dst[0:chans, at] = up
        dst[chans : 2 * chans, at] = mid
        dst[2 * chans : 3 * chans, at] = down


def ends(dst, rows):
    last = dst[0:rows, PIX : PIX + LANES]
    head = dst[0:rows, HALO : HALO + LANES]
    lane = lax.broadcasted_iota(jnp.int32, last.shape, 1)
    zero = jnp.zeros((), BF)
    dst[0:rows, 0:LANES] = jnp.where(lane >= SIDE, pltpu.roll(last, SIDE, 1), zero)
    dst[0:rows, PIX + HALO : PIX + HALO + LANES] = jnp.where(lane < SIDE, pltpu.roll(head, SIDE, 1), zero)


def conv(weight, src, p0, width, chans):
    parts = []
    for a in range(3):
        for b in range(3):
            parts.append(src[a * chans : (a + 1) * chans, pl.ds(al(p0 + b * LANES), width)])
    return dot(weight, jnp.concatenate(parts, axis=0))


def short_weight(weight):
    cols = []
    for b in range(3):
        taps = [weight[:, (3 * a + b) * CH : (3 * a + b + 1) * CH] for a in range(3)]
        cols.append(jnp.concatenate(taps + [jnp.zeros((CH, DEPTH - 3 * CH), BF)], axis=1))
    wide = [col.astype(F32) for col in cols]
    outer, middle = 0.5 * (wide[0] + wide[2]), 0.5 * wide[1]
    return cols[0], (outer + middle).astype(BF), (outer - middle).astype(BF), cols[2]


def conv_short(weight, src, p0, width):
    d = [src[0 : 3 * CH, pl.ds(al(p0 + k * LANES), LANES)] for k in range(width // LANES + 2)]
    pairs = range(0, width // LANES, 2)
    mixed = (
        [d[k] - d[k + 2] for k in pairs],
        [d[k + 1] + d[k + 2] for k in pairs],
        [d[k + 2] - d[k + 1] for k in pairs],
        [d[k + 1] - d[k + 3] for k in pairs],
    )
    rest = jnp.zeros((DEPTH - 3 * CH, width // 2), BF)
    m = [dot(weight[q], jnp.concatenate([jnp.concatenate(mixed[q], axis=1), rest], axis=0)) for q in range(4)]
    both, other = m[1] + m[2], m[1] - m[2]
    even = both + m[0]
    odd = other - m[3]
    outs = []
    for k in range(width // LANES // 2):
        at = slice(k * LANES, (k + 1) * LANES)
        outs += [even[:, at], odd[:, at]]
    return jnp.concatenate(outs, axis=1)


def backward_weight(weight, natural):
    natural[...] = weight.T
    blocks = [natural[(8 - t) * CH : (9 - t) * CH, :] for t in range(9)]
    return jnp.concatenate(blocks, axis=1)


def lane_sum(value):
    total = value[:, 0:LANES]
    for q in range(1, value.shape[1] // LANES):
        total = total + value[:, q * LANES : (q + 1) * LANES]
    return total


def group_mean(gm, *sums):
    joined = sums[0] if len(sums) == 1 else jnp.concatenate(sums, axis=1)
    spread = jnp.dot(gm, joined, precision=lax.Precision.HIGHEST, preferred_element_type=F32)
    share = 1.0 / (PIX * (CH // GROUPS))
    means = [jnp.sum(spread[:, k * LANES : (k + 1) * LANES], axis=1, keepdims=True) * share for k in range(len(sums))]
    return means[0] if len(sums) == 1 else means


def silu_slope(y):
    s = jax.nn.sigmoid(y)
    return s * (1.0 + y * (1.0 - s))


def layer_stats(field):
    mean = jnp.mean(field, axis=0, keepdims=True)
    centered = field - mean
    inv = lax.rsqrt(jnp.mean(centered * centered, axis=0, keepdims=True) + LN_EPS)
    return centered * inv, inv


def layer_back(grad, normed, inv):
    return inv * (
        grad
        - jnp.mean(grad, axis=0, keepdims=True)
        - normed * jnp.mean(grad * normed, axis=0, keepdims=True)
    )


def split(value):
    high = value.astype(BF)
    rest = value - high.astype(F32)
    mid = rest.astype(BF)
    return high, mid, (rest - mid.astype(F32)).astype(BF)


def slot(owner, me, count):
    rel = jnp.bitwise_xor(owner, me)
    return (rel & 1) * (count // 2) + lax.shift_right_logical(rel, 1)


def scatter(dst, value, start, width, lane0, me, count):
    stop = start + value.shape[1]
    for owner in range(count):
        lo, hi = max(start, owner * width), min(stop, (owner + 1) * width)
        if lo < hi:
            at = lane0 + lo - owner * width
            dst[slot(owner, me, count), 0:CH, at : at + hi - lo] = value[:, lo - start : hi - start].astype(BF)


def prologue_kernel(
    steps, table, cond, lat, text, kvproj, wq, wo, gi, got, velt_in, emb, tmlp, tprojt, unet, res,
    base, nz, target, kq, kqb, vo, vob, gvt, gvl, velt, temb, wut, git, wf, wb,
    zs, us, kvs, nat, wsrc, sems,
):
    fetch = [pltpu.make_async_copy(res.at[k], wsrc.at[k], sems.at[k]) for k in range(2)]
    for copy in fetch:
        copy.start()
    index = lax.broadcasted_iota(jnp.int32, (8, LANES), 0) * LANES + lax.broadcasted_iota(jnp.int32, (8, LANES), 1)
    picked = jnp.where(index == steps[0], table[...], 0.0)
    abar = jnp.sum(jnp.sum(picked, axis=1, keepdims=True), axis=0, keepdims=True)
    alpha = jnp.sqrt(abar)
    sigma = jnp.sqrt(1.0 - abar)
    row = lax.broadcasted_iota(jnp.int32, (512, 512), 0)
    col = lax.broadcasted_iota(jnp.int32, (512, 512), 1)
    same = jnp.logical_and((row & 7) == (col >> 6), (row >> 3) == (col & 63))
    perm = jnp.where(same, 1.0, 0.0).astype(BF)
    lane = lax.broadcasted_iota(jnp.int32, (32, 8, LANES), 2)
    for c in range(3):
        zs[...] = lax.dot_general(cond[c], perm, TN, preferred_element_type=F32).reshape(64, 8, 512)
        for k in range(4):
            one = zs[0:32, :, k * LANES : (k + 1) * LANES]
            two = zs[32:64, :, k * LANES : (k + 1) * LANES]
            even = jnp.where(lane < SIDE, one, pltpu.roll(two, SIDE, 2))
            odd = jnp.where(lane < SIDE, pltpu.roll(one, SIDE, 2), two)
            for m in range(32):
                us[16 * k : 16 * k + 8, m * LANES : (m + 1) * LANES] = even[m]
                us[16 * k + 8 : 16 * k + 16, m * LANES : (m + 1) * LANES] = odd[m]
        base[64 * c : 64 * (c + 1), :] = us[...].astype(BF)
    clean = lat[0]
    noise = lat[1]
    noisy = (alpha * clean + sigma * noise).astype(BF).astype(F32)
    target[4:8, :] = jnp.zeros((4, PIX), F32)
    target[0:4, :] = alpha * noise - sigma * clean
    lane = lax.broadcasted_iota(jnp.int32, (4, LANES), 1)
    inside = lane & (SIDE - 1)
    cols = [noisy[:, m * LANES : (m + 1) * LANES] for m in range(32)]
    left = jnp.where(lane >= SIDE, pltpu.roll(cols[31], SIDE, 1), 0.0)
    right = jnp.where(lane < SIDE, pltpu.roll(cols[0], SIDE, 1), 0.0)
    cols = [left] + cols + [right]
    us[0:NZ, :] = jnp.zeros((NZ, PIX), F32)
    for m in range(34):
        up = jnp.where(inside == 0, 0.0, pltpu.roll(cols[m], 1, 1))
        down = jnp.where(inside == SIDE - 1, 0.0, pltpu.roll(cols[m], LANES - 1, 1))
        for a, part in enumerate((up, cols[m], down)):
            for b in range(3):
                at = m - b
                if 0 <= at < 32:
                    r = (3 * a + b) * 4
                    us[r : r + 4, at * LANES : (at + 1) * LANES] = part
    nz[...] = us[0:NZ, :].astype(BF)
    us[0:LANES // 2, 0:CH] = jnp.zeros((LANES // 2, CH), F32)
    us[0:36, 0:CH] = unet[...].astype(F32)
    wide = jnp.concatenate([us[0:64, 0:CH], jnp.zeros((64, CH), F32)], axis=0)
    wut[...] = wide.T.astype(BF)
    kvs[...] = jnp.zeros_like(kvs)
    kvs[0 : text.shape[0], :] = dot(text[...], kvproj[...])
    keys = kvs[:, 0:CH].astype(BF)
    values = kvs[:, CH : 2 * CH].astype(BF)
    head_dim = CH // HEADS
    head = lax.broadcasted_iota(jnp.int32, (TXT, CH), 1)
    own = [jnp.logical_and(head >= h * head_dim, head < (h + 1) * head_dim) for h in range(HEADS)]
    zero = jnp.zeros((), BF)
    kbd = jnp.concatenate([jnp.where(own[h], keys, zero) for h in range(HEADS)], axis=0)
    vbd = jnp.concatenate([jnp.where(own[h], values, zero) for h in range(HEADS)], axis=0)
    scale = head_dim ** (-0.5)
    fold = dot_nt(kbd, wq[...]) * scale
    kq[...] = fold.astype(BF)
    kqb[...] = fold.T.astype(BF)
    fold = dot(vbd, wo[...])
    vob[...] = fold.astype(BF)
    vo[...] = fold.T.astype(BF)
    us[0:8, 0:CH] = jnp.zeros((8, CH), F32)
    us[0:4, 0:CH] = velt_in[...].astype(F32)
    velf = us[0:8, 0:CH]
    velt[...] = velf.astype(BF)
    fold = dot(velf.astype(BF), got[...])
    high = fold.astype(BF).astype(F32)
    both = jnp.concatenate([high, fold - high], axis=0)
    gvt[...] = both.astype(BF)
    wide = jnp.concatenate([both, jnp.zeros((LANES - 16, FF), F32)], axis=0)
    gvl[0:FF, :] = wide.T[:, 0:16].astype(BF)
    wide = jnp.concatenate([velf, jnp.zeros((LANES - 8, CH), F32)], axis=0)
    gvl[FF : FF + CH, :] = wide.T[:, 0:16].astype(BF)
    git[...] = gi[...].T
    hidden = jax.nn.silu(dot(emb[...], tmlp[...])).astype(BF)
    temb[...] = dot_nt(tprojt[...], jnp.concatenate([hidden] * 8, axis=0))
    for k in range(2):
        fetch[k].wait()
        for q, part in enumerate(short_weight(wsrc[k])):
            wf[k, q] = part
        for q, part in enumerate(short_weight(backward_weight(wsrc[k], nat))):
            wb[k, q] = part


def prologue(*args):
    vm = pl.BlockSpec(memory_space=pltpu.VMEM)
    sm = pl.BlockSpec(memory_space=pltpu.SMEM)
    hb = pl.BlockSpec(memory_space=pl.ANY)
    shapes = [
        ((UNS, PIX), BF), ((NZ, PIX), BF), ((8, PIX), F32),
        ((KEYS, CH), BF), ((CH, KEYS), BF), ((CH, KEYS), BF), ((KEYS, CH), BF),
        ((16, FF), BF), ((FF + CH, 16), BF), ((8, CH), BF), ((CH, LANES), F32), ((CH, LANES), BF),
        ((2 * FF, CH), BF), ((2, 4, CH, DEPTH), BF), ((2, 4, CH, DEPTH), BF),
    ]
    return pl.pallas_call(
        prologue_kernel,
        out_shape=[jax.ShapeDtypeStruct(*s) for s in shapes],
        in_specs=[sm] + [vm] * 14 + [hb],
        out_specs=[vm] * len(shapes),
        scratch_shapes=[
            pltpu.VMEM((64, 8, 512), F32),
            pltpu.VMEM((64, PIX), F32),
            pltpu.VMEM((TXT, 2 * CH), F32),
            pltpu.VMEM((9 * CH, CH), BF),
            pltpu.VMEM((2, CH, 9 * CH), BF),
            pltpu.SemaphoreType.DMA((2,)),
        ],
        compiler_params=pltpu.CompilerParams(vmem_limit_bytes=VMEM_LIMIT),
        cost_estimate=pl.CostEstimate(flops=12_000_000_000, bytes_accessed=20_000_000, transcendentals=0),
        name="prologue",
    )(*args)


def main_kernel(
    ints, target, kq, kqb, vo, vob, gvt, gvl, velt, temb, wut, base, nz, wf, wb, git_hbm, gi_hbm, *rest,
):
    count = len(rest) - 27
    pieces = rest[:count]
    (
    gout, gbias, keep_hbm, send_hbm, ginner_hbm, gh_hbm, wcf_hbm, sf_hbm, mx_hbm, ds_hbm, y1_hbm,
    sa, sb, hg, cu, y2s, wbuf, git, gi, acc, stat, gm, bcols, wou, loss, sems, wsems,
    ) = rest[count:]
    length = ints[0]
    flag = ints[1].astype(F32)
    me = ints[2]
    half = count // 2
    w_conv = 9 * CH // count
    w_in = 9 * UNS // count
    w_out = CH // count
    w_bias = 3 * CH // count
    fetch = [
        pltpu.make_async_copy(wf.at[0], wbuf.at[1], sems.at[1]),
        pltpu.make_async_copy(wf.at[1], wbuf.at[0], sems.at[2]),
        pltpu.make_async_copy(wb.at[1], wbuf.at[1], sems.at[3]),
        pltpu.make_async_copy(wb.at[0], wbuf.at[0], sems.at[4]),
    ]
    get_git = pltpu.make_async_copy(git_hbm, git, sems.at[5])
    get_gi = pltpu.make_async_copy(gi_hbm, gi, sems.at[6])
    keep_first = pltpu.make_async_copy(sb, sf_hbm, sems.at[12])

    row = lax.broadcasted_iota(jnp.int32, (CH, CH), 0)
    col = lax.broadcasted_iota(jnp.int32, (CH, CH), 1)
    gm[...] = jnp.where((row * 6554) >> 16 == (col * 6554) >> 16, 1.0, 0.0)

    def norm_silu(field, store, dst, which):
        mean = group_mean(gm[...], acc[0])
        acc[1] = jnp.zeros_like(acc[1])

        def body(p0):
            centered = field[:, pl.ds(p0, TILE)] - mean
            acc[1] += lane_sum(centered * centered)

        tiles(TILE, body)
        inv = lax.rsqrt(group_mean(gm[...], acc[1]) + LN_EPS)
        stat[which] = jnp.broadcast_to(inv, (CH, LANES))
        acc[...] = jnp.zeros_like(acc)

        def make(p0):
            at = pl.ds(p0, TILE)
            y = (field[:, at] - mean) * inv
            store[:, at] = y.astype(BF)
            put(dst, y * jax.nn.sigmoid(y), p0, CH)

        return make

    def head(mx, ds, y1s):
        get_base = pltpu.make_async_copy(base, ds.at[0:UNS, :], sems.at[9])
        get_nz = pltpu.make_async_copy(nz, mx.at[CH : CH + NZ, :], sems.at[10])
        get_base.start()
        get_nz.start()
        get_git.start()
        get_gi.start()
        get_base.wait()

        def make_base(p0):
            put(sa, ds[0:UNS, pl.ds(p0, TILE)], p0, UNS)

        def assemble(got):
            loads = [
                pltpu.make_async_copy(pieces[rel], got.at[jnp.bitwise_xor(me, rel)], wsems.at[rel]) for rel in range(count)
            ]
            for copy in loads:
                copy.start()
            for copy in loads:
                copy.wait()
            mx[0:CH, 0 : 9 * UNS] = jnp.concatenate([got[d, 0:CH, 0:w_in] for d in range(count)], axis=1)
            out_t = jnp.concatenate([got[d, 0:CH, w_in : w_in + w_out] for d in range(count)], axis=1)
            wou[...] = jnp.concatenate([out_t, wut[:, 0:NZ]], axis=1)
            bias = jnp.concatenate([got[d, CH : CH + 8, 0:w_bias].astype(F32) for d in range(count)], axis=1)
            for k in range(3):
                part = jnp.concatenate([bias[:, k * CH : (k + 1) * CH]] * 16, axis=0)
                bcols[k] = part.T
            skip = w_in + w_out
            y1s[:, 0 : 9 * CH] = jnp.concatenate([got[d, 0:CH, skip : skip + w_conv] for d in range(count)], axis=1)
            y1s[:, 9 * CH : W_PAD] = jnp.zeros((CH, W_PAD - 9 * CH), BF)
            for q, part in enumerate(short_weight(y1s[:, 0 : 9 * CH])):
                wbuf[0, q] = part

        pl.run_scoped(assemble, pltpu.VMEM((count,) + pieces[0].shape, BF))

        def body(p0):
            at = pl.ds(p0, TILE)
            first = conv(mx[0:CH, 0 : 9 * UNS], sa, p0, TILE, UNS) + bcols[0, :, 0:1]
            hg[:, at] = first
            put(sb, first, p0, CH)

        stream(TILE, make_base, lambda: ends(sa, 3 * UNS), body)
        ends(sb, 3 * CH)
        keep_first.start()

        get_nz.wait()
        fetch[0].start()
        acc[...] = jnp.zeros_like(acc)
        keep_w = pltpu.make_async_copy(y1s.at[:, 0:W_PAD], wcf_hbm, sems.at[0])
        keep_w.start()

        def body(p0):
            at = pl.ds(p0, TILE)
            inner = conv_short(wbuf.at[0], sb, p0, TILE) + bcols[1, :, 0:1]
            s = jax.nn.sigmoid(inner)
            m = inner * s
            mx[0:CH, at] = m.astype(BF)
            ds[:, at] = (s + m * (1.0 - s)).astype(BF)
            h0 = hg[:, at] + dot(wou[...], mx[:, at]) + bcols[2, :, 0:1]
            hg[:, at] = h0
            acc[0] += lane_sum(h0)

        tiles(TILE, body)
        keep_mx = pltpu.make_async_copy(mx, mx_hbm, sems.at[13])
        keep_ds = pltpu.make_async_copy(ds, ds_hbm, sems.at[14])
        keep_mx.start()
        keep_ds.start()
        keep_w.wait()
        fetch[1].start()
        make = norm_silu(hg, y1s, sa, 0)
        fetch[0].wait()

        def body(p0):
            at = pl.ds(p0, TILE_C)
            c1 = conv_short(wbuf.at[1], sa, p0, TILE_C) + temb[:, 0:1]
            cu[:, at] = c1
            acc[0] += lane_sum(c1)

        stream(TILE, make, lambda: ends(sa, 3 * CH), body)
        keep_y1 = pltpu.make_async_copy(y1s, y1_hbm, sems.at[11])
        keep_y1.start()
        keep_mx.wait()
        keep_ds.wait()
        keep_y1.wait()

    held = (pltpu.VMEM((CH + NZ, PIX), BF), pltpu.VMEM((CH, PIX), BF), pltpu.VMEM((CH, PIX), BF))
    pl.run_scoped(head, *held)
    fetch[2].start()
    keep_first.wait()
    make = norm_silu(cu, y2s, sb, 1)
    tiles(TILE, make)
    ends(sb, 3 * CH)

    fetch[1].wait()
    get_git.wait()
    get_gi.wait()
    loss[...] = jnp.zeros_like(loss)
    token = lax.broadcasted_iota(jnp.int32, (1, TXT, 1), 1)
    bias = jnp.where(token < length, 0.0, -1000000000.0)

    def front(p0, keep):
        uw, attend_k, normed_k, normed2_k, inv_k, gp_k = keep
        at = pl.ds(p0, TILE_D)
        h1 = hg[:, at] + conv_short(wbuf.at[0], sb, p0, TILE_D)
        yield
        normed, inv = layer_stats(h1)
        low = normed.astype(BF)
        normed_k[...] = low
        inv_k[0:1] = inv
        s = dot(kq[...], low).reshape(HEADS, TXT, TILE_D) + bias
        yield
        e = jnp.exp(s - jnp.max(s, axis=1, keepdims=True))
        attend = (e * (1.0 / jnp.sum(e, axis=1, keepdims=True))).reshape(KEYS, TILE_D).astype(BF)
        attend_k[...] = attend
        yield
        h2 = h1 + dot(vo[...], attend)
        normed2, inv2 = layer_stats(h2)
        n2 = normed2.astype(BF)
        normed2_k[...] = n2
        inv_k[1:2] = inv2
        yield
        acts = []
        for n in range(FF // CHUNK):
            f = n * CHUNK
            val = dot(git[f : f + CHUNK, :], n2)
            gate = dot(git[FF + f : FF + f + CHUNK, :], n2)
            phi = 0.5 + 0.5 * lax.erf(gate * 0.5**0.5)
            u = gate * phi
            slope = phi + gate * (jnp.exp(-0.5 * gate * gate) * (2.0 * math.pi) ** (-0.5))
            acts.append((val * u).astype(BF))
            col = n * TILE_D
            uw[:, col : col + TILE_D] = u.astype(uw.dtype)
            uw[:, PIX // 2 + col : PIX // 2 + col + TILE_D] = (val * slope).astype(uw.dtype)
            yield
        both = dot(gvt[...], jnp.concatenate(acts, axis=0))
        diff = both[0:8] + both[8:16] + dot(velt[...], h2.astype(BF)) - target[:, at]
        loss[...] += lane_sum(diff * diff) * flag
        gp = (diff * (2.0 * flag)).astype(BF)
        gp_k[...] = jnp.concatenate([gp, gp], axis=0)
        yield

    def back(p0, keep):
        uw, attend_k, normed_k, normed2_k, inv_k, gp_k = keep
        at = pl.ds(p0, TILE_D)
        gp = gp_k[...]
        pieces = []
        for n in range(FF // CHUNK):
            g_act = dot(gvl[n * CHUNK : (n + 1) * CHUNK, :], gp).astype(uw.dtype)
            col = n * TILE_D
            pieces.insert(n, (g_act * uw[:, col : col + TILE_D]).astype(BF))
            pieces.append((g_act * uw[:, PIX // 2 + col : PIX // 2 + col + TILE_D]).astype(BF))
        yield
        g_n2 = dot(gi[...], jnp.concatenate(pieces, axis=0))
        yield
        g2 = dot(gvl[FF : FF + CH, :], gp) + layer_back(g_n2, normed2_k[...].astype(F32), inv_k[1:2])
        yield
        attend = attend_k[...].astype(F32).reshape(HEADS, TXT, TILE_D)
        prod = attend * dot(vob[...], g2.astype(BF)).reshape(HEADS, TXT, TILE_D)
        yield
        g_s = prod - attend * jnp.sum(prod, axis=1, keepdims=True)
        g_n = dot(kqb[...], g_s.reshape(KEYS, TILE_D).astype(BF))
        yield
        g1 = g2 + layer_back(g_n, normed_k[...].astype(F32), inv_k[0:1])
        hg[:, at] = g1
        put(sa, g1, p0, CH)
        yield

    def weave(*parts):
        parts = list(parts)
        while parts:
            parts = [part for part in parts if next(part, True) is None]

    def stages(uw, *states):
        one, two = (cu,) + states[0:5], (uw,) + states[5:10]
        weave(front(0, one))

        def pair(i, carry):
            p0 = al(i * (2 * TILE_D))
            weave(back(p0, one), front(al(p0 + TILE_D), two))
            weave(back(al(p0 + TILE_D), two), front(al(p0 + 2 * TILE_D), one))
            return carry

        lax.fori_loop(0, PIX // (2 * TILE_D) - 1, pair, 0)
        weave(back(PIX - 2 * TILE_D, one), front(PIX - TILE_D, two))
        weave(back(PIX - TILE_D, two))

    state = (
        pltpu.VMEM((KEYS, TILE_D), BF),
        pltpu.VMEM((CH, TILE_D), BF),
        pltpu.VMEM((CH, TILE_D), BF),
        pltpu.VMEM((8, TILE_D), F32),
        pltpu.VMEM((16, TILE_D), BF),
    )
    pl.run_scoped(stages, pltpu.VMEM((CH, PIX), BF), *state, *state)
    ends(sa, 3 * CH)

    def conv_back(weight, src, ys, make=None):
        def body(p0):
            at = pl.ds(p0, TILE_C)
            y = ys[:, at].astype(F32)
            u = conv_short(weight, src, p0, TILE_C) * silu_slope(y)
            cu[:, at] = u
            acc[0] += lane_sum(u)
            acc[1] += lane_sum(u * y)

        acc[...] = jnp.zeros_like(acc)
        if make is None:
            tiles(TILE_C, body)
        else:
            stream(TILE_C, make, lambda: ends(src, 3 * CH), body)
        return group_mean(gm[...], acc[0], acc[1])

    fetch[3].start()
    fetch[2].wait()
    mean, cross = conv_back(wbuf.at[1], sa, y2s)
    inv = stat[1][:, 0:1]

    mean_two, cross_two, inv_two = mean, cross, inv

    def make_c1(p0):
        at = pl.ds(p0, TILE_C)
        put(sb, inv_two * (cu[:, at] - mean_two - y2s[:, at].astype(F32) * cross_two), p0, CH)

    def foot(mx, ds, y1s):
        back = [
            pltpu.make_async_copy(mx_hbm, mx, sems.at[13]),
            pltpu.make_async_copy(ds_hbm, ds, sems.at[14]),
        ]
        get_y1 = pltpu.make_async_copy(y1_hbm, y1s, sems.at[11])
        get_y1.start()
        for copy in back:
            copy.start()
        fetch[3].wait()
        get_y1.wait()
        mean, cross = conv_back(wbuf.at[0], sb, y1s, make_c1)
        inv = stat[0][:, 0:1]
        get_first = pltpu.make_async_copy(sf_hbm, sb, sems.at[12])
        get_first.start()
        for copy in back:
            copy.wait()
        gbias[...] = jnp.zeros_like(gbias)
        wout = wou[:, 0:CH].T

        def body(p0):
            at = pl.ds(p0, TILE)
            g0 = hg[:, at] + inv * (cu[:, at] - mean - y1s[:, at].astype(F32) * cross)
            hg[:, at] = g0
            branch = g0.astype(BF)
            g_inner = (dot(wout, branch) * ds[:, at].astype(F32)).astype(BF)
            sa[0:CH, at] = g_inner
            y1s[:, at] = branch
            gbias[0] += lane_sum(g_inner.astype(F32))
            gbias[1] += lane_sum(branch.astype(F32))

        tiles(TILE, body)
        gout[...] = dot_nt(y1s[...], mx[0:CH, :])
        get_first.wait()

    pl.run_scoped(foot, *held)
    send_h = pltpu.make_async_copy(hg, gh_hbm, sems.at[7])
    send_g = pltpu.make_async_copy(sa.at[0:CH, 0:PIX], ginner_hbm, sems.at[8])
    send_h.start()
    send_g.start()

    def last(grads):
        for b in range(3):
            grad = dot_nt(sa[0:CH, 0:PIX], sb[:, b * LANES : b * LANES + PIX])
            for a in range(3):
                scatter(grads, grad[:, a * CH : (a + 1) * CH], (3 * a + b) * CH, w_conv, 0, me, count)
        total = jnp.sum(jnp.sum(loss[...], axis=1, keepdims=True), axis=0, keepdims=True)
        lane = lax.broadcasted_iota(jnp.int32, (8, w_conv), 1)
        row = lax.broadcasted_iota(jnp.int32, (8, w_conv), 0)
        value = jnp.where(lane == 0, total, jnp.where(lane == 1, flag * float(4 * PIX), 0.0))
        high, mid, low = [part.astype(F32) for part in split(value)]
        triple = jnp.where(row == 0, high, jnp.where(row == 1, mid, jnp.where(row == 2, low, 0.0))).astype(BF)
        for k in range(count):
            grads[k, CH : CH + 8, :] = triple
        keep = pltpu.make_async_copy(grads.at[0:half], keep_hbm, sems.at[9])
        send = pltpu.make_async_copy(grads.at[half:count], send_hbm, sems.at[10])
        keep.start()
        send.start()
        keep.wait()
        send.wait()

    pl.run_scoped(last, pltpu.VMEM((count, CH + 8, w_conv), BF))
    send_h.wait()
    send_g.wait()


def main_call(ints, outs, pieces, gi):
    base, nz, target, kq, kqb, vo, vob, gvt, gvl, velt, temb, wut, git, wf, wb = outs
    count = len(pieces)
    half = count // 2
    w_grad = 9 * CH // count
    vm = pl.BlockSpec(memory_space=pltpu.VMEM)
    sm = pl.BlockSpec(memory_space=pltpu.SMEM)
    hb = pl.BlockSpec(memory_space=pl.ANY)
    shapes = [
        ((CH, CH), F32), ((2, CH, LANES), F32),
        ((half, CH + 8, w_grad), BF), ((half, CH + 8, w_grad), BF),
        ((CH, PIX), BF), ((CH, PIX), F32), ((CH, W_PAD), BF),
        ((3 * CH, WIDE), BF), ((CH + NZ, PIX), BF), ((CH, PIX), BF), ((CH, PIX), BF),
    ]
    return pl.pallas_call(
        main_kernel,
        out_shape=[jax.ShapeDtypeStruct(*s) for s in shapes],
        in_specs=[sm] + [vm] * 10 + [hb] * (6 + count),
        out_specs=[vm] * 2 + [hb] * 9,
        scratch_shapes=[
            pltpu.VMEM((3 * CH, WIDE), BF),
            pltpu.VMEM((3 * CH, WIDE), BF),
            pltpu.VMEM((CH, PIX), F32),
            pltpu.VMEM((CH, PIX), F32),
            pltpu.VMEM((CH, PIX), BF),
            pltpu.VMEM((2, 4, CH, DEPTH), BF),
            pltpu.VMEM((2 * FF, CH), BF),
            pltpu.VMEM((CH, 2 * FF), BF),
            pltpu.VMEM((2, CH, LANES), F32),
            pltpu.VMEM((2, CH, LANES), F32),
            pltpu.VMEM((CH, CH), F32),
            pltpu.VMEM((3, CH, LANES), F32),
            pltpu.VMEM((CH, CH + NZ), BF),
            pltpu.VMEM((8, LANES), F32),
            pltpu.SemaphoreType.DMA((15,)),
            pltpu.SemaphoreType.DMA((count,)),
        ],
        compiler_params=pltpu.CompilerParams(vmem_limit_bytes=VMEM_LIMIT),
        cost_estimate=pl.CostEstimate(flops=80_000_000_000, bytes_accessed=60_000_000, transcendentals=0),
        name="main",
    )(ints, target, kq, kqb, vo, vob, gvt, gvl, velt, temb, wut, base, nz, wf, wb, git, gi, *pieces)


def tail_kernel(
    ints, ginner, base, wcf, gout, gbias, gh_hbm, keep_hbm, send_hbm,
    sa, sb, gh, gf, nat, wcb, grads, acc, sems,
):
    me = ints[2]
    half = keep_hbm.shape[0]
    count = 2 * half
    w_in = 9 * UNS // count
    w_out = CH // count
    w_bias = 3 * CH // count
    fetch = pltpu.make_async_copy(gh_hbm, gh, sems.at[0])
    fetch.start()
    for q, part in enumerate(short_weight(backward_weight(wcf[:, 0 : 9 * CH], nat))):
        wcb[q] = part

    def make(p0):
        at = pl.ds(p0, TILE)
        put(sa, ginner[:, at], p0, CH)
        put(sb, base[:, at], p0, UNS)

    acc[...] = jnp.zeros_like(acc)
    fetch.wait()

    def body(p0):
        at = pl.ds(p0, TILE)
        g_first = (gh[:, at] + conv_short(wcb, sa, p0, TILE)).astype(BF)
        gf[:, at] = g_first
        acc[...] += lane_sum(g_first.astype(F32))

    stream(TILE, make, lambda: ends(sa, 3 * CH), body)
    ends(sb, 3 * UNS)
    for b in range(3):
        grad = dot_nt(gf[...], sb[:, b * LANES : b * LANES + PIX])
        for a in range(3):
            scatter(grads, grad[:, a * UNS : (a + 1) * UNS], (3 * a + b) * UNS, w_in, 0, me, count)
    scatter(grads, gout[...], 0, w_out, w_in, me, count)
    rows = [jnp.sum(part.T, axis=0, keepdims=True) for part in (acc[...], gbias[0], gbias[1])]
    bias = jnp.concatenate(rows, axis=1)
    first_row = lax.broadcasted_iota(jnp.int32, (8, w_in + w_out), 0) == 0
    for owner in range(count):
        part = bias[:, owner * w_bias : (owner + 1) * w_bias]
        part = jnp.concatenate([part, jnp.zeros((1, w_in + w_out - w_bias), F32)], axis=1)
        grads[slot(owner, me, count), CH : CH + 8, :] = jnp.where(first_row, part, 0.0).astype(BF)
    keep = pltpu.make_async_copy(grads.at[0:half], keep_hbm, sems.at[1])
    send = pltpu.make_async_copy(grads.at[half:count], send_hbm, sems.at[2])
    keep.start()
    send.start()
    keep.wait()
    send.wait()


def tail_call(ints, ginner, base, wcf, gout, gbias, gh, half):
    vm = pl.BlockSpec(memory_space=pltpu.VMEM)
    sm = pl.BlockSpec(memory_space=pltpu.SMEM)
    hb = pl.BlockSpec(memory_space=pl.ANY)
    wide = (9 * UNS + CH) // (2 * half)
    return pl.pallas_call(
        tail_kernel,
        out_shape=[jax.ShapeDtypeStruct((half, CH + 8, wide), BF)] * 2,
        in_specs=[sm] + [vm] * 5 + [hb],
        out_specs=[hb, hb],
        scratch_shapes=[
            pltpu.VMEM((3 * CH, WIDE), BF),
            pltpu.VMEM((3 * UNS, WIDE), BF),
            pltpu.VMEM((CH, PIX), F32),
            pltpu.VMEM((CH, PIX), BF),
            pltpu.VMEM((9 * CH, CH), BF),
            pltpu.VMEM((4, CH, DEPTH), BF),
            pltpu.VMEM((2 * half, CH + 8, wide), BF),
            pltpu.VMEM((CH, LANES), F32),
            pltpu.SemaphoreType.DMA((3,)),
        ],
        compiler_params=pltpu.CompilerParams(vmem_limit_bytes=VMEM_LIMIT),
        cost_estimate=pl.CostEstimate(flops=14_000_000_000, bytes_accessed=16_000_000, transcendentals=0),
        name="tail",
    )(ints, ginner, base, wcf, gout, gbias, gh)


def update(master, first, second, grad):
    new_first = BETA_ONE * first + (1.0 - BETA_ONE) * grad
    new_second = BETA_TWO * second + (1.0 - BETA_TWO) * grad * grad
    first_hat = new_first / (1.0 - BETA_ONE**STEP)
    second_hat = new_second / (1.0 - BETA_TWO**STEP)
    new_master = master - LEARN_RATE * (
        first_hat / (jnp.sqrt(second_hat) + ADAM_EPS) + WEIGHT_DECAY * master
    )
    return new_first, new_second, new_master


def adam_kernel(sums, g_one, g_two, *refs):
    ins, outs, (loss, items, norm) = refs[:12], refs[12:24], refs[24:]
    w_in, w_conv, w_out, w_bias = ins[0].shape[1], ins[1].shape[1], ins[2].shape[0], ins[3].shape[1]
    two = g_two[...].astype(F32)
    spare = two[CH : CH + 1] + two[CH + 1 : CH + 2] + two[CH + 2 : CH + 3]
    loss[...] = spare[:, 0:1]
    count = jnp.maximum(spare[:, 1:2], 1.0)
    items[...] = count
    grad_norm = jnp.sqrt(sums[0:1, 0:1]) / count
    norm[...] = grad_norm
    scale = jnp.minimum(1.0, CLIP_MAX / (grad_norm + 1e-06)) / count
    one = g_one[...].astype(F32) * scale
    first = max((one.shape[1] // LANES - 1) * LANES, 0)
    grads = (
        one[0:CH, 0:w_in],
        two[0:CH] * scale,
        one[0:CH, first:].T[w_in - first : w_in - first + w_out, :],
        one[CH : CH + 1, 0:w_bias],
    )
    for k in range(4):
        values = update(ins[k][...], ins[4 + k][...], ins[8 + k][...], grads[k])
        for n in range(3):
            outs[4 * n + k][...] = values[n]


def adam_call(sums, g_one, g_two, states):
    vm = pl.BlockSpec(memory_space=pltpu.VMEM)
    return pl.pallas_call(
        adam_kernel,
        out_shape=[jax.ShapeDtypeStruct(s.shape, F32) for s in states] + [jax.ShapeDtypeStruct((1, 1), F32)] * 3,
        in_specs=[vm] * 15,
        out_specs=[vm] * 15,
        compiler_params=pltpu.CompilerParams(vmem_limit_bytes=32 * 2**20),
        cost_estimate=pl.CostEstimate(flops=10_000_000, bytes_accessed=6_000_000, transcendentals=0),
        name="adamw",
    )(sums, g_one, g_two, *states)


def swap(value, axis, bit):
    return lax.ppermute(value, axis, [(i, i ^ bit) for i in range(lax.axis_size(axis))])


def from_chips(piece):
    return [swap(piece, "shard", 2 * j) for j in range(1, lax.axis_size("shard") // 2)]


def tree(parts):
    while len(parts) > 1:
        parts = [parts[k] + parts[k + 1] for k in range(0, len(parts), 2)]
    return parts[0]


def add_low(parts, spare):
    wide = [part.astype(F32) for part in parts]
    total = tree(wide).astype(BF)
    if not spare:
        return total
    at = total.shape[-2] - 8
    rows = [part[..., at:, :] for part in wide]
    value = tree([part[..., 0:1, :] + part[..., 1:2, :] + part[..., 2:3, :] for part in rows])
    row = lax.broadcasted_iota(jnp.int32, total.shape, total.ndim - 2)
    for k, part in enumerate(split(value)):
        total = jnp.where(row == at + k, part, total)
    return total


def between_chips(part):
    return [part[0]] + [swap(part[j], "shard", 2 * j) for j in range(1, part.shape[0])]


def early(item, frozen):
    cond, clean, noise, tstep, text = item
    unet_conv, res_conv, time_mlp, time_proj, wq, kvproj, wo, geglu_in, geglu_out, vel = frozen
    half = CH // 2
    freqs = jnp.exp(-math.log(10000.0) * jnp.arange(half, dtype=jnp.int32).astype(F32) / half)
    angles = tstep[0].astype(F32) * freqs
    emb = jnp.concatenate([jnp.cos(angles), jnp.sin(angles)])[None, :].astype(BF)
    lat = jnp.stack([clean, noise]).reshape(2, 4, SIDE, 2, SIDE // 2).transpose(0, 1, 4, 3, 2).reshape(2, 4, PIX)
    wf = res_conv.transpose(0, 2, 1)
    outs = prologue(
        tstep, jnp.asarray(schedule()), cond, lat, text, kvproj, wq, wo, geglu_in, geglu_out.T, vel.T,
        jnp.broadcast_to(emb, (16, CH)), time_mlp, time_proj.T, unet_conv, wf,
    )
    return outs, geglu_in


def piece_kernel(w_in, w_conv, w_out, bias, piece):
    rows = w_out.shape[0]
    tall = jnp.concatenate([w_out[...], jnp.zeros((LANES - rows, CH), F32)], axis=0) if rows % 8 == 0 else None
    out_t = tall.T[:, 0:rows] if rows % 8 == 0 else w_out[...].T
    piece[0:CH, :] = jnp.concatenate([w_in[...], out_t, w_conv[...]], axis=1).astype(BF)
    pad = piece.shape[1] - bias.shape[1]
    row = jnp.concatenate([bias[...], jnp.zeros((1, pad), F32)], axis=1)
    first_row = lax.broadcasted_iota(jnp.int32, (8, piece.shape[1]), 0) == 0
    piece[CH : CH + 8, :] = jnp.where(first_row, row, 0.0).astype(BF)


def piece_of(masters):
    w_in, w_conv, w_out, bias = masters
    vm = pl.BlockSpec(memory_space=pltpu.VMEM)
    width = w_in.shape[0] + w_out.shape[0] + w_conv.shape[0]
    return pl.pallas_call(
        piece_kernel,
        out_shape=jax.ShapeDtypeStruct((CH + 8, width), BF),
        in_specs=[vm] * 4,
        out_specs=vm,
        compiler_params=pltpu.CompilerParams(vmem_limit_bytes=VMEM_LIMIT),
        name="piece",
    )(w_in.T, w_conv.T, w_out, bias[None, :])


def per_device(*args):
    conditions, clean, noise, tsteps, text, lengths, valid = args[:7]
    frozen = args[7:17]
    masters, firsts, seconds = args[17:21], args[21:25], args[25:29]
    piece = piece_of(masters)
    even = [piece] + from_chips(piece)
    me = lax.axis_index("shard").astype(jnp.int32)
    ints = jnp.stack([lengths[0], valid[0], me])
    outs, gi = early((conditions[0], clean[0], noise[0], tsteps, text[0]), frozen)
    even, outs, ints = lax.optimization_barrier((even, outs, ints))
    pieces = []
    for part in even:
        pieces += [part, swap(part, "shard", 1)]
    gout, gbias, keep_two, send_two, ginner, gh, wcf, *_ = main_call(ints, outs, pieces, gi)
    two, ginner = lax.optimization_barrier((add_low([keep_two, swap(send_two, "shard", 1)], True), ginner))
    twos = between_chips(two)
    keep_one, send_one = tail_call(ints, ginner, outs[0], wcf, gout, gbias, gh, len(pieces) // 2)
    twos, keep_one, send_one = lax.optimization_barrier((twos, keep_one, send_one))
    one = add_low([keep_one, swap(send_one, "shard", 1)], False)
    two = add_low(twos, True)
    bits = [1 << k for k in reversed(range((lax.axis_size("dp") - 1).bit_length()))]
    ones = between_chips(one)
    for bit in bits:
        twos = [two, swap(two, "dp", bit)]
        ones, twos = lax.optimization_barrier((ones, twos))
        two, one = add_low(twos, True), add_low(ones, False)
        ones = [one, swap(one, "dp", bit)]
    one = add_low(ones, False)
    squares = jnp.sum(jnp.square(one.astype(F32))) + jnp.sum(jnp.square(two[:CH].astype(F32)))
    sums = jnp.full((8, LANES), squares)
    sums = sums + swap(sums, "shard", 1)
    sums = tree([sums] + from_chips(sums))
    states = []
    for group in (masters, firsts, seconds):
        states += [group[0].T, group[1].T, group[2], group[3][None, :]]
    new = adam_call(sums, one, two, states)
    results = []
    for n in range(3):
        results += [new[4 * n].T, new[4 * n + 1].T, new[4 * n + 2], new[4 * n + 3][0]]
    return (*[entry[0, 0] for entry in new[12:]], *results)


def solution(mesh):
    both = ("dp", "shard")
    placed = (
        (P(both, None, None, None), P(both, None, None), P(both, None, None), P(both), P(both, None, None), P(both), P(both))
        + (P(),) * 10
        + (P("shard", None), P("shard", None), P("shard", None), P("shard")) * 3
    )
    return jax.shard_map(
        per_device,
        mesh=mesh,
        in_specs=placed,
        out_specs=(P(), P(), P()) + (P("shard", None), P("shard", None), P("shard", None), P("shard")) * 3,
        check_vma=False,
    )
```

```python
import math

import jax
import jax.numpy as jnp
import numpy as np
from jax import lax
from jax.experimental import pallas as pl
from jax.experimental.pallas import tpu as pltpu
from jax.sharding import PartitionSpec as P

HEADS = 8
GROUPS = 32
STEP = 10

LN_EPS = 1e-05
CLIP_MAX = 0.01
LEARN_RATE = 0.02
BETA_ONE = 0.9
BETA_TWO = 0.999
ADAM_EPS = 1e-08
WEIGHT_DECAY = 0.01

BF = jnp.bfloat16
F32 = jnp.float32

SIDE = 64
PIX = SIDE * SIDE
LANES = 128
HALO = LANES
WIDE = PIX + 2 * HALO
CH = 320
UNS = 192
FF = 1280
TXT = 80
KEYS = HEADS * TXT
NZ = 48
NT = (((1,), (1,)), ((), ()))
TN = (((0,), (0,)), ((), ()))
VMEM_LIMIT = 62 * 2**20

TILE = 512
TILE_C = 512
TILE_D = 512
W_PAD = 2944
DEPTH = 1024
CHUNK = 320


def schedule():
    start = 0.00085**0.5
    final = 0.012**0.5
    betas = (start + np.arange(1000, dtype=np.float64) * ((final - start) / 999.0)) ** 2
    table = np.zeros(1024, np.float32)
    table[:1000] = np.cumprod(1.0 - betas)
    return table.reshape(8, LANES)


def dot(a, b):
    return jnp.dot(a, b, preferred_element_type=F32)


def dot_nt(a, b):
    return lax.dot_general(a, b, NT, preferred_element_type=F32)


def al(x):
    return x if isinstance(x, int) else pl.multiple_of(x, LANES)


def tiles(width, *bodies):
    for p0 in range(0, PIX, width):
        for body in bodies:
            body(p0)


def stream(width, make, ends, use):
    make(0)
    make(PIX - width)
    ends()
    for p0 in range(0, PIX, width):
        if p0 + 2 * width < PIX:
            make(p0 + width)
        use(p0)


def put(dst, value, p0, chans):
    width = value.shape[1]
    low = value.astype(BF)
    for q in range(width // LANES):
        mid = low[:, q * LANES : (q + 1) * LANES]
        lane = lax.broadcasted_iota(jnp.int32, mid.shape, 1) & (SIDE - 1)
        up = jnp.where(lane == 0, jnp.zeros((), BF), pltpu.roll(mid, 1, 1))
        down = jnp.where(lane == SIDE - 1, jnp.zeros((), BF), pltpu.roll(mid, LANES - 1, 1))
        at = pl.ds(al(p0 + HALO + q * LANES), LANES)
        dst[0:chans, at] = up
        dst[chans : 2 * chans, at] = mid
        dst[2 * chans : 3 * chans, at] = down


def ends(dst, rows):
    last = dst[0:rows, PIX : PIX + LANES]
    head = dst[0:rows, HALO : HALO + LANES]
    lane = lax.broadcasted_iota(jnp.int32, last.shape, 1)
    zero = jnp.zeros((), BF)
    dst[0:rows, 0:LANES] = jnp.where(lane >= SIDE, pltpu.roll(last, SIDE, 1), zero)
    dst[0:rows, PIX + HALO : PIX + HALO + LANES] = jnp.where(lane < SIDE, pltpu.roll(head, SIDE, 1), zero)


def conv(weight, src, p0, width, chans):
    parts = []
    for a in range(3):
        for b in range(3):
            parts.append(src[a * chans : (a + 1) * chans, pl.ds(al(p0 + b * LANES), width)])
    return dot(weight, jnp.concatenate(parts, axis=0))


def short_weight(weight):
    cols = []
    for b in range(3):
        taps = [weight[:, (3 * a + b) * CH : (3 * a + b + 1) * CH] for a in range(3)]
        cols.append(jnp.concatenate(taps + [jnp.zeros((CH, DEPTH - 3 * CH), BF)], axis=1))
    wide = [col.astype(F32) for col in cols]
    outer, middle = 0.5 * (wide[0] + wide[2]), 0.5 * wide[1]
    return cols[0], (outer + middle).astype(BF), (outer - middle).astype(BF), cols[2]


def conv_short(weight, src, p0, width):
    d = [src[0 : 3 * CH, pl.ds(al(p0 + k * LANES), LANES)] for k in range(width // LANES + 2)]
    pairs = range(0, width // LANES, 2)
    mixed = (
        [d[k] - d[k + 2] for k in pairs],
        [d[k + 1] + d[k + 2] for k in pairs],
        [d[k + 2] - d[k + 1] for k in pairs],
        [d[k + 1] - d[k + 3] for k in pairs],
    )
    rest = jnp.zeros((DEPTH - 3 * CH, width // 2), BF)
    m = [dot(weight[q], jnp.concatenate([jnp.concatenate(mixed[q], axis=1), rest], axis=0)) for q in range(4)]
    both, other = m[1] + m[2], m[1] - m[2]
    even = both + m[0]
    odd = other - m[3]
    outs = []
    for k in range(width // LANES // 2):
        at = slice(k * LANES, (k + 1) * LANES)
        outs += [even[:, at], odd[:, at]]
    return jnp.concatenate(outs, axis=1)


def backward_weight(weight, natural):
    natural[...] = weight.T
    blocks = [natural[(8 - t) * CH : (9 - t) * CH, :] for t in range(9)]
    return jnp.concatenate(blocks, axis=1)


def lane_sum(value):
    total = value[:, 0:LANES]
    for q in range(1, value.shape[1] // LANES):
        total = total + value[:, q * LANES : (q + 1) * LANES]
    return total


def group_mean(gm, *sums):
    joined = sums[0] if len(sums) == 1 else jnp.concatenate(sums, axis=1)
    spread = jnp.dot(gm, joined, precision=lax.Precision.HIGHEST, preferred_element_type=F32)
    share = 1.0 / (PIX * (CH // GROUPS))
    means = [jnp.sum(spread[:, k * LANES : (k + 1) * LANES], axis=1, keepdims=True) * share for k in range(len(sums))]
    return means[0] if len(sums) == 1 else means


def silu_slope(y):
    s = jax.nn.sigmoid(y)
    return s * (1.0 + y * (1.0 - s))


def layer_stats(field):
    mean = jnp.mean(field, axis=0, keepdims=True)
    centered = field - mean
    inv = lax.rsqrt(jnp.mean(centered * centered, axis=0, keepdims=True) + LN_EPS)
    return centered * inv, inv


def layer_back(grad, normed, inv):
    return inv * (
        grad
        - jnp.mean(grad, axis=0, keepdims=True)
        - normed * jnp.mean(grad * normed, axis=0, keepdims=True)
    )


def split(value):
    high = value.astype(BF)
    rest = value - high.astype(F32)
    mid = rest.astype(BF)
    return high, mid, (rest - mid.astype(F32)).astype(BF)


def slot(owner, me, count):
    rel = jnp.bitwise_xor(owner, me)
    return (rel & 1) * (count // 2) + lax.shift_right_logical(rel, 1)


def scatter(dst, value, start, width, lane0, me, count):
    stop = start + value.shape[1]
    for owner in range(count):
        lo, hi = max(start, owner * width), min(stop, (owner + 1) * width)
        if lo < hi:
            at = lane0 + lo - owner * width
            dst[slot(owner, me, count), 0:CH, at : at + hi - lo] = value[:, lo - start : hi - start].astype(BF)


def prologue_kernel(
    steps, table, cond, lat, text, kvproj, wq, wo, gi, got, velt_in, emb, tmlp, tprojt, unet, res,
    base, nz, target, kq, kqb, vo, vob, gvt, gvl, velt, temb, wut, git, wf, wb,
    zs, us, kvs, nat, wsrc, sems,
):
    fetch = [pltpu.make_async_copy(res.at[k], wsrc.at[k], sems.at[k]) for k in range(2)]
    for copy in fetch:
        copy.start()
    index = lax.broadcasted_iota(jnp.int32, (8, LANES), 0) * LANES + lax.broadcasted_iota(jnp.int32, (8, LANES), 1)
    picked = jnp.where(index == steps[0], table[...], 0.0)
    abar = jnp.sum(jnp.sum(picked, axis=1, keepdims=True), axis=0, keepdims=True)
    alpha = jnp.sqrt(abar)
    sigma = jnp.sqrt(1.0 - abar)
    row = lax.broadcasted_iota(jnp.int32, (512, 512), 0)
    col = lax.broadcasted_iota(jnp.int32, (512, 512), 1)
    same = jnp.logical_and((row & 7) == (col >> 6), (row >> 3) == (col & 63))
    perm = jnp.where(same, 1.0, 0.0).astype(BF)
    lane = lax.broadcasted_iota(jnp.int32, (32, 8, LANES), 2)
    for c in range(3):
        zs[...] = lax.dot_general(cond[c], perm, TN, preferred_element_type=F32).reshape(64, 8, 512)
        for k in range(4):
            one = zs[0:32, :, k * LANES : (k + 1) * LANES]
            two = zs[32:64, :, k * LANES : (k + 1) * LANES]
            even = jnp.where(lane < SIDE, one, pltpu.roll(two, SIDE, 2))
            odd = jnp.where(lane < SIDE, pltpu.roll(one, SIDE, 2), two)
            for m in range(32):
                us[16 * k : 16 * k + 8, m * LANES : (m + 1) * LANES] = even[m]
                us[16 * k + 8 : 16 * k + 16, m * LANES : (m + 1) * LANES] = odd[m]
        base[64 * c : 64 * (c + 1), :] = us[...].astype(BF)
    clean = lat[0]
    noise = lat[1]
    noisy = (alpha * clean + sigma * noise).astype(BF).astype(F32)
    target[4:8, :] = jnp.zeros((4, PIX), F32)
    target[0:4, :] = alpha * noise - sigma * clean
    lane = lax.broadcasted_iota(jnp.int32, (4, LANES), 1)
    inside = lane & (SIDE - 1)
    cols = [noisy[:, m * LANES : (m + 1) * LANES] for m in range(32)]
    left = jnp.where(lane >= SIDE, pltpu.roll(cols[31], SIDE, 1), 0.0)
    right = jnp.where(lane < SIDE, pltpu.roll(cols[0], SIDE, 1), 0.0)
    cols = [left] + cols + [right]
    us[0:NZ, :] = jnp.zeros((NZ, PIX), F32)
    for m in range(34):
        up = jnp.where(inside == 0, 0.0, pltpu.roll(cols[m], 1, 1))
        down = jnp.where(inside == SIDE - 1, 0.0, pltpu.roll(cols[m], LANES - 1, 1))
        for a, part in enumerate((up, cols[m], down)):
            for b in range(3):
                at = m - b
                if 0 <= at < 32:
                    r = (3 * a + b) * 4
                    us[r : r + 4, at * LANES : (at + 1) * LANES] = part
    nz[...] = us[0:NZ, :].astype(BF)
    us[0:LANES // 2, 0:CH] = jnp.zeros((LANES // 2, CH), F32)
    us[0:36, 0:CH] = unet[...].astype(F32)
    wide = jnp.concatenate([us[0:64, 0:CH], jnp.zeros((64, CH), F32)], axis=0)
    wut[...] = wide.T.astype(BF)
    kvs[...] = jnp.zeros_like(kvs)
    kvs[0 : text.shape[0], :] = dot(text[...], kvproj[...])
    keys = kvs[:, 0:CH].astype(BF)
    values = kvs[:, CH : 2 * CH].astype(BF)
    head_dim = CH // HEADS
    head = lax.broadcasted_iota(jnp.int32, (TXT, CH), 1)
    own = [jnp.logical_and(head >= h * head_dim, head < (h + 1) * head_dim) for h in range(HEADS)]
    zero = jnp.zeros((), BF)
    kbd = jnp.concatenate([jnp.where(own[h], keys, zero) for h in range(HEADS)], axis=0)
    vbd = jnp.concatenate([jnp.where(own[h], values, zero) for h in range(HEADS)], axis=0)
    scale = head_dim ** (-0.5)
    fold = dot_nt(kbd, wq[...]) * scale
    kq[...] = fold.astype(BF)
    kqb[...] = fold.T.astype(BF)
    fold = dot(vbd, wo[...])
    vob[...] = fold.astype(BF)
    vo[...] = fold.T.astype(BF)
    us[0:8, 0:CH] = jnp.zeros((8, CH), F32)
    us[0:4, 0:CH] = velt_in[...].astype(F32)
    velf = us[0:8, 0:CH]
    velt[...] = velf.astype(BF)
    fold = dot(velf.astype(BF), got[...])
    high = fold.astype(BF).astype(F32)
    both = jnp.concatenate([high, fold - high], axis=0)
    gvt[...] = both.astype(BF)
    wide = jnp.concatenate([both, jnp.zeros((LANES - 16, FF), F32)], axis=0)
    gvl[0:FF, :] = wide.T[:, 0:16].astype(BF)
    wide = jnp.concatenate([velf, jnp.zeros((LANES - 8, CH), F32)], axis=0)
    gvl[FF : FF + CH, :] = wide.T[:, 0:16].astype(BF)
    git[...] = gi[...].T
    hidden = jax.nn.silu(dot(emb[...], tmlp[...])).astype(BF)
    temb[...] = dot_nt(tprojt[...], jnp.concatenate([hidden] * 8, axis=0))
    for k in range(2):
        fetch[k].wait()
        for q, part in enumerate(short_weight(wsrc[k])):
            wf[k, q] = part
        for q, part in enumerate(short_weight(backward_weight(wsrc[k], nat))):
            wb[k, q] = part


def prologue(*args):
    vm = pl.BlockSpec(memory_space=pltpu.VMEM)
    sm = pl.BlockSpec(memory_space=pltpu.SMEM)
    hb = pl.BlockSpec(memory_space=pl.ANY)
    shapes = [
        ((UNS, PIX), BF), ((NZ, PIX), BF), ((8, PIX), F32),
        ((KEYS, CH), BF), ((CH, KEYS), BF), ((CH, KEYS), BF), ((KEYS, CH), BF),
        ((16, FF), BF), ((FF + CH, 16), BF), ((8, CH), BF), ((CH, LANES), F32), ((CH, LANES), BF),
        ((2 * FF, CH), BF), ((2, 4, CH, DEPTH), BF), ((2, 4, CH, DEPTH), BF),
    ]
    return pl.pallas_call(
        prologue_kernel,
        out_shape=[jax.ShapeDtypeStruct(*s) for s in shapes],
        in_specs=[sm] + [vm] * 14 + [hb],
        out_specs=[vm] * len(shapes),
        scratch_shapes=[
            pltpu.VMEM((64, 8, 512), F32),
            pltpu.VMEM((64, PIX), F32),
            pltpu.VMEM((TXT, 2 * CH), F32),
            pltpu.VMEM((9 * CH, CH), BF),
            pltpu.VMEM((2, CH, 9 * CH), BF),
            pltpu.SemaphoreType.DMA((2,)),
        ],
        compiler_params=pltpu.CompilerParams(vmem_limit_bytes=VMEM_LIMIT),
        cost_estimate=pl.CostEstimate(flops=12_000_000_000, bytes_accessed=20_000_000, transcendentals=0),
        name="prologue",
    )(*args)


def main_kernel(
    ints, target, kq, kqb, vo, vob, gvt, gvl, velt, temb, wut, base, nz, wf, wb, git_hbm, gi_hbm, *rest,
):
    count = len(rest) - 27
    pieces = rest[:count]
    (
    gout, gbias, keep_hbm, send_hbm, ginner_hbm, gh_hbm, wcf_hbm, sf_hbm, mx_hbm, ds_hbm, y1_hbm,
    sa, sb, hg, cu, y2s, wbuf, git, gi, acc, stat, gm, bcols, wou, loss, sems, wsems,
    ) = rest[count:]
    length = ints[0]
    flag = ints[1].astype(F32)
    me = ints[2]
    half = count // 2
    w_conv = 9 * CH // count
    w_in = 9 * UNS // count
    w_out = CH // count
    w_bias = 3 * CH // count
    fetch = [
        pltpu.make_async_copy(wf.at[0], wbuf.at[1], sems.at[1]),
        pltpu.make_async_copy(wf.at[1], wbuf.at[0], sems.at[2]),
        pltpu.make_async_copy(wb.at[1], wbuf.at[1], sems.at[3]),
        pltpu.make_async_copy(wb.at[0], wbuf.at[0], sems.at[4]),
    ]
    get_git = pltpu.make_async_copy(git_hbm, git, sems.at[5])
    get_gi = pltpu.make_async_copy(gi_hbm, gi, sems.at[6])
    keep_first = pltpu.make_async_copy(sb, sf_hbm, sems.at[12])

    row = lax.broadcasted_iota(jnp.int32, (CH, CH), 0)
    col = lax.broadcasted_iota(jnp.int32, (CH, CH), 1)
    gm[...] = jnp.where((row * 6554) >> 16 == (col * 6554) >> 16, 1.0, 0.0)

    def norm_silu(field, store, dst, which):
        mean = group_mean(gm[...], acc[0])
        acc[1] = jnp.zeros_like(acc[1])

        def body(p0):
            centered = field[:, pl.ds(p0, TILE)] - mean
            acc[1] += lane_sum(centered * centered)

        tiles(TILE, body)
        inv = lax.rsqrt(group_mean(gm[...], acc[1]) + LN_EPS)
        stat[which] = jnp.broadcast_to(inv, (CH, LANES))
        acc[...] = jnp.zeros_like(acc)

        def make(p0):
            at = pl.ds(p0, TILE)
            y = (field[:, at] - mean) * inv
            store[:, at] = y.astype(BF)
            put(dst, y * jax.nn.sigmoid(y), p0, CH)

        return make

    def head(mx, ds, y1s):
        get_base = pltpu.make_async_copy(base, ds.at[0:UNS, :], sems.at[9])
        get_nz = pltpu.make_async_copy(nz, mx.at[CH : CH + NZ, :], sems.at[10])
        get_base.start()
        get_nz.start()

        def make_base(p0):
            put(sa, ds[0:UNS, pl.ds(p0, TILE)], p0, UNS)

        def assemble(got):
            loads = [
                pltpu.make_async_copy(pieces[rel], got.at[jnp.bitwise_xor(me, rel)], wsems.at[rel]) for rel in range(count)
            ]
            for copy in loads:
                copy.start()
            get_git.start()
            get_gi.start()
            get_base.wait()
            tiles(TILE, make_base)
            ends(sa, 3 * UNS)
            for copy in loads:
                copy.wait()
            mx[0:CH, 0 : 9 * UNS] = jnp.concatenate([got[d, 0:CH, 0:w_in] for d in range(count)], axis=1)
            out_t = jnp.concatenate([got[d, 0:CH, w_in : w_in + w_out] for d in range(count)], axis=1)
            wou[...] = jnp.concatenate([out_t, wut[:, 0:NZ]], axis=1)
            bias = jnp.concatenate([got[d, CH : CH + 8, 0:w_bias].astype(F32) for d in range(count)], axis=1)
            for k in range(3):
                part = jnp.concatenate([bias[:, k * CH : (k + 1) * CH]] * 16, axis=0)
                bcols[k] = part.T
            skip = w_in + w_out
            y1s[:, 0 : 9 * CH] = jnp.concatenate([got[d, 0:CH, skip : skip + w_conv] for d in range(count)], axis=1)
            y1s[:, 9 * CH : W_PAD] = jnp.zeros((CH, W_PAD - 9 * CH), BF)
            for q, part in enumerate(short_weight(y1s[:, 0 : 9 * CH])):
                wbuf[0, q] = part

        pl.run_scoped(assemble, pltpu.VMEM((count,) + pieces[0].shape, BF))

        def body(p0):
            at = pl.ds(p0, TILE)
            first = conv(mx[0:CH, 0 : 9 * UNS], sa, p0, TILE, UNS) + bcols[0, :, 0:1]
            hg[:, at] = first
            put(sb, first, p0, CH)

        tiles(TILE, body)
        ends(sb, 3 * CH)
        keep_first.start()

        get_nz.wait()
        fetch[0].start()
        acc[...] = jnp.zeros_like(acc)
        keep_w = pltpu.make_async_copy(y1s.at[:, 0:W_PAD], wcf_hbm, sems.at[0])
        keep_w.start()

        def body(p0):
            at = pl.ds(p0, TILE)
            inner = conv_short(wbuf.at[0], sb, p0, TILE) + bcols[1, :, 0:1]
            s = jax.nn.sigmoid(inner)
            m = inner * s
            mx[0:CH, at] = m.astype(BF)
            ds[:, at] = (s + m * (1.0 - s)).astype(BF)
            h0 = hg[:, at] + dot(wou[...], mx[:, at]) + bcols[2, :, 0:1]
            hg[:, at] = h0
            acc[0] += lane_sum(h0)

        tiles(TILE, body)
        keep_mx = pltpu.make_async_copy(mx, mx_hbm, sems.at[13])
        keep_ds = pltpu.make_async_copy(ds, ds_hbm, sems.at[14])
        keep_mx.start()
        keep_ds.start()
        keep_w.wait()
        fetch[1].start()
        make = norm_silu(hg, y1s, sa, 0)
        fetch[0].wait()

        def body(p0):
            at = pl.ds(p0, TILE_C)
            c1 = conv_short(wbuf.at[1], sa, p0, TILE_C) + temb[:, 0:1]
            cu[:, at] = c1
            acc[0] += lane_sum(c1)

        stream(TILE, make, lambda: ends(sa, 3 * CH), body)
        keep_y1 = pltpu.make_async_copy(y1s, y1_hbm, sems.at[11])
        keep_y1.start()
        keep_mx.wait()
        keep_ds.wait()
        keep_y1.wait()

    held = (pltpu.VMEM((CH + NZ, PIX), BF), pltpu.VMEM((CH, PIX), BF), pltpu.VMEM((CH, PIX), BF))
    pl.run_scoped(head, *held)
    fetch[2].start()
    keep_first.wait()
    make = norm_silu(cu, y2s, sb, 1)
    tiles(TILE, make)
    ends(sb, 3 * CH)

    fetch[1].wait()
    get_git.wait()
    get_gi.wait()
    loss[...] = jnp.zeros_like(loss)
    token = lax.broadcasted_iota(jnp.int32, (1, TXT, 1), 1)
    bias = jnp.where(token < length, 0.0, -1000000000.0)

    def front(p0, keep):
        uw, attend_k, normed_k, normed2_k, inv_k, gp_k = keep
        at = pl.ds(p0, TILE_D)
        h1 = hg[:, at] + conv_short(wbuf.at[0], sb, p0, TILE_D)
        yield
        normed, inv = layer_stats(h1)
        low = normed.astype(BF)
        normed_k[...] = low
        inv_k[0:1] = inv
        s = dot(kq[...], low).reshape(HEADS, TXT, TILE_D) + bias
        yield
        e = jnp.exp(s - jnp.max(s, axis=1, keepdims=True))
        attend = (e * (1.0 / jnp.sum(e, axis=1, keepdims=True))).reshape(KEYS, TILE_D).astype(BF)
        attend_k[...] = attend
        yield
        h2 = h1 + dot(vo[...], attend)
        normed2, inv2 = layer_stats(h2)
        n2 = normed2.astype(BF)
        normed2_k[...] = n2
        inv_k[1:2] = inv2
        yield
        acts = []
        for n in range(FF // CHUNK):
            f = n * CHUNK
            val = dot(git[f : f + CHUNK, :], n2)
            gate = dot(git[FF + f : FF + f + CHUNK, :], n2)
            phi = 0.5 + 0.5 * lax.erf(gate * 0.5**0.5)
            u = gate * phi
            slope = phi + gate * (jnp.exp(-0.5 * gate * gate) * (2.0 * math.pi) ** (-0.5))
            acts.append((val * u).astype(BF))
            col = n * TILE_D
            uw[:, col : col + TILE_D] = u.astype(uw.dtype)
            uw[:, PIX // 2 + col : PIX // 2 + col + TILE_D] = (val * slope).astype(uw.dtype)
            yield
        both = dot(gvt[...], jnp.concatenate(acts, axis=0))
        diff = both[0:8] + both[8:16] + dot(velt[...], h2.astype(BF)) - target[:, at]
        loss[...] += lane_sum(diff * diff) * flag
        gp = (diff * (2.0 * flag)).astype(BF)
        gp_k[...] = jnp.concatenate([gp, gp], axis=0)
        yield

    def back(p0, keep):
        uw, attend_k, normed_k, normed2_k, inv_k, gp_k = keep
        at = pl.ds(p0, TILE_D)
        gp = gp_k[...]
        pieces = []
        for n in range(FF // CHUNK):
            g_act = dot(gvl[n * CHUNK : (n + 1) * CHUNK, :], gp).astype(uw.dtype)
            col = n * TILE_D
            pieces.insert(n, (g_act * uw[:, col : col + TILE_D]).astype(BF))
            pieces.append((g_act * uw[:, PIX // 2 + col : PIX // 2 + col + TILE_D]).astype(BF))
        yield
        g_n2 = dot(gi[...], jnp.concatenate(pieces, axis=0))
        yield
        g2 = dot(gvl[FF : FF + CH, :], gp) + layer_back(g_n2, normed2_k[...].astype(F32), inv_k[1:2])
        yield
        attend = attend_k[...].astype(F32).reshape(HEADS, TXT, TILE_D)
        prod = attend * dot(vob[...], g2.astype(BF)).reshape(HEADS, TXT, TILE_D)
        yield
        g_s = prod - attend * jnp.sum(prod, axis=1, keepdims=True)
        g_n = dot(kqb[...], g_s.reshape(KEYS, TILE_D).astype(BF))
        yield
        g1 = g2 + layer_back(g_n, normed_k[...].astype(F32), inv_k[0:1])
        hg[:, at] = g1
        put(sa, g1, p0, CH)
        yield

    def weave(*parts):
        parts = list(parts)
        while parts:
            parts = [part for part in parts if next(part, True) is None]

    def stages(uw, *states):
        one, two = (cu,) + states[0:5], (uw,) + states[5:10]
        weave(front(0, one))

        def pair(i, carry):
            p0 = al(i * (2 * TILE_D))
            weave(back(p0, one), front(al(p0 + TILE_D), two))
            weave(back(al(p0 + TILE_D), two), front(al(p0 + 2 * TILE_D), one))
            return carry

        lax.fori_loop(0, PIX // (2 * TILE_D) - 1, pair, 0)
        weave(back(PIX - 2 * TILE_D, one), front(PIX - TILE_D, two))
        weave(back(PIX - TILE_D, two))

    state = (
        pltpu.VMEM((KEYS, TILE_D), BF),
        pltpu.VMEM((CH, TILE_D), BF),
        pltpu.VMEM((CH, TILE_D), BF),
        pltpu.VMEM((8, TILE_D), F32),
        pltpu.VMEM((16, TILE_D), BF),
    )
    pl.run_scoped(stages, pltpu.VMEM((CH, PIX), BF), *state, *state)
    ends(sa, 3 * CH)

    def conv_back(weight, src, ys, make=None):
        def body(p0):
            at = pl.ds(p0, TILE_C)
            y = ys[:, at].astype(F32)
            u = conv_short(weight, src, p0, TILE_C) * silu_slope(y)
            cu[:, at] = u
            acc[0] += lane_sum(u)
            acc[1] += lane_sum(u * y)

        acc[...] = jnp.zeros_like(acc)
        if make is None:
            tiles(TILE_C, body)
        else:
            stream(TILE_C, make, lambda: ends(src, 3 * CH), body)
        return group_mean(gm[...], acc[0], acc[1])

    fetch[3].start()
    fetch[2].wait()
    mean, cross = conv_back(wbuf.at[1], sa, y2s)
    inv = stat[1][:, 0:1]

    mean_two, cross_two, inv_two = mean, cross, inv

    def make_c1(p0):
        at = pl.ds(p0, TILE_C)
        put(sb, inv_two * (cu[:, at] - mean_two - y2s[:, at].astype(F32) * cross_two), p0, CH)

    def foot(mx, ds, y1s):
        back = [
            pltpu.make_async_copy(mx_hbm, mx, sems.at[13]),
            pltpu.make_async_copy(ds_hbm, ds, sems.at[14]),
        ]
        get_y1 = pltpu.make_async_copy(y1_hbm, y1s, sems.at[11])
        get_y1.start()
        for copy in back:
            copy.start()
        fetch[3].wait()
        get_y1.wait()
        mean, cross = conv_back(wbuf.at[0], sb, y1s, make_c1)
        inv = stat[0][:, 0:1]
        get_first = pltpu.make_async_copy(sf_hbm, sb, sems.at[12])
        get_first.start()
        for copy in back:
            copy.wait()
        gbias[...] = jnp.zeros_like(gbias)
        wout = wou[:, 0:CH].T

        def body(p0):
            at = pl.ds(p0, TILE)
            g0 = hg[:, at] + inv * (cu[:, at] - mean - y1s[:, at].astype(F32) * cross)
            hg[:, at] = g0
            branch = g0.astype(BF)
            g_inner = (dot(wout, branch) * ds[:, at].astype(F32)).astype(BF)
            sa[0:CH, at] = g_inner
            y1s[:, at] = branch
            gbias[0] += lane_sum(g_inner.astype(F32))
            gbias[1] += lane_sum(branch.astype(F32))

        tiles(TILE, body)
        gout[...] = dot_nt(y1s[...], mx[0:CH, :])
        get_first.wait()

    pl.run_scoped(foot, *held)
    send_h = pltpu.make_async_copy(hg, gh_hbm, sems.at[7])
    send_g = pltpu.make_async_copy(sa.at[0:CH, 0:PIX], ginner_hbm, sems.at[8])
    send_h.start()
    send_g.start()

    def last(grads):
        for b in range(3):
            grad = dot_nt(sa[0:CH, 0:PIX], sb[:, b * LANES : b * LANES + PIX])
            for a in range(3):
                scatter(grads, grad[:, a * CH : (a + 1) * CH], (3 * a + b) * CH, w_conv, 0, me, count)
        total = jnp.sum(jnp.sum(loss[...], axis=1, keepdims=True), axis=0, keepdims=True)
        lane = lax.broadcasted_iota(jnp.int32, (8, w_conv), 1)
        row = lax.broadcasted_iota(jnp.int32, (8, w_conv), 0)
        value = jnp.where(lane == 0, total, jnp.where(lane == 1, flag * float(4 * PIX), 0.0))
        high, mid, low = [part.astype(F32) for part in split(value)]
        triple = jnp.where(row == 0, high, jnp.where(row == 1, mid, jnp.where(row == 2, low, 0.0))).astype(BF)
        for k in range(count):
            grads[k, CH : CH + 8, :] = triple
        keep = pltpu.make_async_copy(grads.at[0:half], keep_hbm, sems.at[9])
        send = pltpu.make_async_copy(grads.at[half:count], send_hbm, sems.at[10])
        keep.start()
        send.start()
        keep.wait()
        send.wait()

    pl.run_scoped(last, pltpu.VMEM((count, CH + 8, w_conv), BF))
    send_h.wait()
    send_g.wait()


def main_call(ints, outs, pieces, gi):
    base, nz, target, kq, kqb, vo, vob, gvt, gvl, velt, temb, wut, git, wf, wb = outs
    count = len(pieces)
    half = count // 2
    w_grad = 9 * CH // count
    vm = pl.BlockSpec(memory_space=pltpu.VMEM)
    sm = pl.BlockSpec(memory_space=pltpu.SMEM)
    hb = pl.BlockSpec(memory_space=pl.ANY)
    shapes = [
        ((CH, CH), F32), ((2, CH, LANES), F32),
        ((half, CH + 8, w_grad), BF), ((half, CH + 8, w_grad), BF),
        ((CH, PIX), BF), ((CH, PIX), F32), ((CH, W_PAD), BF),
        ((3 * CH, WIDE), BF), ((CH + NZ, PIX), BF), ((CH, PIX), BF), ((CH, PIX), BF),
    ]
    return pl.pallas_call(
        main_kernel,
        out_shape=[jax.ShapeDtypeStruct(*s) for s in shapes],
        in_specs=[sm] + [vm] * 10 + [hb] * (6 + count),
        out_specs=[vm] * 2 + [hb] * 9,
        scratch_shapes=[
            pltpu.VMEM((3 * CH, WIDE), BF),
            pltpu.VMEM((3 * CH, WIDE), BF),
            pltpu.VMEM((CH, PIX), F32),
            pltpu.VMEM((CH, PIX), F32),
            pltpu.VMEM((CH, PIX), BF),
            pltpu.VMEM((2, 4, CH, DEPTH), BF),
            pltpu.VMEM((2 * FF, CH), BF),
            pltpu.VMEM((CH, 2 * FF), BF),
            pltpu.VMEM((2, CH, LANES), F32),
            pltpu.VMEM((2, CH, LANES), F32),
            pltpu.VMEM((CH, CH), F32),
            pltpu.VMEM((3, CH, LANES), F32),
            pltpu.VMEM((CH, CH + NZ), BF),
            pltpu.VMEM((8, LANES), F32),
            pltpu.SemaphoreType.DMA((15,)),
            pltpu.SemaphoreType.DMA((count,)),
        ],
        compiler_params=pltpu.CompilerParams(vmem_limit_bytes=VMEM_LIMIT),
        cost_estimate=pl.CostEstimate(flops=80_000_000_000, bytes_accessed=60_000_000, transcendentals=0),
        name="main",
    )(ints, target, kq, kqb, vo, vob, gvt, gvl, velt, temb, wut, base, nz, wf, wb, git, gi, *pieces)


def tail_kernel(
    ints, ginner, base, wcf, gout, gbias, gh_hbm, keep_hbm, send_hbm,
    sa, sb, gh, gf, nat, wcb, grads, acc, sems,
):
    me = ints[2]
    half = keep_hbm.shape[0]
    count = 2 * half
    w_in = 9 * UNS // count
    w_out = CH // count
    w_bias = 3 * CH // count
    fetch = pltpu.make_async_copy(gh_hbm, gh, sems.at[0])
    fetch.start()
    for q, part in enumerate(short_weight(backward_weight(wcf[:, 0 : 9 * CH], nat))):
        wcb[q] = part

    def make(p0):
        at = pl.ds(p0, TILE)
        put(sa, ginner[:, at], p0, CH)
        put(sb, base[:, at], p0, UNS)

    acc[...] = jnp.zeros_like(acc)
    fetch.wait()

    def body(p0):
        at = pl.ds(p0, TILE)
        g_first = (gh[:, at] + conv_short(wcb, sa, p0, TILE)).astype(BF)
        gf[:, at] = g_first
        acc[...] += lane_sum(g_first.astype(F32))

    stream(TILE, make, lambda: ends(sa, 3 * CH), body)
    ends(sb, 3 * UNS)
    for b in range(3):
        grad = dot_nt(gf[...], sb[:, b * LANES : b * LANES + PIX])
        for a in range(3):
            scatter(grads, grad[:, a * UNS : (a + 1) * UNS], (3 * a + b) * UNS, w_in, 0, me, count)
    scatter(grads, gout[...], 0, w_out, w_in, me, count)
    rows = [jnp.sum(part.T, axis=0, keepdims=True) for part in (acc[...], gbias[0], gbias[1])]
    bias = jnp.concatenate(rows, axis=1)
    first_row = lax.broadcasted_iota(jnp.int32, (8, w_in + w_out), 0) == 0
    for owner in range(count):
        part = bias[:, owner * w_bias : (owner + 1) * w_bias]
        part = jnp.concatenate([part, jnp.zeros((1, w_in + w_out - w_bias), F32)], axis=1)
        grads[slot(owner, me, count), CH : CH + 8, :] = jnp.where(first_row, part, 0.0).astype(BF)
    keep = pltpu.make_async_copy(grads.at[0:half], keep_hbm, sems.at[1])
    send = pltpu.make_async_copy(grads.at[half:count], send_hbm, sems.at[2])
    keep.start()
    send.start()
    keep.wait()
    send.wait()


def tail_call(ints, ginner, base, wcf, gout, gbias, gh, half):
    vm = pl.BlockSpec(memory_space=pltpu.VMEM)
    sm = pl.BlockSpec(memory_space=pltpu.SMEM)
    hb = pl.BlockSpec(memory_space=pl.ANY)
    wide = (9 * UNS + CH) // (2 * half)
    return pl.pallas_call(
        tail_kernel,
        out_shape=[jax.ShapeDtypeStruct((half, CH + 8, wide), BF)] * 2,
        in_specs=[sm] + [vm] * 5 + [hb],
        out_specs=[hb, hb],
        scratch_shapes=[
            pltpu.VMEM((3 * CH, WIDE), BF),
            pltpu.VMEM((3 * UNS, WIDE), BF),
            pltpu.VMEM((CH, PIX), F32),
            pltpu.VMEM((CH, PIX), BF),
            pltpu.VMEM((9 * CH, CH), BF),
            pltpu.VMEM((4, CH, DEPTH), BF),
            pltpu.VMEM((2 * half, CH + 8, wide), BF),
            pltpu.VMEM((CH, LANES), F32),
            pltpu.SemaphoreType.DMA((3,)),
        ],
        compiler_params=pltpu.CompilerParams(vmem_limit_bytes=VMEM_LIMIT),
        cost_estimate=pl.CostEstimate(flops=14_000_000_000, bytes_accessed=16_000_000, transcendentals=0),
        name="tail",
    )(ints, ginner, base, wcf, gout, gbias, gh)


def update(master, first, second, grad):
    new_first = BETA_ONE * first + (1.0 - BETA_ONE) * grad
    new_second = BETA_TWO * second + (1.0 - BETA_TWO) * grad * grad
    first_hat = new_first / (1.0 - BETA_ONE**STEP)
    second_hat = new_second / (1.0 - BETA_TWO**STEP)
    new_master = master - LEARN_RATE * (
        first_hat / (jnp.sqrt(second_hat) + ADAM_EPS) + WEIGHT_DECAY * master
    )
    return new_first, new_second, new_master


def adam_kernel(sums, g_one, g_two, *refs):
    ins, outs, (loss, items, norm) = refs[:12], refs[12:24], refs[24:]
    w_in, w_conv, w_out, w_bias = ins[0].shape[1], ins[1].shape[1], ins[2].shape[0], ins[3].shape[1]
    two = g_two[...].astype(F32)
    spare = two[CH : CH + 1] + two[CH + 1 : CH + 2] + two[CH + 2 : CH + 3]
    loss[...] = spare[:, 0:1]
    count = jnp.maximum(spare[:, 1:2], 1.0)
    items[...] = count
    grad_norm = jnp.sqrt(sums[0:1, 0:1]) / count
    norm[...] = grad_norm
    scale = jnp.minimum(1.0, CLIP_MAX / (grad_norm + 1e-06)) / count
    one = g_one[...].astype(F32) * scale
    first = max((one.shape[1] // LANES - 1) * LANES, 0)
    grads = (
        one[0:CH, 0:w_in],
        two[0:CH] * scale,
        one[0:CH, first:].T[w_in - first : w_in - first + w_out, :],
        one[CH : CH + 1, 0:w_bias],
    )
    for k in range(4):
        values = update(ins[k][...], ins[4 + k][...], ins[8 + k][...], grads[k])
        for n in range(3):
            outs[4 * n + k][...] = values[n]


def adam_call(sums, g_one, g_two, states):
    vm = pl.BlockSpec(memory_space=pltpu.VMEM)
    return pl.pallas_call(
        adam_kernel,
        out_shape=[jax.ShapeDtypeStruct(s.shape, F32) for s in states] + [jax.ShapeDtypeStruct((1, 1), F32)] * 3,
        in_specs=[vm] * 15,
        out_specs=[vm] * 15,
        compiler_params=pltpu.CompilerParams(vmem_limit_bytes=32 * 2**20),
        cost_estimate=pl.CostEstimate(flops=10_000_000, bytes_accessed=6_000_000, transcendentals=0),
        name="adamw",
    )(sums, g_one, g_two, *states)


def swap(value, axis, bit):
    return lax.ppermute(value, axis, [(i, i ^ bit) for i in range(lax.axis_size(axis))])


def from_chips(piece):
    return [swap(piece, "shard", 2 * j) for j in range(1, lax.axis_size("shard") // 2)]


def tree(parts):
    while len(parts) > 1:
        parts = [parts[k] + parts[k + 1] for k in range(0, len(parts), 2)]
    return parts[0]


def add_low(parts, spare):
    wide = [part.astype(F32) for part in parts]
    total = tree(wide).astype(BF)
    if not spare:
        return total
    at = total.shape[-2] - 8
    rows = [part[..., at:, :] for part in wide]
    value = tree([part[..., 0:1, :] + part[..., 1:2, :] + part[..., 2:3, :] for part in rows])
    row = lax.broadcasted_iota(jnp.int32, total.shape, total.ndim - 2)
    for k, part in enumerate(split(value)):
        total = jnp.where(row == at + k, part, total)
    return total


def between_chips(part):
    return [part[0]] + [swap(part[j], "shard", 2 * j) for j in range(1, part.shape[0])]


def early(item, frozen):
    cond, clean, noise, tstep, text = item
    unet_conv, res_conv, time_mlp, time_proj, wq, kvproj, wo, geglu_in, geglu_out, vel = frozen
    half = CH // 2
    freqs = jnp.exp(-math.log(10000.0) * jnp.arange(half, dtype=jnp.int32).astype(F32) / half)
    angles = tstep[0].astype(F32) * freqs
    emb = jnp.concatenate([jnp.cos(angles), jnp.sin(angles)])[None, :].astype(BF)
    lat = jnp.stack([clean, noise]).reshape(2, 4, SIDE, 2, SIDE // 2).transpose(0, 1, 4, 3, 2).reshape(2, 4, PIX)
    wf = res_conv.transpose(0, 2, 1)
    outs = prologue(
        tstep, jnp.asarray(schedule()), cond, lat, text, kvproj, wq, wo, geglu_in, geglu_out.T, vel.T,
        jnp.broadcast_to(emb, (16, CH)), time_mlp, time_proj.T, unet_conv, wf,
    )
    return outs, geglu_in


def piece_kernel(w_in, w_conv, w_out, bias, piece):
    rows = w_out.shape[0]
    tall = jnp.concatenate([w_out[...], jnp.zeros((LANES - rows, CH), F32)], axis=0) if rows % 8 == 0 else None
    out_t = tall.T[:, 0:rows] if rows % 8 == 0 else w_out[...].T
    piece[0:CH, :] = jnp.concatenate([w_in[...], out_t, w_conv[...]], axis=1).astype(BF)
    pad = piece.shape[1] - bias.shape[1]
    row = jnp.concatenate([bias[...], jnp.zeros((1, pad), F32)], axis=1)
    first_row = lax.broadcasted_iota(jnp.int32, (8, piece.shape[1]), 0) == 0
    piece[CH : CH + 8, :] = jnp.where(first_row, row, 0.0).astype(BF)


def piece_of(masters):
    w_in, w_conv, w_out, bias = masters
    vm = pl.BlockSpec(memory_space=pltpu.VMEM)
    width = w_in.shape[0] + w_out.shape[0] + w_conv.shape[0]
    return pl.pallas_call(
        piece_kernel,
        out_shape=jax.ShapeDtypeStruct((CH + 8, width), BF),
        in_specs=[vm] * 4,
        out_specs=vm,
        compiler_params=pltpu.CompilerParams(vmem_limit_bytes=VMEM_LIMIT),
        name="piece",
    )(w_in.T, w_conv.T, w_out, bias[None, :])


def per_device(*args):
    conditions, clean, noise, tsteps, text, lengths, valid = args[:7]
    frozen = args[7:17]
    masters, firsts, seconds = args[17:21], args[21:25], args[25:29]
    piece = piece_of(masters)
    even = [piece] + from_chips(piece)
    me = lax.axis_index("shard").astype(jnp.int32)
    ints = jnp.stack([lengths[0], valid[0], me])
    outs, gi = early((conditions[0], clean[0], noise[0], tsteps, text[0]), frozen)
    even, outs, ints = lax.optimization_barrier((even, outs, ints))
    pieces = []
    for part in even:
        pieces += [part, swap(part, "shard", 1)]
    gout, gbias, keep_two, send_two, ginner, gh, wcf, *_ = main_call(ints, outs, pieces, gi)
    two, ginner = lax.optimization_barrier((add_low([keep_two, swap(send_two, "shard", 1)], True), ginner))
    twos = between_chips(two)
    keep_one, send_one = tail_call(ints, ginner, outs[0], wcf, gout, gbias, gh, len(pieces) // 2)
    twos, keep_one, send_one = lax.optimization_barrier((twos, keep_one, send_one))
    one = add_low([keep_one, swap(send_one, "shard", 1)], False)
    two = add_low(twos, True)
    bits = [1 << k for k in reversed(range((lax.axis_size("dp") - 1).bit_length()))]
    ones = between_chips(one)
    for bit in bits:
        twos = [two, swap(two, "dp", bit)]
        ones, twos = lax.optimization_barrier((ones, twos))
        two, one = add_low(twos, True), add_low(ones, False)
        ones = [one, swap(one, "dp", bit)]
    one = add_low(ones, False)
    squares = jnp.sum(jnp.square(one.astype(F32))) + jnp.sum(jnp.square(two[:CH].astype(F32)))
    sums = jnp.full((8, LANES), squares)
    sums = sums + swap(sums, "shard", 1)
    sums = tree([sums] + from_chips(sums))
    states = []
    for group in (masters, firsts, seconds):
        states += [group[0].T, group[1].T, group[2], group[3][None, :]]
    new = adam_call(sums, one, two, states)
    results = []
    for n in range(3):
        results += [new[4 * n].T, new[4 * n + 1].T, new[4 * n + 2], new[4 * n + 3][0]]
    return (*[entry[0, 0] for entry in new[12:]], *results)


def solution(mesh):
    both = ("dp", "shard")
    placed = (
        (P(both, None, None, None), P(both, None, None), P(both, None, None), P(both), P(both, None, None), P(both), P(both))
        + (P(),) * 10
        + (P("shard", None), P("shard", None), P("shard", None), P("shard")) * 3
    )
    return jax.shard_map(
        per_device,
        mesh=mesh,
        in_specs=placed,
        out_specs=(P(), P(), P()) + (P("shard", None), P("shard", None), P("shard", None), P("shard")) * 3,
        check_vma=False,
    )
```
